512 devices in a mesh: member: 16 (over x, y_hi, core), grid: 32 (over y_lo, z).
Axes of the slice: x: 4, y: 4 (y_hi: 2, y_lo: 2; y = y_hi * 2 + y_lo), z: 16, core: 2. Of those that a mesh axis runs over, the one named last changes fastest.
Arguments:
- mesh_latent: bfloat16 [16, 8192, 1024], P('member', 'grid'), may hold values from -6 to 6
- grid_latent: bfloat16 [8192, 1024], P('grid'), may hold values from -6 to 6
- node_weight: bfloat16 [1024, 1024], replicated, may hold values from -0.1875 to 0.1875
- out_weight: bfloat16 [100, 1024], replicated, may hold values from -0.1875 to 0.1875
- target: float32 [100, 8192], P(None, 'grid'), may hold values from -6 to 6
- area_weight: float32 [8192], P('grid'), may hold values from 0.3 to 3
- var_weight: float32 [100], replicated, may hold values from 0.2 to 2
- edge_src: int32 [32, 3, 512], P('grid'), may hold values from 0 to 255
- edge_dst: int32 [32, 3, 512], P('grid'), may hold values from 0 to 255
- edge_count: int32 [32, 3], P('grid'), may hold values from 1 to 512, as said below
Outputs:
- grad_mesh: bfloat16 [16, 8192, 1024], P('member', 'grid')
- grad_grid: bfloat16 [8192, 1024], P('grid', 'member')
The draws below stay inside these ranges and needn't reach their ends.
Inputs may be any that keep to these rules, and one draw needn't show every extreme that they name: Each destination shard takes edges only from its own shard and its two neighbours along the closed band of shards, as the offsets say; slots c with c >= edge_count[d, o] carry no edge; in every draw some destination shard has all 512 slots used for all three offsets.
All inputs are finite; a program needn't handle non-finite values.
Results may differ from the reference program's by a relative error of at most 0.0087.
Values may be sent and summed in bfloat16 or wider, within the bound.
No kernel may reach another device: no remote copies, remote signals or barrier semaphores. Data moves between devices by JAX's collectives and lax.ppermute only.
A program may use at most 64 MiB of HBM per device.

```python
import math
import jax
import jax.numpy as jnp
from jax import lax

LAT = 1024
VARS = 100
GRID_DEV = 256
MESH_DEV = 256
SHARDS = 32
MEMBERS = 16
CAP = 512
GRID = 8192
MESH = 8192


def draw_edge_count(key, part):
    key = jax.random.fold_in(key, 7)
    first_key, second_key = jax.random.split(key)
    counts = jax.random.randint(first_key, (SHARDS, 3), 1, CAP + 1, dtype=jnp.int32)
    full_row = jax.random.randint(second_key, (), 0, SHARDS, dtype=jnp.int32)
    row_ids = jnp.arange(SHARDS, dtype=jnp.int32)
    return jnp.where((row_ids == full_row)[:, None], CAP, counts).astype(jnp.int32)


def set_ends(entries, own_key, least, largest):
    extent = entries.shape
    place = [jax.random.randint(jax.random.fold_in(own_key, axis), (), 0, extent[axis]) for axis in range(len(extent))]
    entries = entries.at[tuple(place)].set(least)
    longest = extent.index(max(extent))
    place[longest] = (place[longest] + 1) % extent[longest]
    return entries.at[tuple(place)].set(largest)


def block_scale(key, extent, pieces, low, top_value):
    factor_of = 1.0
    for dim, blocks in pieces:
        heights = jax.random.uniform(jax.random.fold_in(jax.random.fold_in(key, 6), dim), (blocks,), jnp.float32, low / len(pieces), top_value / len(pieces))
        factor_of = factor_of * jnp.repeat(jnp.exp(heights), extent[dim] // blocks).reshape((-1,) + (1,) * (len(extent) - 1 - dim))
    return factor_of


def bell_draw(stream_key, dims, width, bound, cuts=(), kind=jnp.bfloat16):
    array = width * jax.random.normal(stream_key, dims, jnp.float32)
    if cuts:
        array = array * block_scale(stream_key, dims, cuts, -0.22, 0.18)
    return jnp.clip(array, -bound, bound).astype(kind)


def setup_inputs(seed: int = 0) -> dict:
    arg_keys = jax.random.split(jax.random.key(seed), 11)
    return {
        "mesh_latent": bell_draw(arg_keys[0], (MEMBERS, MESH, LAT), 1.0, 6.0, ((0, 16), (1, 32))),
        "grid_latent": bell_draw(arg_keys[1], (GRID, LAT), 1.0, 6.0, ((0, 32),)),
        "node_weight": bell_draw(arg_keys[2], (LAT, LAT), LAT ** -0.5, 0.1875),
        "out_weight": bell_draw(arg_keys[3], (VARS, LAT), LAT ** -0.5, 0.1875),
        "target": bell_draw(arg_keys[4], (VARS, GRID), 1.0, 6.0, ((1, 32),), jnp.float32),
        "area_weight": jnp.clip(jnp.exp(math.log(3.0) - 2.3025851 * jax.random.uniform(arg_keys[5], (GRID,), jnp.float32) ** block_scale(arg_keys[5], (GRID,), ((0, 32),), -0.2, 0.2)), 0.3, 3.0),
        "var_weight": jnp.clip(jnp.exp(jax.random.uniform(arg_keys[6], (VARS,), jnp.float32, math.log(0.2), math.log(2.0))), 0.2, 2.0),
        "edge_src": set_ends(jax.random.randint(arg_keys[7], (SHARDS, 3, CAP), 0, MESH_DEV), jax.random.fold_in(arg_keys[7], 1), 0, MESH_DEV - 1).astype(jnp.int32),
        "edge_dst": set_ends(jax.random.randint(arg_keys[8], (SHARDS, 3, CAP), 0, GRID_DEV), jax.random.fold_in(arg_keys[8], 1), 0, GRID_DEV - 1).astype(jnp.int32),
        "edge_count": draw_edge_count(jax.random.fold_in(arg_keys[10], 71), 0),
    }


SMOOTH = 0.1
ALPHA = 0.95
EPS = 1e-05

def smooth_slope(difference):
    return difference / jnp.sqrt(difference * difference + SMOOTH * SMOOTH)

def decode_forward(gathered, grid_latent, node_weight, out_weight):
    summed = gathered + grid_latent.astype(jnp.float32)
    centered = summed - lax.optimization_barrier(jnp.mean(summed, axis=-1, keepdims=True))
    inverse = lax.rsqrt(lax.optimization_barrier(jnp.mean(centered * centered, axis=-1, keepdims=True)) + EPS)
    normed = centered * inverse
    pre_act = jnp.dot(normed.astype(jnp.bfloat16), node_weight, preferred_element_type=jnp.float32)
    hidden = jax.nn.silu(pre_act).astype(jnp.bfloat16)
    predicted = lax.dot_general(out_weight, hidden, (((1,), (1,)), ((), ())), preferred_element_type=jnp.float32)
    return (predicted, normed, inverse, pre_act)

def decode_backward(grad_pred, normed, inverse, pre_act, node_weight, out_weight):
    grad_hidden = lax.dot_general(grad_pred.astype(jnp.bfloat16), out_weight, (((0,), (0,)), ((), ())), preferred_element_type=jnp.float32)
    gate_sig = jax.nn.sigmoid(pre_act)
    grad_pre = (grad_hidden * gate_sig * (1.0 + pre_act * (1.0 - gate_sig))).astype(jnp.bfloat16)
    grad_normed = lax.dot_general(grad_pre, node_weight, (((1,), (1,)), ((), ())), preferred_element_type=jnp.float32)
    return inverse * (grad_normed - lax.optimization_barrier(jnp.mean(grad_normed, axis=-1, keepdims=True)) - normed * lax.optimization_barrier(jnp.mean(grad_normed * normed, axis=-1, keepdims=True)))

def reference(mesh_latent, grid_latent, node_weight, out_weight, target, area_weight, var_weight, edge_src, edge_dst, edge_count):
    shard_ids = jnp.arange(SHARDS, dtype=jnp.int32)
    offsets = jnp.arange(3, dtype=jnp.int32)
    slot_lanes = jnp.arange(CAP, dtype=jnp.int32)
    source_shard = ((shard_ids[:, None] + SHARDS + 1 - offsets[None, :]) % SHARDS).astype(jnp.int32)
    keep_mask = (slot_lanes[None, None, :] < edge_count[:, :, None]).reshape(-1)
    keep_float = keep_mask.astype(jnp.float32)[:, None]
    source_index = (source_shard[:, :, None] * MESH_DEV + edge_src).reshape(-1).astype(jnp.int32)
    target_index = (shard_ids[:, None, None] * GRID_DEV + edge_dst).reshape(-1).astype(jnp.int32)

    def aggregate(latent):
        slot_rows = latent[source_index].astype(jnp.float32) * keep_float
        return jax.ops.segment_sum(slot_rows, target_index, num_segments=GRID)

    def member_pred(latent):
        return decode_forward(aggregate(latent), grid_latent, node_weight, out_weight)[0]
    predictions = lax.map(member_pred, mesh_latent)
    pair_scale = (1.0 - (1.0 - ALPHA) / MEMBERS) / (MEMBERS - 1)
    weights = area_weight[None, :] * var_weight[:, None]

    def member_grad(own_pred):
        pair_sum = lax.optimization_barrier(jnp.sum(smooth_slope(own_pred[None] - predictions), axis=0))
        return weights * (smooth_slope(own_pred - target) - pair_scale * pair_sum)
    grad_preds = lax.map(member_grad, predictions)

    def member_back(grid_sum, inputs):
        latent, grad_pred = inputs
        unused, normed, inverse, pre_act = decode_forward(aggregate(latent), grid_latent, node_weight, out_weight)
        grad_summed = decode_backward(grad_pred, normed, inverse, pre_act, node_weight, out_weight)
        slot_grads = grad_summed.astype(jnp.bfloat16)[target_index].astype(jnp.float32) * keep_float
        grad_latent = jax.ops.segment_sum(slot_grads, source_index, num_segments=MESH)
        return (grid_sum + grad_summed, grad_latent.astype(jnp.bfloat16))
    grid_sum, grad_mesh = lax.scan(member_back, jnp.zeros((GRID, LAT), jnp.float32), (mesh_latent, grad_preds))
    return (grad_mesh, grid_sum.astype(jnp.bfloat16))
```

```python
import jax
import jax.numpy as jnp
from jax import lax
from jax.sharding import PartitionSpec as P

SMOOTH = 0.1
ALPHA = 0.95
EPS = 1e-05


def from_behind(value, axis, steps):
    count = lax.axis_size(axis)
    pairs = [(source, (source + steps) % count) for source in range(count)]
    return lax.ppermute(value, axis, pairs)


def smooth_slope(difference):
    return difference * lax.rsqrt(difference * difference + SMOOTH * SMOOTH)


def counts_of(rows_pick, columns_pick, rows, columns):
    row_hot = (jnp.arange(rows, dtype=jnp.int32)[:, None] == rows_pick[None, :]).astype(jnp.bfloat16)
    column_hot = (columns_pick[:, None] == jnp.arange(columns, dtype=jnp.int32)[None, :]).astype(
        jnp.bfloat16
    )
    counts = jnp.dot(row_hot, column_hot, preferred_element_type=jnp.float32)
    high = counts.astype(jnp.bfloat16)
    return high, (counts - high.astype(jnp.float32)).astype(jnp.bfloat16)


def per_device(
    mesh_latent,
    grid_latent,
    node_weight,
    out_weight,
    target,
    area_weight,
    var_weight,
    edge_src,
    edge_dst,
    edge_count,
):
    members = lax.axis_size("member")
    latent = mesh_latent[0]
    mesh_rows = latent.shape[0]
    grid_rows, width = grid_latent.shape
    capacity = edge_dst.shape[2]
    live = jnp.arange(capacity, dtype=jnp.int32)[None, :] < edge_count[0][:, None]
    picks = jnp.where(live, edge_dst[0], -1)
    from_left = from_behind(latent, "grid", 1)
    from_right = from_behind(latent, "grid", -1)
    edges = jnp.stack([edge_src[0], picks], axis=1)
    edges_left = from_behind(edges[0], "grid", 1)
    edges_right = from_behind(edges[2], "grid", -1)

    parts = [counts_of(picks[o], edge_src[0, o], grid_rows, mesh_rows) for o in range(3)]
    spread = jnp.concatenate([p[0] for p in parts] + [p[1] for p in parts], axis=1)
    rows = jnp.concatenate([from_right, latent, from_left] * 2, axis=0)
    gathered = jnp.dot(spread, rows, preferred_element_type=jnp.float32)

    summed = gathered + grid_latent.astype(jnp.float32)
    centered = summed - jnp.mean(summed, axis=-1, keepdims=True)
    inverse = lax.rsqrt(jnp.mean(centered * centered, axis=-1, keepdims=True) + EPS)
    normed = centered * inverse
    pre_act = jnp.dot(normed.astype(jnp.bfloat16), node_weight, preferred_element_type=jnp.float32)
    hidden = jax.nn.silu(pre_act).astype(jnp.bfloat16)
    variables = out_weight.shape[0]
    out_padded = jnp.pad(out_weight, ((0, 128 - variables), (0, 0)))
    predicted = lax.dot_general(
        hidden, out_padded, (((1,), (1,)), ((), ())), preferred_element_type=jnp.float32
    )
    shared = jnp.broadcast_to(predicted.astype(jnp.bfloat16)[None], (members, grid_rows, 128))
    everyone = lax.all_to_all(shared, "member", 0, 0, tiled=True)
    own = lax.axis_index("member")
    others = jnp.where(
        jnp.arange(members)[:, None, None] == own, predicted[None], everyone.astype(jnp.float32)
    )
    pair_sum = jnp.sum(smooth_slope(predicted[None] - others), axis=0)
    pair_scale = (1.0 - (1.0 - ALPHA) / members) / (members - 1)
    target_padded = jnp.pad(target, ((0, 128 - variables), (0, 0))).T
    var_padded = jnp.pad(var_weight, (0, 128 - variables))
    grad_pred = (
        area_weight[:, None]
        * var_padded[None, :]
        * (smooth_slope(predicted - target_padded) - pair_scale * pair_sum)
    )
    grad_hidden = jnp.dot(
        grad_pred.astype(jnp.bfloat16), out_padded, preferred_element_type=jnp.float32
    )
    gate_sig = jax.nn.sigmoid(pre_act)
    grad_pre = (grad_hidden * gate_sig * (1.0 + pre_act * (1.0 - gate_sig))).astype(jnp.bfloat16)
    grad_normed = lax.dot_general(
        grad_pre, node_weight, (((1,), (1,)), ((), ())), preferred_element_type=jnp.float32
    )
    grad_summed = inverse * (
        grad_normed
        - jnp.mean(grad_normed, axis=-1, keepdims=True)
        - normed * jnp.mean(grad_normed * normed, axis=-1, keepdims=True)
    )
    grad_send = grad_summed.astype(jnp.bfloat16)
    back_left = from_behind(grad_send, "grid", 1)
    back_right = from_behind(grad_send, "grid", -1)
    share = width // members
    blocks = grad_send.reshape(2, grid_rows // 2, members, share).transpose(2, 1, 0, 3)
    blocks = blocks.reshape(members, grid_rows // 2, 2 * share)
    landed = lax.all_to_all(blocks, "member", 0, 0, tiled=True)
    grid_sum = jnp.sum(landed.astype(jnp.float32), axis=0).astype(jnp.bfloat16)
    grid_share = grid_sum.reshape(grid_rows // 2, 2, share).transpose(1, 0, 2)
    grid_share = grid_share.reshape(grid_rows, share)

    own_edges = (edge_src[0, 1], picks[1])
    back = [
        counts_of(dst, src, grid_rows, mesh_rows)
        for src, dst in (edges_left, own_edges, edges_right)
    ]
    collect = jnp.concatenate([p[0] for p in back] + [p[1] for p in back], axis=0)
    grads = jnp.concatenate([back_left, grad_send, back_right] * 2, axis=0)
    grad_latent = lax.dot_general(
        collect, grads, (((0,), (0,)), ((), ())), preferred_element_type=jnp.float32
    )
    return (grad_latent.astype(jnp.bfloat16)[None], grid_share)


def solution(mesh):
    return jax.shard_map(
        per_device,
        mesh=mesh,
        in_specs=(
            P("member", "grid", None),
            P("grid", None),
            P(),
            P(),
            P(None, "grid"),
            P("grid"),
            P(),
            P("grid", None, None),
            P("grid", None, None),
            P("grid", None),
        ),
        out_specs=(P("member", "grid", None), P("grid", "member")),
        check_vma=False,
    )
```

```python
import functools

import jax
import jax.numpy as jnp
from jax import lax
from jax.experimental import pallas as pl
from jax.experimental.pallas import tpu as pltpu
from jax.sharding import PartitionSpec as P

SMOOTH = 0.1
ALPHA = 0.95
EPS = 1e-05
LANES = 128
VARS = 100
MAIN = 208
FOLD = 25
FOLDS = 4
STEPS = 32767.0
CODE = 256.0
LOWEST = -20.0
VMEM_LIMIT = 28 * 1024 * 1024


def from_behind(value, axis, steps):
    count = lax.axis_size(axis)
    pairs = [(source, (source + steps) % count) for source in range(count)]
    return lax.ppermute(value, axis, pairs)


def smooth_slope(difference):
    return difference * lax.rsqrt(difference * difference + SMOOTH * SMOOTH)


def turn(values, shift):
    shift = shift % LANES
    return pltpu.roll(values, shift, 1) if shift else values


def lanes_of(values):
    return lax.broadcasted_iota(jnp.int32, values.shape, 1)


def one_hot(picks, rows):
    places = lax.broadcasted_iota(jnp.int32, (rows, picks.shape[1]), 0)
    return jnp.where(places == picks, 1.0, 0.0).astype(jnp.bfloat16)


def count_pairs(row_picks, column_picks, rows, columns):
    return lax.dot_general(
        one_hot(row_picks, rows),
        one_hot(column_picks, columns),
        (((1,), (1,)), ((), ())),
        preferred_element_type=jnp.float32,
    )


def store_counts(counts, at, high_ref, low_ref):
    high = counts.astype(jnp.bfloat16)
    high_ref[:, at] = high
    low_ref[:, at] = (counts - high.astype(jnp.float32)).astype(jnp.bfloat16)
    return jnp.max(counts)


def edges_kernel(count_ref, src_ref, dst_ref, out_ref, high_ref, low_ref, over_ref, first_ref, last_ref, pad_ref, turned_ref):
    grid_rows = high_ref.shape[0]
    mesh_rows = high_ref.shape[1] // 3
    slots = src_ref.shape[1]
    slot = lax.broadcasted_iota(jnp.int32, (1, slots), 1)
    most = 0.0
    for offset in range(3):
        picks = jnp.where(slot < count_ref[0, offset], dst_ref[offset : offset + 1, :], -1)
        sources = src_ref[offset : offset + 1, :]
        counts = count_pairs(picks, sources, grid_rows, mesh_rows)
        at = slice(offset * mesh_rows, (offset + 1) * mesh_rows)
        most = jnp.maximum(most, store_counts(counts, at, high_ref, low_ref))
        if offset != 1:
            ref = first_ref if offset == 0 else last_ref
            ref[0:1, :] = sources
            ref[1:2, :] = picks
    over_ref[0, 0] = (most > 256.0).astype(jnp.int32)
    variables, width = out_ref.shape
    padded = jnp.concatenate(
        [out_ref[...].astype(jnp.float32), jnp.zeros((LANES - variables, width), jnp.float32)], axis=0
    )
    pad_ref[...] = padded.astype(jnp.bfloat16)
    turned_ref[...] = padded.T.astype(jnp.bfloat16)


def back_edges_kernel(count_ref, src_ref, dst_ref, left_ref, right_ref, high_ref, low_ref, over_ref):
    mesh_rows = high_ref.shape[0]
    grid_rows = high_ref.shape[1] // 3
    slots = src_ref.shape[1]
    slot = lax.broadcasted_iota(jnp.int32, (1, slots), 1)
    own = jnp.where(slot < count_ref[0, 1], dst_ref[1:2, :], -1)
    triples = (
        (left_ref[0:1, :], left_ref[1:2, :]),
        (src_ref[1:2, :], own),
        (right_ref[0:1, :], right_ref[1:2, :]),
    )
    most = 0.0
    for place, (sources, picks) in enumerate(triples):
        counts = count_pairs(sources, picks, mesh_rows, grid_rows)
        at = slice(place * grid_rows, (place + 1) * grid_rows)
        most = jnp.maximum(most, store_counts(counts, at, high_ref, low_ref))
    over_ref[0, 0] = (most > 256.0).astype(jnp.int32)


def forward_kernel(
    over_ref, high_ref, low_ref, right_ref, own_ref, left_ref, grid_ref, node_ref, turned_ref,
    shared_ref, pred_ref, normed_ref, inverse_ref, pre_ref, sum_ref,
):
    mesh_rows = own_ref.shape[0]
    rows = (right_ref, own_ref, left_ref)

    def gather(counts_ref):
        return sum(
            jnp.dot(
                counts_ref[:, i * mesh_rows : (i + 1) * mesh_rows],
                rows[i][...],
                preferred_element_type=jnp.float32,
            )
            for i in range(3)
        )

    sum_ref[...] = gather(high_ref) + grid_ref[...].astype(jnp.float32)

    @pl.when(over_ref[0, 0] > 0)
    def _():
        sum_ref[...] += gather(low_ref)

    summed = sum_ref[...]
    centered = summed - jnp.mean(summed, axis=-1, keepdims=True)
    inverse = lax.rsqrt(jnp.mean(centered * centered, axis=-1, keepdims=True) + EPS)
    normed = centered * inverse
    normed_ref[...] = normed
    inverse_ref[...] = inverse
    pre_act = jnp.dot(normed.astype(jnp.bfloat16), node_ref[...], preferred_element_type=jnp.float32)
    pre_ref[...] = pre_act
    hidden = (pre_act * (0.5 + 0.5 * jnp.tanh(0.5 * pre_act))).astype(jnp.bfloat16)
    pred = jnp.dot(hidden, turned_ref[...], preferred_element_type=jnp.float32)
    pred_ref[...] = pred
    largest = jnp.max(jnp.abs(pred), axis=0, keepdims=True)
    code = jnp.ceil(jnp.log2(jnp.maximum(largest, 2.0**LOWEST)) * CODE)
    whole = jnp.round(pred * (jnp.exp2(code * (-1.0 / CODE)) * STEPS))
    packed = fold(whole, code).astype(jnp.int16)
    for member in range(shared_ref.shape[0]):
        shared_ref[member] = packed


def fold(values, code=None):
    rest = values[MAIN:, :]
    tail = jnp.zeros((MAIN - FOLDS * rest.shape[0], LANES), values.dtype)
    if code is not None:
        wide = jnp.broadcast_to(code, tail.shape)
        row = lax.broadcasted_iota(jnp.int32, tail.shape, 0)
        for k in range(FOLDS):
            tail = jnp.where(row == k, turn(wide, VARS - FOLD * k), tail)
    pieces = [turn(rest, VARS - FOLD * k) for k in range(FOLDS)] + [tail]
    spare = jnp.concatenate(pieces, axis=0)
    main = values[:MAIN, :]
    lane = lanes_of(main)
    return jnp.where(lane < VARS, main, jnp.where(lane < VARS + FOLD, spare, jnp.zeros_like(main)))


def unfold(values, rows):
    rest_rows = rows - MAIN
    lane = lax.broadcasted_iota(jnp.int32, (rest_rows, LANES), 1)
    rest = jnp.zeros((rest_rows, LANES), values.dtype)
    for k in range(FOLDS):
        piece = turn(values[k * rest_rows : (k + 1) * rest_rows, :], FOLD * k - VARS)
        rest = jnp.where((lane >= FOLD * k) & (lane < FOLD * (k + 1)), piece, rest)
    return jnp.concatenate([values, rest], axis=0)


def middle_kernel(
    pre_ref, pred_ref, target_ref, area_ref, var_ref, node_ref,
    gate_ref, lead_ref, weight_ref, fold_ref, turned_ref, *, pair_scale
):
    pre_act = pre_ref[...]
    gate_sig = 0.5 + 0.5 * jnp.tanh(0.5 * pre_act)
    gate_ref[...] = gate_sig * (1.0 + pre_act * (1.0 - gate_sig))
    variables, grid_rows = target_ref.shape
    padded = jnp.concatenate(
        [target_ref[...], jnp.zeros((LANES - variables, grid_rows), jnp.float32)], axis=0
    )
    weight = area_ref[...] * var_ref[...]
    lead_ref[...] = weight * smooth_slope(pred_ref[...] - padded.T)
    weight_ref[...] = weight * pair_scale
    fold_ref[...] = fold(pred_ref[...])
    turned_ref[...] = node_ref[...].T


def backward_kernel(
    me_ref, everyone_ref, fold_ref, lead_ref, weight_ref, gate_ref, normed_ref, inverse_ref, pad_ref, turned_ref,
    send_ref, blocks_ref, scale_ref,
):
    members = everyone_ref.shape[0]
    grid_rows, width = normed_ref.shape
    rest_rows = grid_rows - MAIN
    me = me_ref[0]
    first = FOLDS * rest_rows
    lane = lax.broadcasted_iota(jnp.int32, (members, LANES), 1)
    tails = everyone_ref[:, first:MAIN, :].astype(jnp.float32)
    code = jnp.zeros((members, LANES), jnp.float32)
    for k in range(FOLDS):
        piece = turn(tails[:, k, :], FOLD * k - VARS)
        code = jnp.where((lane >= FOLD * k) & (lane < FOLD * (k + 1)), piece, code)
    scale = jnp.exp2(code * (1.0 / CODE)) * (1.0 / STEPS)
    for k in range(FOLDS):
        scale_ref[k] = jnp.where(lane < VARS, scale, turn(scale, VARS - FOLD * k))

    bounds = [(k * rest_rows, (k + 1) * rest_rows) for k in range(FOLDS)] + [(first, MAIN)]
    parts = [jnp.zeros((high - low, LANES), jnp.float32) for low, high in bounds]
    for step in range(1, members):
        other = lax.rem(me + step, members)
        for i, (low, high) in enumerate(bounds):
            factor = scale_ref[min(i, FOLDS - 1), pl.ds(other, 1), :]
            theirs = everyone_ref[other, low:high, :].astype(jnp.float32) * factor
            parts[i] = parts[i] + smooth_slope(fold_ref[low:high, :] - theirs)
    pair_sum = unfold(jnp.concatenate(parts, axis=0), grid_rows)
    real = lanes_of(pair_sum) < VARS
    grad_pred = lead_ref[...] - weight_ref[...] * jnp.where(real, pair_sum, 0.0)
    grad_hidden = jnp.dot(
        grad_pred.astype(jnp.bfloat16), pad_ref[...], preferred_element_type=jnp.float32
    )
    grad_pre = (grad_hidden * gate_ref[...]).astype(jnp.bfloat16)
    grad_normed = jnp.dot(grad_pre, turned_ref[...], preferred_element_type=jnp.float32)
    normed = normed_ref[...]
    grad_summed = inverse_ref[...] * (
        grad_normed
        - jnp.mean(grad_normed, axis=-1, keepdims=True)
        - normed * jnp.mean(grad_normed * normed, axis=-1, keepdims=True)
    )
    send_ref[...] = grad_summed.astype(jnp.bfloat16)
    half = grid_rows // 2
    lower = lax.broadcasted_iota(jnp.int32, (half, LANES), 1) < LANES // 2
    for pair in range(width // LANES):
        at = slice(pair * LANES, (pair + 1) * LANES)
        top = grad_summed[:half, at]
        bottom = grad_summed[half:, at]
        blocks_ref[2 * pair] = jnp.where(lower, top, turn(bottom, LANES // 2)).astype(jnp.bfloat16)
        blocks_ref[2 * pair + 1] = jnp.where(lower, turn(top, LANES // 2), bottom).astype(jnp.bfloat16)


def member_sum_kernel(landed_ref, out_ref):
    total = landed_ref[0].astype(jnp.float32)
    for member in range(1, landed_ref.shape[0]):
        total = total + landed_ref[member].astype(jnp.float32)
    half = total.shape[0]
    share = out_ref.shape[1]
    out_ref[:half, :] = total[:, :share].astype(jnp.bfloat16)
    out_ref[half:, :] = turn(total, LANES // 2)[:, :share].astype(jnp.bfloat16)


def spread_kernel(over_ref, high_ref, low_ref, left_ref, own_ref, right_ref, out_ref, sum_ref):
    rows = left_ref.shape[0]
    grads = (left_ref, own_ref, right_ref)

    def spread(counts_ref):
        return sum(
            jnp.dot(
                counts_ref[:, i * rows : (i + 1) * rows], grads[i][...], preferred_element_type=jnp.float32
            )
            for i in range(3)
        )

    sum_ref[...] = spread(high_ref)

    @pl.when(over_ref[0, 0] > 0)
    def _():
        sum_ref[...] += spread(low_ref)

    out_ref[...] = sum_ref[...].astype(jnp.bfloat16)


def shape(dims, dtype):
    return jax.ShapeDtypeStruct(dims, dtype)


SMEM = pl.BlockSpec(memory_space=pltpu.SMEM)
VMEM = pl.BlockSpec(memory_space=pltpu.VMEM)


def call(kernel, outs, ins, scratch=(), cost=(0, 0), small=()):
    return pl.pallas_call(
        kernel,
        out_shape=[o for o in outs],
        in_specs=[SMEM if ("in", i) in small else VMEM for i in range(len(ins))],
        out_specs=[SMEM if ("out", i) in small else VMEM for i in range(len(outs))],
        scratch_shapes=list(scratch),
        compiler_params=pltpu.CompilerParams(vmem_limit_bytes=VMEM_LIMIT),
        cost_estimate=pl.CostEstimate(flops=cost[0], bytes_accessed=cost[1], transcendentals=0),
    )(*ins)


def per_device(
    mesh_latent, grid_latent, node_weight, out_weight, target, area_weight, var_weight, edge_src, edge_dst, edge_count
):
    f32, b16, i32 = jnp.float32, jnp.bfloat16, jnp.int32
    members = lax.axis_size("member")
    latent = mesh_latent[0]
    mesh_rows = latent.shape[0]
    grid_rows, width = grid_latent.shape
    slots = edge_dst.shape[2]
    variables = out_weight.shape[0]
    mega = 1 << 20

    from_left = from_behind(latent, "grid", 1)
    from_right = from_behind(latent, "grid", -1)
    src, dst = edge_src[0], edge_dst[0]
    high, low, over, first_edges, last_edges, out_pad, out_turned = call(
        edges_kernel,
        [
            shape((grid_rows, 3 * mesh_rows), b16),
            shape((grid_rows, 3 * mesh_rows), b16),
            shape((1, 1), i32),
            shape((2, slots), i32),
            shape((2, slots), i32),
            shape((LANES, width), b16),
            shape((width, LANES), b16),
        ],
        [edge_count, src, dst, out_weight],
        small=(("in", 0), ("out", 2)),
        cost=(300 * mega, 2 * mega),
    )
    left_edges = from_behind(first_edges, "grid", 1)
    right_edges = from_behind(last_edges, "grid", -1)

    shared, pred, normed, inverse, pre_act = call(
        forward_kernel,
        [
            shape((members, MAIN, LANES), jnp.int16),
            shape((grid_rows, LANES), f32),
            shape((grid_rows, width), f32),
            shape((grid_rows, 1), f32),
            shape((grid_rows, width), f32),
        ],
        [over, high, low, from_right, latent, from_left, grid_latent, node_weight, out_turned],
        scratch=[pltpu.VMEM((grid_rows, width), f32)],
        small=(("in", 0),),
        cost=(1000 * mega, 8 * mega),
    )
    everyone = lax.all_to_all(shared, "member", 0, 0, tiled=True)

    back_high, back_low, back_over = call(
        back_edges_kernel,
        [
            shape((mesh_rows, 3 * grid_rows), b16),
            shape((mesh_rows, 3 * grid_rows), b16),
            shape((1, 1), i32),
        ],
        [edge_count, src, dst, left_edges, right_edges],
        small=(("in", 0), ("out", 2)),
        cost=(300 * mega, 2 * mega),
    )
    pair_scale = (1.0 - (1.0 - ALPHA) / members) / (members - 1)
    gate, lead, weight, folded, node_turned = call(
        functools.partial(middle_kernel, pair_scale=pair_scale),
        [
            shape((grid_rows, width), f32),
            shape((grid_rows, LANES), f32),
            shape((grid_rows, LANES), f32),
            shape((MAIN, LANES), f32),
            shape((width, width), b16),
        ],
        [
            pre_act,
            pred,
            target,
            area_weight[:, None],
            jnp.pad(var_weight, (0, LANES - variables))[None, :],
            node_weight,
        ],
        cost=(10 * mega, 6 * mega),
    )
    me = lax.axis_index("member").astype(i32)[None]
    grad_send, blocks = call(
        backward_kernel,
        [
            shape((grid_rows, width), b16),
            shape((members, grid_rows // 2, LANES), b16),
        ],
        [me, everyone, folded, lead, weight, gate, normed, inverse, out_pad, node_turned],
        scratch=[pltpu.VMEM((FOLDS, members, LANES), f32)],
        small=(("in", 0),),
        cost=(700 * mega, 8 * mega),
    )
    back_left = from_behind(grad_send, "grid", 1)
    back_right = from_behind(grad_send, "grid", -1)
    landed = lax.all_to_all(blocks, "member", 0, 0, tiled=True)
    (grid_share,) = call(
        member_sum_kernel,
        [shape((grid_rows, width // members), b16)],
        [landed],
        cost=(mega, mega),
    )
    (grad_latent,) = call(
        spread_kernel,
        [shape((mesh_rows, width), b16)],
        [back_over, back_high, back_low, back_left, grad_send, back_right],
        scratch=[pltpu.VMEM((mesh_rows, width), f32)],
        small=(("in", 0),),
        cost=(400 * mega, 3 * mega),
    )
    return (grad_latent[None], grid_share)


def solution(mesh):
    return jax.shard_map(
        per_device,
        mesh=mesh,
        in_specs=(
            P("member", "grid", None),
            P("grid", None),
            P(),
            P(),
            P(None, "grid"),
            P("grid"),
            P(),
            P("grid", None, None),
            P("grid", None, None),
            P("grid", None),
        ),
        out_specs=(P("member", "grid", None), P("grid", "member")),
        check_vma=False,
    )
```

```python
import functools

import jax
import jax.numpy as jnp
from jax import lax
from jax.experimental import pallas as pl
from jax.experimental.pallas import tpu as pltpu
from jax.sharding import PartitionSpec as P

SMOOTH = 0.1
ALPHA = 0.95
EPS = 1e-05
LANES = 128
VARS = 100
MAIN = 208
FOLD = 25
FOLDS = 4
STEPS = 32767.0
CODE = 256.0
LOWEST = -20.0
VMEM_LIMIT = 48 * 1024 * 1024


def to_neighbours(value, side):
    members, shards = lax.axis_size("member"), lax.axis_size("grid")
    pairs = [
        (member * shards + shard, member * shards + (shard + (1 if member % 2 == side else -1)) % shards)
        for member in range(members)
        for shard in range(shards)
    ]
    return lax.ppermute(value, ("member", "grid"), pairs)


def smooth_slope(difference):
    return difference * lax.rsqrt(difference * difference + SMOOTH * SMOOTH)


def turn(values, shift):
    shift = shift % LANES
    return pltpu.roll(values, shift, 1) if shift else values


def lanes_of(values):
    return lax.broadcasted_iota(jnp.int32, values.shape, 1)


def one_hot(picks, rows):
    places = lax.broadcasted_iota(jnp.int32, (rows, picks.shape[1]), 0)
    return jnp.where(places == picks, 1.0, 0.0).astype(jnp.bfloat16)


def count_pairs(row_hot, column_hot):
    return lax.dot_general(
        row_hot, column_hot, (((1,), (1,)), ((), ())), preferred_element_type=jnp.float32
    )


def store_counts(counts, at, high_ref, low_ref):
    high = counts.astype(jnp.bfloat16)
    high_ref[:, at] = high
    low_ref[:, at] = (counts - high.astype(jnp.float32)).astype(jnp.bfloat16)
    return jnp.max(counts)


def edges_kernel(
    me_ref, count_ref, src_ref, dst_ref, out_ref,
    high_ref, low_ref, back_high_ref, back_low_ref, over_ref, pad_ref, turned_ref,
):
    size = high_ref.shape[0]
    slots = src_ref.shape[1]
    slot = lax.broadcasted_iota(jnp.int32, (1, slots), 1)
    odd = lax.rem(me_ref[0], 2)
    most = 0.0
    for place, offset in enumerate((2 - 2 * odd, 1, 2 * odd)):
        live = slot < count_ref[0, offset]
        targets = one_hot(jnp.where(live, dst_ref[pl.ds(offset, 1), :], -1), size)
        sources = one_hot(src_ref[pl.ds(offset, 1), :], size)
        counts = count_pairs(targets, sources)
        most = jnp.maximum(
            most, store_counts(counts, slice(place * size, (place + 1) * size), high_ref, low_ref)
        )
        back = 2 - place
        store_counts(
            count_pairs(sources, targets), slice(back * size, (back + 1) * size), back_high_ref, back_low_ref
        )
    over_ref[0] = (most > 256.0).astype(jnp.int32)
    variables, width = out_ref.shape
    padded = jnp.concatenate(
        [out_ref[...].astype(jnp.float32), jnp.zeros((LANES - variables, width), jnp.float32)], axis=0
    )
    pad_ref[...] = padded.astype(jnp.bfloat16)
    turned_ref[...] = padded.T.astype(jnp.bfloat16)


def start_all(sources, targets, sems):
    copies = [pltpu.make_async_copy(s, t, sems.at[i]) for i, (s, t) in enumerate(zip(sources, targets))]
    for copy in copies:
        copy.start()
    return copies


def dot(left, right):
    return jnp.dot(left, right, preferred_element_type=jnp.float32)


def forward_kernel(
    over_ref, high_hbm, own_hbm, first_hbm, second_hbm, grid_hbm, node_hbm, turned_hbm, low_hbm,
    shared_hbm, pred_hbm, normed_hbm, inverse_hbm, pre_hbm,
    high_ref, own_ref, first_ref, second_ref, grid_ref, node_ref, turned_ref, low_ref,
    packed_ref, pred_ref, normed_ref, inverse_ref, pre_ref, sum_ref,
    in_sems, low_sem, out_sems, share_sems,
):
    size = own_ref.shape[0]
    loads = start_all(
        (high_hbm, own_hbm, first_hbm, second_hbm, grid_hbm, node_hbm, turned_hbm),
        (high_ref, own_ref, first_ref, second_ref, grid_ref, node_ref, turned_ref),
        in_sems,
    )
    outs = [
        pltpu.make_async_copy(s, t, out_sems.at[i])
        for i, (s, t) in enumerate(
            ((normed_ref, normed_hbm), (inverse_ref, inverse_hbm), (pre_ref, pre_hbm), (pred_ref, pred_hbm))
        )
    ]
    for load in loads[:5]:
        load.wait()

    def gather(counts_ref):
        return (
            dot(counts_ref[:, :size], first_ref[...])
            + dot(counts_ref[:, size : 2 * size], own_ref[...])
            + dot(counts_ref[:, 2 * size :], second_ref[...])
        )

    sum_ref[...] = gather(high_ref) + grid_ref[...].astype(jnp.float32)

    @pl.when(over_ref[0] > 0)
    def _():
        copy = pltpu.make_async_copy(low_hbm, low_ref, low_sem)
        copy.start()
        copy.wait()
        sum_ref[...] += gather(low_ref)

    summed = sum_ref[...]
    centered = summed - jnp.mean(summed, axis=-1, keepdims=True)
    inverse = lax.rsqrt(jnp.mean(centered * centered, axis=-1, keepdims=True) + EPS)
    normed = centered * inverse
    normed_ref[...] = normed
    inverse_ref[...] = inverse
    outs[0].start()
    outs[1].start()
    loads[5].wait()
    pre_act = dot(normed.astype(jnp.bfloat16), node_ref[...])
    pre_ref[...] = pre_act
    outs[2].start()
    hidden = (pre_act * (0.5 + 0.5 * jnp.tanh(0.5 * pre_act))).astype(jnp.bfloat16)
    loads[6].wait()
    pred = dot(hidden, turned_ref[...])
    pred_ref[...] = pred
    outs[3].start()
    largest = jnp.max(jnp.abs(pred), axis=0, keepdims=True)
    code = jnp.ceil(jnp.log2(jnp.maximum(largest, 2.0**LOWEST)) * CODE)
    whole = jnp.round(pred * (jnp.exp2(code * (-1.0 / CODE)) * STEPS))
    packed_ref[...] = fold(whole, code).astype(jnp.int16)
    members = shared_hbm.shape[0]
    shares = start_all([packed_ref] * members, [shared_hbm.at[m] for m in range(members)], share_sems)
    for copy in outs + shares:
        copy.wait()


def fold(values, code=None):
    rest = values[MAIN:, :]
    tail = jnp.zeros((MAIN - FOLDS * rest.shape[0], LANES), values.dtype)
    if code is not None:
        wide = jnp.broadcast_to(code, tail.shape)
        row = lax.broadcasted_iota(jnp.int32, tail.shape, 0)
        for k in range(FOLDS):
            tail = jnp.where(row == k, turn(wide, VARS - FOLD * k), tail)
    pieces = [turn(rest, VARS - FOLD * k) for k in range(FOLDS)] + [tail]
    spare = jnp.concatenate(pieces, axis=0)
    main = values[:MAIN, :]
    lane = lanes_of(main)
    return jnp.where(lane < VARS, main, jnp.where(lane < VARS + FOLD, spare, jnp.zeros_like(main)))


def unfold(values, rows):
    rest_rows = rows - MAIN
    lane = lax.broadcasted_iota(jnp.int32, (rest_rows, LANES), 1)
    rest = jnp.zeros((rest_rows, LANES), values.dtype)
    for k in range(FOLDS):
        piece = turn(values[k * rest_rows : (k + 1) * rest_rows, :], FOLD * k - VARS)
        rest = jnp.where((lane >= FOLD * k) & (lane < FOLD * (k + 1)), piece, rest)
    return jnp.concatenate([values, rest], axis=0)


def middle_kernel(
    pre_ref, pred_ref, target_ref, area_ref, var_ref, node_ref,
    gate_ref, lead_ref, weight_ref, fold_ref, turned_ref, *, pair_scale
):
    pre_act = pre_ref[...]
    gate_sig = 0.5 + 0.5 * jnp.tanh(0.5 * pre_act)
    gate_ref[...] = gate_sig * (1.0 + pre_act * (1.0 - gate_sig))
    variables, grid_rows = target_ref.shape
    padded = jnp.concatenate(
        [target_ref[...], jnp.zeros((LANES - variables, grid_rows), jnp.float32)], axis=0
    )
    weight = area_ref[...] * var_ref[...]
    lead_ref[...] = weight * smooth_slope(pred_ref[...] - padded.T)
    weight_ref[...] = weight * pair_scale
    fold_ref[...] = fold(pred_ref[...])
    turned_ref[...] = node_ref[...].T


def backward_kernel(
    me_ref, over_ref,
    everyone_hbm, fold_hbm, lead_hbm, weight_hbm, pad_hbm, gate_hbm, turned_hbm, normed_hbm, inverse_hbm, counts_hbm, low_hbm,
    first_hbm, second_hbm, blocks_hbm, send_hbm,
    everyone_ref, fold_ref, lead_ref, weight_ref, pad_ref, gate_ref, turned_ref, normed_ref, inverse_ref, counts_ref, low_ref,
    first_ref, second_ref, blocks_ref, send_ref, scale_ref,
    in_sems, low_sem, out_sems,
):
    loads = start_all(
        (everyone_hbm, fold_hbm, lead_hbm, weight_hbm, pad_hbm, gate_hbm, turned_hbm, normed_hbm, inverse_hbm, counts_hbm),
        (everyone_ref, fold_ref, lead_ref, weight_ref, pad_ref, gate_ref, turned_ref, normed_ref, inverse_ref, counts_ref),
        in_sems,
    )
    outs = [
        pltpu.make_async_copy(s, t, out_sems.at[i])
        for i, (s, t) in enumerate(
            ((send_ref, send_hbm), (first_ref, first_hbm), (second_ref, second_hbm), (blocks_ref, blocks_hbm))
        )
    ]
    members = everyone_ref.shape[0]
    grid_rows, width = normed_ref.shape
    rest_rows = grid_rows - MAIN
    me = me_ref[0]
    first = FOLDS * rest_rows
    lane = lax.broadcasted_iota(jnp.int32, (members, LANES), 1)
    loads[0].wait()
    loads[1].wait()
    tails = everyone_ref[:, first:MAIN, :].astype(jnp.float32)
    code = jnp.zeros((members, LANES), jnp.float32)
    for k in range(FOLDS):
        piece = turn(tails[:, k, :], FOLD * k - VARS)
        code = jnp.where((lane >= FOLD * k) & (lane < FOLD * (k + 1)), piece, code)
    scale = jnp.exp2(code * (1.0 / CODE)) * (1.0 / STEPS)
    for k in range(FOLDS):
        scale_ref[k] = jnp.where(lane < VARS, scale, turn(scale, VARS - FOLD * k))

    bounds = [(k * rest_rows, (k + 1) * rest_rows) for k in range(FOLDS)] + [(first, MAIN)]
    parts = [jnp.zeros((high - low, LANES), jnp.float32) for low, high in bounds]
    for step in range(1, members):
        other = lax.rem(me + step, members)
        for i, (low, high) in enumerate(bounds):
            factor = scale_ref[min(i, FOLDS - 1), pl.ds(other, 1), :]
            theirs = everyone_ref[other, low:high, :].astype(jnp.float32) * factor
            parts[i] = parts[i] + smooth_slope(fold_ref[low:high, :] - theirs)
    pair_sum = unfold(jnp.concatenate(parts, axis=0), grid_rows)
    real = lanes_of(pair_sum) < VARS
    for load in loads[2:6]:
        load.wait()
    grad_pred = lead_ref[...] - weight_ref[...] * jnp.where(real, pair_sum, 0.0)
    grad_hidden = dot(grad_pred.astype(jnp.bfloat16), pad_ref[...])
    grad_pre = (grad_hidden * gate_ref[...]).astype(jnp.bfloat16)
    for load in loads[6:]:
        load.wait()
    grad_normed = dot(grad_pre, turned_ref[...])
    normed = normed_ref[...]
    grad_summed = inverse_ref[...] * (
        grad_normed
        - jnp.mean(grad_normed, axis=-1, keepdims=True)
        - normed * jnp.mean(grad_normed * normed, axis=-1, keepdims=True)
    )
    send_ref[...] = grad_summed.astype(jnp.bfloat16)
    outs[0].start()
    half = grid_rows // 2
    lower = lax.broadcasted_iota(jnp.int32, (half, LANES), 1) < LANES // 2
    for pair in range(width // LANES):
        at = slice(pair * LANES, (pair + 1) * LANES)
        top = grad_summed[:half, at]
        bottom = grad_summed[half:, at]
        blocks_ref[2 * pair] = jnp.where(lower, top, turn(bottom, LANES // 2)).astype(jnp.bfloat16)
        blocks_ref[2 * pair + 1] = jnp.where(lower, turn(top, LANES // 2), bottom).astype(jnp.bfloat16)
    outs[3].start()
    size = first_ref.shape[0]
    first_ref[...] = dot(counts_ref[:, :grid_rows], send_ref[...]).astype(jnp.bfloat16)
    second_ref[...] = dot(counts_ref[:, 2 * grid_rows :], send_ref[...]).astype(jnp.bfloat16)

    @pl.when(over_ref[0] > 0)
    def _():
        copy = pltpu.make_async_copy(low_hbm, low_ref, low_sem)
        copy.start()
        copy.wait()
        for ref, at in ((first_ref, slice(0, grid_rows)), (second_ref, slice(2 * grid_rows, 3 * grid_rows))):
            total = dot(counts_ref[:, at], send_ref[...]) + dot(low_ref[:, at], send_ref[...])
            ref[...] = total.astype(jnp.bfloat16)

    outs[1].start()
    outs[2].start()
    for copy in outs:
        copy.wait()


def own_kernel(over_ref, high_ref, low_ref, send_ref, out_ref):
    rows = send_ref.shape[0]
    out_ref[...] = dot(high_ref[:, rows : 2 * rows], send_ref[...])

    @pl.when(over_ref[0] > 0)
    def _():
        out_ref[...] += dot(low_ref[:, rows : 2 * rows], send_ref[...])


def member_sum_kernel(landed_ref, out_ref):
    total = landed_ref[0].astype(jnp.float32)
    for member in range(1, landed_ref.shape[0]):
        total = total + landed_ref[member].astype(jnp.float32)
    half = total.shape[0]
    share = out_ref.shape[0]
    flipped = total.T
    out_ref[:, :half] = flipped[:share, :].astype(jnp.bfloat16)
    out_ref[:, half:] = flipped[share:, :].astype(jnp.bfloat16)


def shape(dims, dtype):
    return jax.ShapeDtypeStruct(dims, dtype)


def whole(value):
    dims = value.shape
    return pl.BlockSpec(dims, lambda step: (0,) * len(dims))


SMEM = pl.BlockSpec(memory_space=pltpu.SMEM)
HBM = pl.BlockSpec(memory_space=pltpu.HBM)


def cost_of(mega_flops, mega_bytes):
    return pl.CostEstimate(
        flops=mega_flops << 20, bytes_accessed=mega_bytes << 20, transcendentals=0
    )


PARAMS = pltpu.CompilerParams(vmem_limit_bytes=VMEM_LIMIT)


def staged(kernel, outs, ins, scalars_in=(), scalars_out=(), cost=(0, 0)):
    return pl.pallas_call(
        kernel,
        grid=(1,),
        out_shape=list(outs),
        in_specs=[SMEM if i in scalars_in else whole(v) for i, v in enumerate(ins)],
        out_specs=[SMEM if i in scalars_out else whole(v) for i, v in enumerate(outs)],
        compiler_params=PARAMS,
        cost_estimate=cost_of(*cost),
    )(*ins)


def held(value):
    return pltpu.VMEM(value.shape, value.dtype)


def per_device(
    mesh_latent, grid_latent, node_weight, out_weight, target, area_weight, var_weight, edge_src, edge_dst, edge_count
):
    f32, b16, i32 = jnp.float32, jnp.bfloat16, jnp.int32
    members = lax.axis_size("member")
    me = lax.axis_index("member").astype(i32)[None]
    latent = mesh_latent[0]
    mesh_rows = latent.shape[0]
    grid_rows, width = grid_latent.shape
    variables = out_weight.shape[0]
    dma = pltpu.SemaphoreType.DMA

    first = to_neighbours(latent, 0)
    second = to_neighbours(latent, 1)
    high, low, back_high, back_low, over, out_pad, out_turned = staged(
        edges_kernel,
        [
            shape((grid_rows, 3 * mesh_rows), b16),
            shape((grid_rows, 3 * mesh_rows), b16),
            shape((mesh_rows, 3 * grid_rows), b16),
            shape((mesh_rows, 3 * grid_rows), b16),
            shape((1,), i32),
            shape((LANES, width), b16),
            shape((width, LANES), b16),
        ],
        [me, edge_count, edge_src[0], edge_dst[0], out_weight],
        scalars_in=(0, 1),
        scalars_out=(4,),
        cost=(400, 3),
    )

    ins = [high, latent, first, second, grid_latent, node_weight, out_turned, low]
    outs = [
        shape((members, MAIN, LANES), jnp.int16),
        shape((grid_rows, LANES), f32),
        shape((grid_rows, width), f32),
        shape((grid_rows, 1), f32),
        shape((grid_rows, width), f32),
    ]
    shared, pred, normed, inverse, pre_act = pl.pallas_call(
        forward_kernel,
        out_shape=outs,
        in_specs=[SMEM] + [HBM] * len(ins),
        out_specs=[HBM] * len(outs),
        scratch_shapes=[held(v) for v in ins]
        + [pltpu.VMEM((MAIN, LANES), jnp.int16)]
        + [held(v) for v in outs[1:]]
        + [pltpu.VMEM((grid_rows, width), f32), dma((len(ins) - 1,)), dma, dma((len(outs) - 1,)), dma((members,))],
        compiler_params=PARAMS,
        cost_estimate=cost_of(1000, 8),
    )(over, *ins)
    everyone = lax.all_to_all(shared, "member", 0, 0, tiled=True)

    pair_scale = (1.0 - (1.0 - ALPHA) / members) / (members - 1)
    gate, lead, weight, folded, node_turned = staged(
        functools.partial(middle_kernel, pair_scale=pair_scale),
        [
            shape((grid_rows, width), f32),
            shape((grid_rows, LANES), f32),
            shape((grid_rows, LANES), f32),
            shape((MAIN, LANES), f32),
            shape((width, width), b16),
        ],
        [
            pre_act,
            pred,
            target,
            area_weight[:, None],
            jnp.pad(var_weight, (0, LANES - variables))[None, :],
            node_weight,
        ],
        cost=(10, 8),
    )

    ins = [everyone, folded, lead, weight, out_pad, gate, node_turned, normed, inverse, back_high, back_low]
    outs = [
        shape((mesh_rows, width), b16),
        shape((mesh_rows, width), b16),
        shape((members, grid_rows // 2, LANES), b16),
        shape((grid_rows, width), b16),
    ]
    first_part, second_part, blocks, grad_send = pl.pallas_call(
        backward_kernel,
        out_shape=outs,
        in_specs=[SMEM] * 2 + [HBM] * len(ins),
        out_specs=[HBM] * len(outs),
        scratch_shapes=[held(v) for v in ins + outs]
        + [pltpu.VMEM((FOLDS, members, LANES), f32), dma((len(ins) - 1,)), dma, dma((len(outs),))],
        compiler_params=PARAMS,
        cost_estimate=cost_of(1000, 8),
    )(me, over, *ins)
    first_back = to_neighbours(first_part, 0)
    second_back = to_neighbours(second_part, 1)
    landed = lax.all_to_all(blocks, "member", 0, 0, tiled=True)
    (own_part,) = staged(
        own_kernel,
        [shape((mesh_rows, width), f32)],
        [over, back_high, back_low, grad_send],
        scalars_in=(0,),
        cost=(130, 2),
    )
    (grid_share,) = staged(
        member_sum_kernel, [shape((width // members, grid_rows), b16)], [landed], cost=(1, 1)
    )
    grad_latent = own_part + first_back.astype(f32) + second_back.astype(f32)
    return (grad_latent.astype(b16)[None], grid_share.T)


def solution(mesh):
    return jax.shard_map(
        per_device,
        mesh=mesh,
        in_specs=(
            P("member", "grid", None),
            P("grid", None),
            P(),
            P(),
            P(None, "grid"),
            P("grid"),
            P(),
            P("grid", None, None),
            P("grid", None, None),
            P("grid", None),
        ),
        out_specs=(P("member", "grid", None), P("grid", "member")),
        check_vma=False,
    )
```

```python
import functools

import jax
import jax.numpy as jnp
from jax import lax
from jax.experimental import pallas as pl
from jax.experimental.pallas import tpu as pltpu
from jax.sharding import PartitionSpec as P

SMOOTH = 0.1
ALPHA = 0.95
EPS = 1e-05
LANES = 128
VARS = 100
MAIN = 208
FOLD = 25
FOLDS = 4
STEPS = 32767.0
CODE = 256.0
LOWEST = -20.0
VMEM_LIMIT = 20 * 1024 * 1024


def to_neighbours(value, side):
    members, shards = lax.axis_size("member"), lax.axis_size("grid")
    pairs = [
        (member * shards + shard, member * shards + (shard + (1 if member % 2 == side else -1)) % shards)
        for member in range(members)
        for shard in range(shards)
    ]
    return lax.ppermute(value, ("member", "grid"), pairs)


def smooth_slope(difference):
    return difference * lax.rsqrt(difference * difference + SMOOTH * SMOOTH)


def turn(values, shift):
    shift = shift % LANES
    return pltpu.roll(values, shift, 1) if shift else values


def lanes_of(values):
    return lax.broadcasted_iota(jnp.int32, values.shape, 1)


def one_hot(picks, rows):
    places = lax.broadcasted_iota(jnp.int32, (rows, picks.shape[1]), 0)
    return jnp.where(places == picks, 1.0, 0.0).astype(jnp.bfloat16)


def count_pairs(row_hot, column_hot):
    return lax.dot_general(
        row_hot, column_hot, (((1,), (1,)), ((), ())), preferred_element_type=jnp.float32
    )


def store_counts(counts, at, high_ref, low_ref):
    high = counts.astype(jnp.bfloat16)
    high_ref[:, at] = high
    low_ref[:, at] = (counts - high.astype(jnp.float32)).astype(jnp.bfloat16)
    return jnp.max(counts)


def edges_kernel(
    me_ref, count_ref, src_ref, dst_ref, out_ref, target_ref, area_ref, var_ref, latent_hbm, grid_hbm, node_hbm,
    over_ref, low_hbm, back_low_hbm,
    high_ref, back_high_ref, base_ref, node_ref, node_turned_ref, pad_ref, turned_ref, target_turned_ref, weight_ref,
    latent_ref, grid_ref, low_ref, back_low_ref, in_sems, out_sems,
):
    loads = start_all((latent_hbm, grid_hbm, node_hbm), (latent_ref, grid_ref, node_ref), in_sems)
    size = high_ref.shape[0]
    slots = src_ref.shape[1]
    slot = lax.broadcasted_iota(jnp.int32, (1, slots), 1)
    odd = lax.rem(me_ref[0], 2)
    most = 0.0
    for place, offset in enumerate((2 - 2 * odd, 1, 2 * odd)):
        live = slot < count_ref[0, offset]
        targets = one_hot(jnp.where(live, dst_ref[pl.ds(offset, 1), :], -1), size)
        sources = one_hot(src_ref[pl.ds(offset, 1), :], size)
        counts = count_pairs(targets, sources)
        most = jnp.maximum(
            most, store_counts(counts, slice(place * size, (place + 1) * size), high_ref, low_ref)
        )
        back = 2 - place
        store_counts(
            count_pairs(sources, targets), slice(back * size, (back + 1) * size), back_high_ref, back_low_ref
        )
    over_ref[0] = (most > 256.0).astype(jnp.int32)
    stores = start_all((low_ref, back_low_ref), (low_hbm, back_low_hbm), out_sems)
    variables, width = out_ref.shape
    padded = jnp.concatenate(
        [out_ref[...].astype(jnp.float32), jnp.zeros((LANES - variables, width), jnp.float32)], axis=0
    )
    pad_ref[...] = padded.astype(jnp.bfloat16)
    turned_ref[...] = padded.T.astype(jnp.bfloat16)
    target = jnp.concatenate(
        [target_ref[...], jnp.zeros((LANES - variables, target_ref.shape[1]), jnp.float32)], axis=0
    )
    target_turned_ref[...] = target.T
    weight_ref[...] = area_ref[...] * var_ref[...]
    for load in loads:
        load.wait()
    node_turned_ref[...] = node_ref[...].T
    own = slice(size, 2 * size)
    base_ref[...] = dot(high_ref[:, own], latent_ref[...]) + grid_ref[...].astype(jnp.float32)

    @pl.when(over_ref[0] > 0)
    def _():
        base_ref[...] += dot(low_ref[:, own], latent_ref[...])

    for store in stores:
        store.wait()


def start_all(sources, targets, sems):
    copies = [pltpu.make_async_copy(s, t, sems.at[i]) for i, (s, t) in enumerate(zip(sources, targets))]
    for copy in copies:
        copy.start()
    return copies


def dot(left, right):
    return jnp.dot(left, right, preferred_element_type=jnp.float32)


def forward_kernel(
    over_ref, high_ref, base_ref, first_ref, second_ref, node_ref, turned_ref, target_ref, weight_ref, low_hbm,
    shared_ref, fold_ref, lead_ref, gate_ref, normed_ref, inverse_ref,
    low_ref, sum_ref, low_sem,
):
    size = first_ref.shape[0]

    def gather(counts_ref):
        return dot(counts_ref[:, :size], first_ref[...]) + dot(counts_ref[:, 2 * size :], second_ref[...])

    sum_ref[...] = gather(high_ref) + base_ref[...]

    @pl.when(over_ref[0] > 0)
    def _():
        copy = pltpu.make_async_copy(low_hbm, low_ref, low_sem)
        copy.start()
        copy.wait()
        sum_ref[...] += gather(low_ref)

    summed = sum_ref[...]
    centered = summed - jnp.mean(summed, axis=-1, keepdims=True)
    inverse = lax.rsqrt(jnp.mean(centered * centered, axis=-1, keepdims=True) + EPS)
    normed = centered * inverse
    normed_ref[...] = normed
    inverse_ref[...] = inverse
    pre_act = dot(normed.astype(jnp.bfloat16), node_ref[...])
    gate_sig = 0.5 + 0.5 * jnp.tanh(0.5 * pre_act)
    gate_ref[...] = gate_sig * (1.0 + pre_act * (1.0 - gate_sig))
    hidden = (pre_act * gate_sig).astype(jnp.bfloat16)
    pred = dot(hidden, turned_ref[...])
    largest = jnp.max(jnp.abs(pred), axis=0, keepdims=True)
    code = jnp.ceil(jnp.log2(jnp.maximum(largest, 2.0**LOWEST)) * CODE)
    whole = jnp.round(pred * (jnp.exp2(code * (-1.0 / CODE)) * STEPS))
    packed = fold(whole, code).astype(jnp.int16)
    for member in range(shared_ref.shape[0]):
        shared_ref[member] = packed
    lead_ref[...] = weight_ref[...] * smooth_slope(pred - target_ref[...])
    fold_ref[...] = fold(pred)


def fold(values, code=None):
    rest = values[MAIN:, :]
    tail = jnp.zeros((MAIN - FOLDS * rest.shape[0], LANES), values.dtype)
    if code is not None:
        wide = jnp.broadcast_to(code, tail.shape)
        row = lax.broadcasted_iota(jnp.int32, tail.shape, 0)
        for k in range(FOLDS):
            tail = jnp.where(row == k, turn(wide, VARS - FOLD * k), tail)
    pieces = [turn(rest, VARS - FOLD * k) for k in range(FOLDS)] + [tail]
    spare = jnp.concatenate(pieces, axis=0)
    main = values[:MAIN, :]
    lane = lanes_of(main)
    return jnp.where(lane < VARS, main, jnp.where(lane < VARS + FOLD, spare, jnp.zeros_like(main)))


def unfold(values, rows):
    rest_rows = rows - MAIN
    lane = lax.broadcasted_iota(jnp.int32, (rest_rows, LANES), 1)
    rest = jnp.zeros((rest_rows, LANES), values.dtype)
    for k in range(FOLDS):
        piece = turn(values[k * rest_rows : (k + 1) * rest_rows, :], FOLD * k - VARS)
        rest = jnp.where((lane >= FOLD * k) & (lane < FOLD * (k + 1)), piece, rest)
    return jnp.concatenate([values, rest], axis=0)


def backward_kernel(
    me_ref, over_ref, everyone_ref, fold_ref, lead_ref, weight_ref, gate_ref,
    pad_ref, turned_ref, normed_ref, inverse_ref, high_ref, low_hbm,
    blocks_ref, first_ref, second_ref, send_ref,
    low_ref, scale_ref, low_sem, *, pair_scale
):
    members = everyone_ref.shape[0]
    grid_rows, width = normed_ref.shape
    rest_rows = grid_rows - MAIN
    me = me_ref[0]
    first = FOLDS * rest_rows
    lane = lax.broadcasted_iota(jnp.int32, (members, LANES), 1)
    tails = everyone_ref[:, first:MAIN, :].astype(jnp.float32)
    code = jnp.zeros((members, LANES), jnp.float32)
    for k in range(FOLDS):
        piece = turn(tails[:, k, :], FOLD * k - VARS)
        code = jnp.where((lane >= FOLD * k) & (lane < FOLD * (k + 1)), piece, code)
    scale = jnp.exp2(code * (1.0 / CODE)) * (1.0 / STEPS)
    for k in range(FOLDS):
        scale_ref[k] = jnp.where(lane < VARS, scale, turn(scale, VARS - FOLD * k))

    bounds = [(k * rest_rows, (k + 1) * rest_rows) for k in range(FOLDS)] + [(first, MAIN)]
    parts = [jnp.zeros((high - low, LANES), jnp.float32) for low, high in bounds]
    for step in range(1, members):
        other = lax.rem(me + step, members)
        for i, (low, high) in enumerate(bounds):
            factor = scale_ref[min(i, FOLDS - 1), pl.ds(other, 1), :]
            theirs = everyone_ref[other, low:high, :].astype(jnp.float32) * factor
            parts[i] = parts[i] + smooth_slope(fold_ref[low:high, :] - theirs)
    pair_sum = unfold(jnp.concatenate(parts, axis=0), grid_rows)
    real = lanes_of(pair_sum) < VARS
    grad_pred = lead_ref[...] - pair_scale * weight_ref[...] * jnp.where(real, pair_sum, 0.0)
    grad_hidden = dot(grad_pred.astype(jnp.bfloat16), pad_ref[...])
    grad_pre = (grad_hidden * gate_ref[...]).astype(jnp.bfloat16)
    grad_normed = dot(grad_pre, turned_ref[...])
    normed = normed_ref[...]
    grad_summed = inverse_ref[...] * (
        grad_normed
        - jnp.mean(grad_normed, axis=-1, keepdims=True)
        - normed * jnp.mean(grad_normed * normed, axis=-1, keepdims=True)
    )
    send_ref[...] = grad_summed.astype(jnp.bfloat16)
    half = grid_rows // 2
    lower = lax.broadcasted_iota(jnp.int32, (half, LANES), 1) < LANES // 2
    for pair in range(width // LANES):
        at = slice(pair * LANES, (pair + 1) * LANES)
        top = grad_summed[:half, at]
        bottom = grad_summed[half:, at]
        blocks_ref[2 * pair] = jnp.where(lower, top, turn(bottom, LANES // 2)).astype(jnp.bfloat16)
        blocks_ref[2 * pair + 1] = jnp.where(lower, turn(top, LANES // 2), bottom).astype(jnp.bfloat16)
    places = ((first_ref, slice(0, grid_rows)), (second_ref, slice(2 * grid_rows, 3 * grid_rows)))
    for ref, at in places:
        ref[...] = dot(high_ref[:, at], send_ref[...]).astype(jnp.bfloat16)

    @pl.when(over_ref[0] > 0)
    def _():
        copy = pltpu.make_async_copy(low_hbm, low_ref, low_sem)
        copy.start()
        copy.wait()
        for ref, at in places:
            total = dot(high_ref[:, at], send_ref[...]) + dot(low_ref[:, at], send_ref[...])
            ref[...] = total.astype(jnp.bfloat16)


def tail_kernel(
    over_ref, high_ref, send_ref, first_ref, second_ref, landed_ref, low_hbm, out_hbm, share_ref,
    low_ref, sum_ref, out_ref, low_sem, out_sems
):
    rows = send_ref.shape[0]
    own = slice(rows, 2 * rows)
    sum_ref[...] = dot(high_ref[:, own], send_ref[...])

    @pl.when(over_ref[0] > 0)
    def _():
        copy = pltpu.make_async_copy(low_hbm, low_ref, low_sem)
        copy.start()
        copy.wait()
        sum_ref[...] += dot(low_ref[:, own], send_ref[...])

    parts = out_sems.shape[0]
    stores = []
    for part in range(parts):
        at = slice(part * rows // parts, (part + 1) * rows // parts)
        total = sum_ref[at, :] + first_ref[at, :].astype(jnp.float32) + second_ref[at, :].astype(jnp.float32)
        out_ref[at, :] = total.astype(jnp.bfloat16)
        stores.append(pltpu.make_async_copy(out_ref.at[at, :], out_hbm.at[at, :], out_sems.at[part]))
        stores[-1].start()
    total = landed_ref[0].astype(jnp.float32)
    for member in range(1, landed_ref.shape[0]):
        total = total + landed_ref[member].astype(jnp.float32)
    half = total.shape[0]
    share = share_ref.shape[0]
    flipped = total.T
    share_ref[:, :half] = flipped[:share, :].astype(jnp.bfloat16)
    share_ref[:, half:] = flipped[share:, :].astype(jnp.bfloat16)
    for store in stores:
        store.wait()


def shape(dims, dtype):
    return jax.ShapeDtypeStruct(dims, dtype)


SMEM = pl.BlockSpec(memory_space=pltpu.SMEM)
VMEM = pl.BlockSpec(memory_space=pltpu.VMEM)
HBM = pl.BlockSpec(memory_space=pltpu.HBM)


def in_hbm(*values):
    return [pltpu.with_memory_space_constraint(v, pltpu.HBM) for v in values]


def cost_of(mega_flops, mega_bytes):
    return pl.CostEstimate(
        flops=mega_flops << 20, bytes_accessed=mega_bytes << 20, transcendentals=0
    )


PARAMS = pltpu.CompilerParams(vmem_limit_bytes=VMEM_LIMIT)


def held(value):
    return pltpu.VMEM(value.shape, value.dtype)


def per_device(
    mesh_latent, grid_latent, node_weight, out_weight, target, area_weight, var_weight, edge_src, edge_dst, edge_count
):
    f32, b16, i32 = jnp.float32, jnp.bfloat16, jnp.int32
    members = lax.axis_size("member")
    me = lax.axis_index("member").astype(i32)[None]
    latent = mesh_latent[0]
    mesh_rows = latent.shape[0]
    grid_rows, width = grid_latent.shape
    variables = out_weight.shape[0]
    dma = pltpu.SemaphoreType.DMA

    first = to_neighbours(latent, 0)
    second = to_neighbours(latent, 1)
    outs = [
        shape((1,), i32),
        pltpu.HBM((grid_rows, 3 * mesh_rows), b16),
        pltpu.HBM((mesh_rows, 3 * grid_rows), b16),
        pltpu.VMEM((grid_rows, 3 * mesh_rows), b16),
        pltpu.VMEM((mesh_rows, 3 * grid_rows), b16),
        pltpu.VMEM((grid_rows, width), f32),
        pltpu.VMEM((width, width), b16),
        pltpu.VMEM((width, width), b16),
        pltpu.VMEM((LANES, width), b16),
        pltpu.VMEM((width, LANES), b16),
        pltpu.VMEM((grid_rows, LANES), f32),
        pltpu.VMEM((grid_rows, LANES), f32),
    ]
    (
        over, low, back_low, high, back_high, base, node, node_turned, out_pad, out_turned, target_turned, weight
    ) = pl.pallas_call(
        edges_kernel,
        out_shape=outs,
        in_specs=[SMEM] * 2 + [VMEM] * 6 + [HBM] * 3,
        out_specs=[SMEM] + [HBM] * 2 + [VMEM] * 9,
        scratch_shapes=[held(v) for v in (latent, grid_latent, *outs[1:3])] + [dma((3,)), dma((2,))],
        compiler_params=PARAMS,
        cost_estimate=cost_of(500, 8),
    )(
        me,
        edge_count,
        edge_src[0],
        edge_dst[0],
        out_weight,
        target,
        area_weight[:, None],
        jnp.pad(var_weight, (0, LANES - variables))[None, :],
        *in_hbm(latent, grid_latent, node_weight),
    )

    outs = [
        pltpu.VMEM((members, MAIN, LANES), jnp.int16),
        pltpu.VMEM((MAIN, LANES), f32),
        pltpu.VMEM((grid_rows, LANES), f32),
        pltpu.VMEM((grid_rows, width), f32),
        pltpu.VMEM((grid_rows, width), f32),
        pltpu.VMEM((grid_rows, 1), f32),
    ]
    shared, folded, lead, gate, normed, inverse = pl.pallas_call(
        forward_kernel,
        out_shape=outs,
        in_specs=[SMEM] + [VMEM] * 8 + [HBM],
        out_specs=[VMEM] * len(outs),
        scratch_shapes=[held(low), pltpu.VMEM((grid_rows, width), f32), dma],
        compiler_params=PARAMS,
        cost_estimate=cost_of(1000, 8),
    )(over, high, base, first, second, node, out_turned, target_turned, weight, *in_hbm(low))
    everyone = lax.all_to_all(shared, "member", 0, 0, tiled=True)

    pair_scale = (1.0 - (1.0 - ALPHA) / members) / (members - 1)
    outs = [
        pltpu.VMEM((members, grid_rows // 2, LANES), b16),
        pltpu.VMEM((mesh_rows, width), b16),
        pltpu.VMEM((mesh_rows, width), b16),
        pltpu.VMEM((grid_rows, width), b16),
    ]
    blocks, first_part, second_part, grad_send = pl.pallas_call(
        functools.partial(backward_kernel, pair_scale=pair_scale),
        out_shape=outs,
        in_specs=[SMEM] * 2 + [VMEM] * 10 + [HBM],
        out_specs=[VMEM] * 4,
        scratch_shapes=[held(back_low), pltpu.VMEM((FOLDS, members, LANES), f32), dma],
        compiler_params=PARAMS,
        cost_estimate=cost_of(1000, 8),
    )(
        me, over, everyone, folded, lead, weight, gate, out_pad, node_turned, normed, inverse, back_high,
        *in_hbm(back_low),
    )
    landed = lax.all_to_all(blocks, "member", 0, 0, tiled=True)
    first_back = to_neighbours(first_part, 0)
    second_back = to_neighbours(second_part, 1)
    grad_latent, grid_share = pl.pallas_call(
        tail_kernel,
        out_shape=[pltpu.HBM((mesh_rows, width), b16), shape((width // members, grid_rows), b16)],
        in_specs=[SMEM] + [VMEM] * 5 + [HBM],
        out_specs=[HBM, VMEM],
        scratch_shapes=[
            held(back_low),
            pltpu.VMEM((mesh_rows, width), f32),
            pltpu.VMEM((mesh_rows, width), b16),
            dma,
            dma((4,)),
        ],
        compiler_params=PARAMS,
        cost_estimate=cost_of(130, 3),
    )(over, back_high, grad_send, first_back, second_back, landed, *in_hbm(back_low))
    return (grad_latent[None], grid_share.T)


def solution(mesh):
    return jax.shard_map(
        per_device,
        mesh=mesh,
        in_specs=(
            P("member", "grid", None),
            P("grid", None),
            P(),
            P(),
            P(None, "grid"),
            P("grid"),
            P(),
            P("grid", None, None),
            P("grid", None, None),
            P("grid", None),
        ),
        out_specs=(P("member", "grid", None), P("grid", "member")),
        check_vma=False,
    )
```

```python
import functools

import jax
import jax.numpy as jnp
from jax import lax
from jax.experimental import pallas as pl
from jax.experimental.pallas import tpu as pltpu
from jax.sharding import PartitionSpec as P

SMOOTH = 0.1
ALPHA = 0.95
EPS = 1e-05
LANES = 128
VARS = 100
MAIN = 208
FOLD = 25
FOLDS = 4
STEPS = 32767.0
CODE = 256.0
LOWEST = -20.0
VMEM_LIMIT = 20 * 1024 * 1024


def to_neighbours(value, side):
    members, shards = lax.axis_size("member"), lax.axis_size("grid")
    pairs = [
        (member * shards + shard, member * shards + (shard + (1 if member % 2 == side else -1)) % shards)
        for member in range(members)
        for shard in range(shards)
    ]
    return lax.ppermute(value, ("member", "grid"), pairs)


def smooth_slope(difference):
    return difference * lax.rsqrt(difference * difference + SMOOTH * SMOOTH)


def turn(values, shift):
    shift = shift % LANES
    return pltpu.roll(values, shift, 1) if shift else values


def lanes_of(values):
    return lax.broadcasted_iota(jnp.int32, values.shape, 1)


def one_hot(picks, rows):
    places = lax.broadcasted_iota(jnp.int32, (rows, picks.shape[1]), 0)
    return jnp.where(places == picks, 1.0, 0.0).astype(jnp.bfloat16)


def count_pairs(row_hot, column_hot):
    return lax.dot_general(
        row_hot, column_hot, (((1,), (1,)), ((), ())), preferred_element_type=jnp.float32
    )


def store_counts(counts, at, high_ref, low_ref):
    high = counts.astype(jnp.bfloat16)
    high_ref[:, at] = high
    low_ref[:, at] = (counts - high.astype(jnp.float32)).astype(jnp.bfloat16)
    return jnp.max(counts)


def edges_kernel(
    me_hbm, count_hbm, src_hbm, dst_hbm, area_hbm, var_hbm, out_hbm, target_hbm, node_hbm, latent_hbm, grid_hbm,
    flags_ref, low_hbm, back_low_hbm,
    high_ref, back_high_ref, base_ref, node_ref, node_turned_ref, pad_ref, turned_ref, target_turned_ref, weight_ref,
    me_ref, count_ref, src_ref, dst_ref, area_ref, var_ref, out_ref, target_ref, latent_ref, grid_ref,
    low_ref, back_low_ref, in_sems, out_sems,
):
    loads = start_all(
        (me_hbm, count_hbm, src_hbm, dst_hbm, area_hbm, var_hbm, out_hbm, target_hbm, node_hbm, latent_hbm, grid_hbm),
        (me_ref, count_ref, src_ref, dst_ref, area_ref, var_ref, out_ref, target_ref, node_ref, latent_ref, grid_ref),
        in_sems,
    )
    size = high_ref.shape[0]
    slots = src_ref.shape[1] // 3
    slot = lax.broadcasted_iota(jnp.int32, (1, slots), 1)
    for load in loads[:4]:
        load.wait()
    odd = lax.rem(me_ref[0], 2)
    most = 0.0
    for place, offset in enumerate((2 - 2 * odd, 1, 2 * odd)):
        at = pl.ds(pl.multiple_of(offset * slots, LANES), slots)
        live = slot < count_ref[0, offset]
        targets = one_hot(jnp.where(live, dst_ref[:, at], -1), size)
        sources = one_hot(src_ref[:, at], size)
        counts = count_pairs(targets, sources)
        most = jnp.maximum(
            most, store_counts(counts, slice(place * size, (place + 1) * size), high_ref, low_ref)
        )
        back = 2 - place
        store_counts(
            count_pairs(sources, targets), slice(back * size, (back + 1) * size), back_high_ref, back_low_ref
        )
    flags_ref[0] = (most > 256.0).astype(jnp.int32)
    flags_ref[1] = me_ref[0]
    stores = start_all((low_ref, back_low_ref), (low_hbm, back_low_hbm), out_sems)
    for load in loads[4:8]:
        load.wait()
    variables, width = out_ref.shape
    padded = jnp.concatenate(
        [out_ref[...].astype(jnp.float32), jnp.zeros((LANES - variables, width), jnp.float32)], axis=0
    )
    pad_ref[...] = padded.astype(jnp.bfloat16)
    turned_ref[...] = padded.T.astype(jnp.bfloat16)
    target = jnp.concatenate(
        [target_ref[...], jnp.zeros((LANES - variables, target_ref.shape[1]), jnp.float32)], axis=0
    )
    target_turned_ref[...] = target.T
    area = jnp.broadcast_to(area_ref[...], (LANES, area_ref.shape[1])).T
    scales = jnp.concatenate([var_ref[...], jnp.zeros((1, LANES - variables), jnp.float32)], axis=1)
    weight_ref[...] = area * scales
    for load in loads[8:]:
        load.wait()
    node_turned_ref[...] = node_ref[...].T
    own = slice(size, 2 * size)
    base_ref[...] = dot(high_ref[:, own], latent_ref[...]) + grid_ref[...].astype(jnp.float32)

    @pl.when(flags_ref[0] > 0)
    def _():
        base_ref[...] += dot(low_ref[:, own], latent_ref[...])

    for store in stores:
        store.wait()


def start_all(sources, targets, sems):
    copies = [pltpu.make_async_copy(s, t, sems.at[i]) for i, (s, t) in enumerate(zip(sources, targets))]
    for copy in copies:
        copy.start()
    return copies


def dot(left, right):
    return jnp.dot(left, right, preferred_element_type=jnp.float32)


def forward_kernel(
    flags_ref, high_ref, base_ref, first_ref, second_ref, node_ref, turned_ref, target_ref, weight_ref, low_hbm,
    shared_ref, fold_ref, lead_ref, gate_ref, normed_ref, inverse_ref,
    low_ref, sum_ref, low_sem,
):
    size = first_ref.shape[0]

    def gather(counts_ref):
        return dot(counts_ref[:, :size], first_ref[...]) + dot(counts_ref[:, 2 * size :], second_ref[...])

    sum_ref[...] = gather(high_ref) + base_ref[...]

    @pl.when(flags_ref[0] > 0)
    def _():
        copy = pltpu.make_async_copy(low_hbm, low_ref, low_sem)
        copy.start()
        copy.wait()
        sum_ref[...] += gather(low_ref)

    summed = sum_ref[...]
    centered = summed - jnp.mean(summed, axis=-1, keepdims=True)
    inverse = lax.rsqrt(jnp.mean(centered * centered, axis=-1, keepdims=True) + EPS)
    normed = centered * inverse
    normed_ref[...] = normed
    inverse_ref[...] = inverse
    pre_act = dot(normed.astype(jnp.bfloat16), node_ref[...])
    gate_sig = 0.5 + 0.5 * jnp.tanh(0.5 * pre_act)
    gate_ref[...] = gate_sig * (1.0 + pre_act * (1.0 - gate_sig))
    hidden = (pre_act * gate_sig).astype(jnp.bfloat16)
    pred = dot(hidden, turned_ref[...])
    largest = jnp.max(jnp.abs(pred), axis=0, keepdims=True)
    code = jnp.ceil(jnp.log2(jnp.maximum(largest, 2.0**LOWEST)) * CODE)
    whole = jnp.round(pred * (jnp.exp2(code * (-1.0 / CODE)) * STEPS))
    packed = fold(whole, code).astype(jnp.int16)
    for member in range(shared_ref.shape[0]):
        shared_ref[member] = packed
    lead_ref[...] = weight_ref[...] * smooth_slope(pred - target_ref[...])
    fold_ref[...] = fold(pred)


def fold(values, code=None):
    rest = values[MAIN:, :]
    tail = jnp.zeros((MAIN - FOLDS * rest.shape[0], LANES), values.dtype)
    if code is not None:
        wide = jnp.broadcast_to(code, tail.shape)
        row = lax.broadcasted_iota(jnp.int32, tail.shape, 0)
        for k in range(FOLDS):
            tail = jnp.where(row == k, turn(wide, VARS - FOLD * k), tail)
    pieces = [turn(rest, VARS - FOLD * k) for k in range(FOLDS)] + [tail]
    spare = jnp.concatenate(pieces, axis=0)
    main = values[:MAIN, :]
    lane = lanes_of(main)
    return jnp.where(lane < VARS, main, jnp.where(lane < VARS + FOLD, spare, jnp.zeros_like(main)))


def unfold(values, rows):
    rest_rows = rows - MAIN
    lane = lax.broadcasted_iota(jnp.int32, (rest_rows, LANES), 1)
    rest = jnp.zeros((rest_rows, LANES), values.dtype)
    for k in range(FOLDS):
        piece = turn(values[k * rest_rows : (k + 1) * rest_rows, :], FOLD * k - VARS)
        rest = jnp.where((lane >= FOLD * k) & (lane < FOLD * (k + 1)), piece, rest)
    return jnp.concatenate([values, rest], axis=0)


def backward_kernel(
    flags_ref, everyone_ref, fold_ref, lead_ref, weight_ref, gate_ref,
    pad_ref, turned_ref, normed_ref, inverse_ref, high_ref, low_hbm,
    blocks_ref, first_ref, second_ref, send_ref,
    low_ref, scale_ref, low_sem, *, pair_scale
):
    members = everyone_ref.shape[0]
    grid_rows, width = normed_ref.shape
    rest_rows = grid_rows - MAIN
    me = flags_ref[1]
    first = FOLDS * rest_rows
    lane = lax.broadcasted_iota(jnp.int32, (members, LANES), 1)
    tails = everyone_ref[:, first:MAIN, :].astype(jnp.float32)
    code = jnp.zeros((members, LANES), jnp.float32)
    for k in range(FOLDS):
        piece = turn(tails[:, k, :], FOLD * k - VARS)
        code = jnp.where((lane >= FOLD * k) & (lane < FOLD * (k + 1)), piece, code)
    scale = jnp.exp2(code * (1.0 / CODE)) * (1.0 / STEPS)
    for k in range(FOLDS):
        scale_ref[k] = jnp.where(lane < VARS, scale, turn(scale, VARS - FOLD * k))

    bounds = [(k * rest_rows, (k + 1) * rest_rows) for k in range(FOLDS)] + [(first, MAIN)]
    parts = [jnp.zeros((high - low, LANES), jnp.float32) for low, high in bounds]
    for step in range(1, members):
        other = lax.rem(me + step, members)
        for i, (low, high) in enumerate(bounds):
            factor = scale_ref[min(i, FOLDS - 1), pl.ds(other, 1), :]
            theirs = everyone_ref[other, low:high, :].astype(jnp.float32) * factor
            parts[i] = parts[i] + smooth_slope(fold_ref[low:high, :] - theirs)
    pair_sum = unfold(jnp.concatenate(parts, axis=0), grid_rows)
    real = lanes_of(pair_sum) < VARS
    grad_pred = lead_ref[...] - pair_scale * weight_ref[...] * jnp.where(real, pair_sum, 0.0)
    grad_hidden = dot(grad_pred.astype(jnp.bfloat16), pad_ref[...])
    grad_pre = (grad_hidden * gate_ref[...]).astype(jnp.bfloat16)
    grad_normed = dot(grad_pre, turned_ref[...])
    normed = normed_ref[...]
    grad_summed = inverse_ref[...] * (
        grad_normed
        - jnp.mean(grad_normed, axis=-1, keepdims=True)
        - normed * jnp.mean(grad_normed * normed, axis=-1, keepdims=True)
    )
    send_ref[...] = grad_summed.astype(jnp.bfloat16)
    half = grid_rows // 2
    lower = lax.broadcasted_iota(jnp.int32, (half, LANES), 1) < LANES // 2
    for pair in range(width // LANES):
        at = slice(pair * LANES, (pair + 1) * LANES)
        top = grad_summed[:half, at]
        bottom = grad_summed[half:, at]
        blocks_ref[2 * pair] = jnp.where(lower, top, turn(bottom, LANES // 2)).astype(jnp.bfloat16)
        blocks_ref[2 * pair + 1] = jnp.where(lower, turn(top, LANES // 2), bottom).astype(jnp.bfloat16)
    places = ((first_ref, slice(0, grid_rows)), (second_ref, slice(2 * grid_rows, 3 * grid_rows)))
    for ref, at in places:
        ref[...] = dot(high_ref[:, at], send_ref[...]).astype(jnp.bfloat16)

    @pl.when(flags_ref[0] > 0)
    def _():
        copy = pltpu.make_async_copy(low_hbm, low_ref, low_sem)
        copy.start()
        copy.wait()
        for ref, at in places:
            total = dot(high_ref[:, at], send_ref[...]) + dot(low_ref[:, at], send_ref[...])
            ref[...] = total.astype(jnp.bfloat16)


def tail_kernel(
    flags_ref, high_ref, send_ref, first_ref, second_ref, landed_ref, low_hbm, out_hbm, share_ref,
    low_ref, sum_ref, out_ref, low_sem, out_sems
):
    rows = send_ref.shape[0]
    own = slice(rows, 2 * rows)
    sum_ref[...] = dot(high_ref[:, own], send_ref[...])

    @pl.when(flags_ref[0] > 0)
    def _():
        copy = pltpu.make_async_copy(low_hbm, low_ref, low_sem)
        copy.start()
        copy.wait()
        sum_ref[...] += dot(low_ref[:, own], send_ref[...])

    parts = out_sems.shape[0]
    stores = []
    for part in range(parts):
        at = slice(part * rows // parts, (part + 1) * rows // parts)
        total = sum_ref[at, :] + first_ref[at, :].astype(jnp.float32) + second_ref[at, :].astype(jnp.float32)
        out_ref[at, :] = total.astype(jnp.bfloat16)
        stores.append(pltpu.make_async_copy(out_ref.at[at, :], out_hbm.at[at, :], out_sems.at[part]))
        stores[-1].start()
    total = landed_ref[0].astype(jnp.float32)
    for member in range(1, landed_ref.shape[0]):
        total = total + landed_ref[member].astype(jnp.float32)
    half = total.shape[0]
    share = share_ref.shape[0]
    flipped = total.T
    share_ref[:, :half] = flipped[:share, :].astype(jnp.bfloat16)
    share_ref[:, half:] = flipped[share:, :].astype(jnp.bfloat16)
    for store in stores:
        store.wait()


def shape(dims, dtype):
    return jax.ShapeDtypeStruct(dims, dtype)


SMEM = pl.BlockSpec(memory_space=pltpu.SMEM)
VMEM = pl.BlockSpec(memory_space=pltpu.VMEM)
HBM = pl.BlockSpec(memory_space=pltpu.HBM)


def in_hbm(*values):
    return [pltpu.with_memory_space_constraint(v, pltpu.HBM) for v in values]


def cost_of(mega_flops, mega_bytes):
    return pl.CostEstimate(
        flops=mega_flops << 20, bytes_accessed=mega_bytes << 20, transcendentals=0
    )


PARAMS = pltpu.CompilerParams(vmem_limit_bytes=VMEM_LIMIT)


def held(value):
    return pltpu.VMEM(value.shape, value.dtype)


def per_device(
    mesh_latent, grid_latent, node_weight, out_weight, target, area_weight, var_weight, edge_src, edge_dst, edge_count
):
    f32, b16, i32 = jnp.float32, jnp.bfloat16, jnp.int32
    members = lax.axis_size("member")
    me = lax.axis_index("member").astype(i32)[None]
    latent = mesh_latent[0]
    mesh_rows = latent.shape[0]
    grid_rows, width = grid_latent.shape
    variables = out_weight.shape[0]
    dma = pltpu.SemaphoreType.DMA

    first = to_neighbours(latent, 0)
    second = to_neighbours(latent, 1)
    outs = [
        pltpu.SMEM((2,), i32),
        pltpu.HBM((grid_rows, 3 * mesh_rows), b16),
        pltpu.HBM((mesh_rows, 3 * grid_rows), b16),
        pltpu.VMEM((grid_rows, 3 * mesh_rows), b16),
        pltpu.VMEM((mesh_rows, 3 * grid_rows), b16),
        pltpu.VMEM((grid_rows, width), f32),
        pltpu.VMEM((width, width), b16),
        pltpu.VMEM((width, width), b16),
        pltpu.VMEM((LANES, width), b16),
        pltpu.VMEM((width, LANES), b16),
        pltpu.VMEM((grid_rows, LANES), f32),
        pltpu.VMEM((grid_rows, LANES), f32),
    ]
    ins = [
        me,
        edge_count,
        edge_src.reshape(1, -1),
        edge_dst.reshape(1, -1),
        area_weight[None, :],
        var_weight[None, :],
        out_weight,
        target,
        node_weight,
        latent,
        grid_latent,
    ]
    smem = pltpu.SMEM
    (
        flags, low, back_low, high, back_high, base, node, node_turned, out_pad, out_turned, target_turned, weight
    ) = pl.pallas_call(
        edges_kernel,
        out_shape=outs,
        in_specs=[HBM] * len(ins),
        out_specs=[SMEM] + [HBM] * 2 + [VMEM] * 9,
        scratch_shapes=[smem((1,), i32), smem(edge_count.shape, i32)]
        + [held(v) for v in (*ins[2:8], *ins[9:], *outs[1:3])]
        + [dma((len(ins),)), dma((2,))],
        compiler_params=PARAMS,
        cost_estimate=cost_of(500, 8),
    )(*in_hbm(*ins))
    flags = pltpu.with_memory_space_constraint(flags, pltpu.SMEM)

    outs = [
        pltpu.VMEM((members, MAIN, LANES), jnp.int16),
        pltpu.VMEM((MAIN, LANES), f32),
        pltpu.VMEM((grid_rows, LANES), f32),
        pltpu.VMEM((grid_rows, width), f32),
        pltpu.VMEM((grid_rows, width), f32),
        pltpu.VMEM((grid_rows, 1), f32),
    ]
    shared, folded, lead, gate, normed, inverse = pl.pallas_call(
        forward_kernel,
        out_shape=outs,
        in_specs=[SMEM] + [VMEM] * 8 + [HBM],
        out_specs=[VMEM] * len(outs),
        scratch_shapes=[held(low), pltpu.VMEM((grid_rows, width), f32), dma],
        compiler_params=PARAMS,
        cost_estimate=cost_of(1000, 8),
    )(flags, high, base, first, second, node, out_turned, target_turned, weight, *in_hbm(low))
    everyone = lax.all_to_all(shared, "member", 0, 0, tiled=True)

    pair_scale = (1.0 - (1.0 - ALPHA) / members) / (members - 1)
    outs = [
        pltpu.VMEM((members, grid_rows // 2, LANES), b16),
        pltpu.VMEM((mesh_rows, width), b16),
        pltpu.VMEM((mesh_rows, width), b16),
        pltpu.VMEM((grid_rows, width), b16),
    ]
    blocks, first_part, second_part, grad_send = pl.pallas_call(
        functools.partial(backward_kernel, pair_scale=pair_scale),
        out_shape=outs,
        in_specs=[SMEM] + [VMEM] * 10 + [HBM],
        out_specs=[VMEM] * 4,
        scratch_shapes=[held(back_low), pltpu.VMEM((FOLDS, members, LANES), f32), dma],
        compiler_params=PARAMS,
        cost_estimate=cost_of(1000, 8),
    )(
        flags, everyone, folded, lead, weight, gate, out_pad, node_turned, normed, inverse, back_high,
        *in_hbm(back_low),
    )
    landed = lax.all_to_all(blocks, "member", 0, 0, tiled=True)
    first_back = to_neighbours(first_part, 0)
    second_back = to_neighbours(second_part, 1)
    grad_latent, grid_share = pl.pallas_call(
        tail_kernel,
        out_shape=[pltpu.HBM((mesh_rows, width), b16), shape((width // members, grid_rows), b16)],
        in_specs=[SMEM] + [VMEM] * 5 + [HBM],
        out_specs=[HBM, VMEM],
        scratch_shapes=[
            held(back_low),
            pltpu.VMEM((mesh_rows, width), f32),
            pltpu.VMEM((mesh_rows, width), b16),
            dma,
            dma((4,)),
        ],
        compiler_params=PARAMS,
        cost_estimate=cost_of(130, 3),
    )(flags, back_high, grad_send, first_back, second_back, landed, *in_hbm(back_low))
    return (grad_latent[None], grid_share.T)


def solution(mesh):
    return jax.shard_map(
        per_device,
        mesh=mesh,
        in_specs=(
            P("member", "grid", None),
            P("grid", None),
            P(),
            P(),
            P(None, "grid"),
            P("grid"),
            P(),
            P("grid", None, None),
            P("grid", None, None),
            P("grid", None),
        ),
        out_specs=(P("member", "grid", None), P("grid", "member")),
        check_vma=False,
    )
```

```python
import functools

import jax
import jax.numpy as jnp
from jax import lax
from jax.experimental import pallas as pl
from jax.experimental.pallas import tpu as pltpu
from jax.sharding import PartitionSpec as P

SMOOTH = 0.1
ALPHA = 0.95
EPS = 1e-05
LANES = 128
VARS = 100
MAIN = 208
FOLD = 25
FOLDS = 4
STEPS = 32767.0
CODE = 256.0
LOWEST = -20.0
VMEM_LIMIT = 20 * 1024 * 1024


def to_neighbours(value, side):
    members, shards = lax.axis_size("member"), lax.axis_size("grid")
    pairs = [
        (member * shards + shard, member * shards + (shard + (1 if member % 2 == side else -1)) % shards)
        for member in range(members)
        for shard in range(shards)
    ]
    return lax.ppermute(value, ("member", "grid"), pairs)


def smooth_slope(difference):
    return difference * lax.rsqrt(difference * difference + SMOOTH * SMOOTH)


def turn(values, shift):
    shift = shift % LANES
    return pltpu.roll(values, shift, 1) if shift else values


def lanes_of(values):
    return lax.broadcasted_iota(jnp.int32, values.shape, 1)


def one_hot(picks, rows):
    places = lax.broadcasted_iota(jnp.int32, (rows, picks.shape[1]), 0)
    return jnp.where(places == picks, 1.0, 0.0).astype(jnp.bfloat16)


def count_pairs(row_hot, column_hot):
    return lax.dot_general(
        row_hot, column_hot, (((1,), (1,)), ((), ())), preferred_element_type=jnp.float32
    )


def store_counts(counts, at, high_ref, low_ref):
    high = counts.astype(jnp.bfloat16)
    high_ref[:, at] = high
    low_ref[:, at] = (counts - high.astype(jnp.float32)).astype(jnp.bfloat16)
    return jnp.max(counts)


def edges_kernel(
    me_hbm, count_hbm, src_hbm, dst_hbm, area_hbm, var_hbm, out_hbm, target_hbm, node_hbm, latent_hbm, grid_hbm,
    flags_ref, low_hbm, back_low_hbm,
    high_ref, back_high_ref, base_ref, node_ref, node_turned_ref, pad_ref, turned_ref, target_turned_ref, weight_ref,
    me_ref, count_ref, src_ref, dst_ref, area_ref, var_ref, out_ref, target_ref, latent_ref, grid_ref,
    low_ref, back_low_ref, in_sems, out_sems,
):
    loads = start_all(
        (me_hbm, count_hbm, src_hbm, dst_hbm, area_hbm, var_hbm, out_hbm, target_hbm, node_hbm, latent_hbm, grid_hbm),
        (me_ref, count_ref, src_ref, dst_ref, area_ref, var_ref, out_ref, target_ref, node_ref, latent_ref, grid_ref),
        in_sems,
    )
    size = high_ref.shape[0]
    slots = src_ref.shape[1] // 3
    slot = lax.broadcasted_iota(jnp.int32, (1, slots), 1)
    for load in loads[:4]:
        load.wait()
    odd = lax.rem(me_ref[0], 2)
    most = 0.0
    for place, offset in enumerate((2 - 2 * odd, 1, 2 * odd)):
        at = pl.ds(pl.multiple_of(offset * slots, LANES), slots)
        live = slot < count_ref[0, offset]
        targets = one_hot(jnp.where(live, dst_ref[:, at], -1), size)
        sources = one_hot(src_ref[:, at], size)
        counts = count_pairs(targets, sources)
        most = jnp.maximum(
            most, store_counts(counts, slice(place * size, (place + 1) * size), high_ref, low_ref)
        )
        back = 2 - place
        store_counts(
            count_pairs(sources, targets), slice(back * size, (back + 1) * size), back_high_ref, back_low_ref
        )
    flags_ref[0] = (most > 256.0).astype(jnp.int32)
    flags_ref[1] = me_ref[0]
    stores = start_all((low_ref, back_low_ref), (low_hbm, back_low_hbm), out_sems)
    for load in loads[4:8]:
        load.wait()
    variables, width = out_ref.shape
    padded = jnp.concatenate(
        [out_ref[...].astype(jnp.float32), jnp.zeros((LANES - variables, width), jnp.float32)], axis=0
    )
    pad_ref[...] = padded.astype(jnp.bfloat16)
    turned_ref[...] = padded.T.astype(jnp.bfloat16)
    target = jnp.concatenate(
        [target_ref[...], jnp.zeros((LANES - variables, target_ref.shape[1]), jnp.float32)], axis=0
    )
    target_turned_ref[...] = target.T
    area = jnp.broadcast_to(area_ref[...], (LANES, area_ref.shape[1])).T
    scales = jnp.concatenate([var_ref[...], jnp.zeros((1, LANES - variables), jnp.float32)], axis=1)
    weight_ref[...] = area * scales
    for load in loads[8:]:
        load.wait()
    node_turned_ref[...] = node_ref[...].T
    own = slice(size, 2 * size)
    base_ref[...] = dot(high_ref[:, own], latent_ref[...]) + grid_ref[...].astype(jnp.float32)

    @pl.when(flags_ref[0] > 0)
    def _():
        base_ref[...] += dot(low_ref[:, own], latent_ref[...])

    for store in stores:
        store.wait()


def start_all(sources, targets, sems):
    copies = [pltpu.make_async_copy(s, t, sems.at[i]) for i, (s, t) in enumerate(zip(sources, targets))]
    for copy in copies:
        copy.start()
    return copies


def dot(left, right):
    return jnp.dot(left, right, preferred_element_type=jnp.float32)


def forward_kernel(
    flags_ref, high_ref, base_ref, first_ref, second_ref, node_ref, turned_ref, target_ref, weight_ref, low_hbm,
    shared_ref, fold_ref, lead_ref, gate_ref, normed_ref, inverse_ref,
    low_ref, sum_ref, low_sem,
):
    size = first_ref.shape[0]

    def gather(counts_ref):
        return dot(counts_ref[:, :size], first_ref[...]) + dot(counts_ref[:, 2 * size :], second_ref[...])

    sum_ref[...] = gather(high_ref) + base_ref[...]

    @pl.when(flags_ref[0] > 0)
    def _():
        copy = pltpu.make_async_copy(low_hbm, low_ref, low_sem)
        copy.start()
        copy.wait()
        sum_ref[...] += gather(low_ref)

    summed = sum_ref[...]
    centered = summed - jnp.mean(summed, axis=-1, keepdims=True)
    inverse = lax.rsqrt(jnp.mean(centered * centered, axis=-1, keepdims=True) + EPS)
    normed = centered * inverse
    normed_ref[...] = normed
    inverse_ref[...] = inverse
    pre_act = dot(normed.astype(jnp.bfloat16), node_ref[...])
    gate_sig = 0.5 + 0.5 * jnp.tanh(0.5 * pre_act)
    gate_ref[...] = gate_sig * (1.0 + pre_act * (1.0 - gate_sig))
    hidden = (pre_act * gate_sig).astype(jnp.bfloat16)
    pred = dot(hidden, turned_ref[...])
    largest = jnp.max(jnp.abs(pred), axis=0, keepdims=True)
    code = jnp.ceil(jnp.log2(jnp.maximum(largest, 2.0**LOWEST)) * CODE)
    whole = jnp.round(pred * (jnp.exp2(code * (-1.0 / CODE)) * STEPS))
    packed = fold(whole, code).astype(jnp.int16)
    for member in range(shared_ref.shape[0]):
        shared_ref[member] = packed
    lead_ref[...] = weight_ref[...] * smooth_slope(pred - target_ref[...])
    fold_ref[...] = fold(pred)


def fold(values, code=None):
    rest = values[MAIN:, :]
    tail = jnp.zeros((MAIN - FOLDS * rest.shape[0], LANES), values.dtype)
    if code is not None:
        wide = jnp.broadcast_to(code, tail.shape)
        row = lax.broadcasted_iota(jnp.int32, tail.shape, 0)
        for k in range(FOLDS):
            tail = jnp.where(row == k, turn(wide, VARS - FOLD * k), tail)
    pieces = [turn(rest, VARS - FOLD * k) for k in range(FOLDS)] + [tail]
    spare = jnp.concatenate(pieces, axis=0)
    main = values[:MAIN, :]
    lane = lanes_of(main)
    return jnp.where(lane < VARS, main, jnp.where(lane < VARS + FOLD, spare, jnp.zeros_like(main)))


def unfold(values, rows):
    rest_rows = rows - MAIN
    lane = lax.broadcasted_iota(jnp.int32, (rest_rows, LANES), 1)
    rest = jnp.zeros((rest_rows, LANES), values.dtype)
    for k in range(FOLDS):
        piece = turn(values[k * rest_rows : (k + 1) * rest_rows, :], FOLD * k - VARS)
        rest = jnp.where((lane >= FOLD * k) & (lane < FOLD * (k + 1)), piece, rest)
    return jnp.concatenate([values, rest], axis=0)


def backward_kernel(
    flags_ref, everyone_ref, fold_ref, lead_ref, weight_ref, gate_ref,
    pad_ref, turned_ref, normed_ref, inverse_ref, high_ref, low_hbm,
    keep_ref, give_ref, first_ref, second_ref, send_ref,
    low_ref, scale_ref, low_sem, *, pair_scale
):
    members = everyone_ref.shape[0]
    grid_rows, width = normed_ref.shape
    rest_rows = grid_rows - MAIN
    me = flags_ref[1]
    first = FOLDS * rest_rows
    lane = lax.broadcasted_iota(jnp.int32, (members, LANES), 1)
    tails = everyone_ref[:, first:MAIN, :].astype(jnp.float32)
    code = jnp.zeros((members, LANES), jnp.float32)
    for k in range(FOLDS):
        piece = turn(tails[:, k, :], FOLD * k - VARS)
        code = jnp.where((lane >= FOLD * k) & (lane < FOLD * (k + 1)), piece, code)
    scale = jnp.exp2(code * (1.0 / CODE)) * (1.0 / STEPS)
    for k in range(FOLDS):
        scale_ref[k] = jnp.where(lane < VARS, scale, turn(scale, VARS - FOLD * k))

    bounds = [(k * rest_rows, (k + 1) * rest_rows) for k in range(FOLDS)] + [(first, MAIN)]
    parts = [jnp.zeros((high - low, LANES), jnp.float32) for low, high in bounds]
    for step in range(1, members):
        other = lax.rem(me + step, members)
        for i, (low, high) in enumerate(bounds):
            factor = scale_ref[min(i, FOLDS - 1), pl.ds(other, 1), :]
            theirs = everyone_ref[other, low:high, :].astype(jnp.float32) * factor
            parts[i] = parts[i] + smooth_slope(fold_ref[low:high, :] - theirs)
    pair_sum = unfold(jnp.concatenate(parts, axis=0), grid_rows)
    real = lanes_of(pair_sum) < VARS
    grad_pred = lead_ref[...] - pair_scale * weight_ref[...] * jnp.where(real, pair_sum, 0.0)
    grad_hidden = dot(grad_pred.astype(jnp.bfloat16), pad_ref[...])
    grad_pre = (grad_hidden * gate_ref[...]).astype(jnp.bfloat16)
    grad_normed = dot(grad_pre, turned_ref[...])
    normed = normed_ref[...]
    grad_summed = inverse_ref[...] * (
        grad_normed
        - jnp.mean(grad_normed, axis=-1, keepdims=True)
        - normed * jnp.mean(grad_normed * normed, axis=-1, keepdims=True)
    )
    send_ref[...] = grad_summed.astype(jnp.bfloat16)
    half = grid_rows // 2
    lower = lax.broadcasted_iota(jnp.int32, (half, LANES), 1) < LANES // 2
    odd = lax.rem(me, 2) == 1
    for pair in range(width // LANES):
        at = slice(pair * LANES, (pair + 1) * LANES)
        top = grad_summed[:half, at]
        bottom = grad_summed[half:, at]
        even_block = jnp.where(lower, top, turn(bottom, LANES // 2))
        odd_block = jnp.where(lower, turn(top, LANES // 2), bottom)
        keep_ref[pair] = jnp.where(odd, odd_block, even_block)
        give_ref[pair] = jnp.where(odd, even_block, odd_block).astype(jnp.bfloat16)
    places = ((first_ref, slice(0, grid_rows)), (second_ref, slice(2 * grid_rows, 3 * grid_rows)))
    for ref, at in places:
        ref[...] = dot(high_ref[:, at], send_ref[...]).astype(jnp.bfloat16)

    @pl.when(flags_ref[0] > 0)
    def _():
        copy = pltpu.make_async_copy(low_hbm, low_ref, low_sem)
        copy.start()
        copy.wait()
        for ref, at in places:
            total = dot(high_ref[:, at], send_ref[...]) + dot(low_ref[:, at], send_ref[...])
            ref[...] = total.astype(jnp.bfloat16)


def pair_add_kernel(keep_ref, got_ref, out_ref):
    out_ref[...] = (keep_ref[...] + got_ref[...].astype(jnp.float32)).astype(jnp.bfloat16)


def tail_kernel(
    flags_ref, high_ref, send_ref, first_ref, second_ref, landed_ref, low_hbm, out_hbm, share_ref,
    low_ref, sum_ref, out_ref, low_sem, out_sems
):
    rows = send_ref.shape[0]
    own = slice(rows, 2 * rows)
    sum_ref[...] = dot(high_ref[:, own], send_ref[...])

    @pl.when(flags_ref[0] > 0)
    def _():
        copy = pltpu.make_async_copy(low_hbm, low_ref, low_sem)
        copy.start()
        copy.wait()
        sum_ref[...] += dot(low_ref[:, own], send_ref[...])

    parts = out_sems.shape[0]
    stores = []
    for part in range(parts):
        at = slice(part * rows // parts, (part + 1) * rows // parts)
        total = sum_ref[at, :] + first_ref[at, :].astype(jnp.float32) + second_ref[at, :].astype(jnp.float32)
        out_ref[at, :] = total.astype(jnp.bfloat16)
        stores.append(pltpu.make_async_copy(out_ref.at[at, :], out_hbm.at[at, :], out_sems.at[part]))
        stores[-1].start()
    total = landed_ref[0].astype(jnp.float32)
    for member in range(1, landed_ref.shape[0]):
        total = total + landed_ref[member].astype(jnp.float32)
    half = total.shape[0]
    share = share_ref.shape[0]
    flipped = total.T
    share_ref[:, :half] = flipped[:share, :].astype(jnp.bfloat16)
    share_ref[:, half:] = flipped[share:, :].astype(jnp.bfloat16)
    for store in stores:
        store.wait()


def shape(dims, dtype):
    return jax.ShapeDtypeStruct(dims, dtype)


SMEM = pl.BlockSpec(memory_space=pltpu.SMEM)
VMEM = pl.BlockSpec(memory_space=pltpu.VMEM)
HBM = pl.BlockSpec(memory_space=pltpu.HBM)


def in_hbm(*values):
    return [pltpu.with_memory_space_constraint(v, pltpu.HBM) for v in values]


def cost_of(mega_flops, mega_bytes):
    return pl.CostEstimate(
        flops=mega_flops << 20, bytes_accessed=mega_bytes << 20, transcendentals=0
    )


PARAMS = pltpu.CompilerParams(vmem_limit_bytes=VMEM_LIMIT)


def held(value):
    return pltpu.VMEM(value.shape, value.dtype)


def per_device(
    mesh_latent, grid_latent, node_weight, out_weight, target, area_weight, var_weight, edge_src, edge_dst, edge_count
):
    f32, b16, i32 = jnp.float32, jnp.bfloat16, jnp.int32
    members = lax.axis_size("member")
    me = lax.axis_index("member").astype(i32)[None]
    latent = mesh_latent[0]
    mesh_rows = latent.shape[0]
    grid_rows, width = grid_latent.shape
    variables = out_weight.shape[0]
    dma = pltpu.SemaphoreType.DMA

    first = to_neighbours(latent, 0)
    second = to_neighbours(latent, 1)
    outs = [
        pltpu.SMEM((2,), i32),
        pltpu.HBM((grid_rows, 3 * mesh_rows), b16),
        pltpu.HBM((mesh_rows, 3 * grid_rows), b16),
        pltpu.VMEM((grid_rows, 3 * mesh_rows), b16),
        pltpu.VMEM((mesh_rows, 3 * grid_rows), b16),
        pltpu.VMEM((grid_rows, width), f32),
        pltpu.VMEM((width, width), b16),
        pltpu.VMEM((width, width), b16),
        pltpu.VMEM((LANES, width), b16),
        pltpu.VMEM((width, LANES), b16),
        pltpu.VMEM((grid_rows, LANES), f32),
        pltpu.VMEM((grid_rows, LANES), f32),
    ]
    ins = [
        me,
        edge_count,
        edge_src.reshape(1, -1),
        edge_dst.reshape(1, -1),
        area_weight[None, :],
        var_weight[None, :],
        out_weight,
        target,
        node_weight,
        latent,
        grid_latent,
    ]
    smem = pltpu.SMEM
    (
        flags, low, back_low, high, back_high, base, node, node_turned, out_pad, out_turned, target_turned, weight
    ) = pl.pallas_call(
        edges_kernel,
        out_shape=outs,
        in_specs=[HBM] * len(ins),
        out_specs=[SMEM] + [HBM] * 2 + [VMEM] * 9,
        scratch_shapes=[smem((1,), i32), smem(edge_count.shape, i32)]
        + [held(v) for v in (*ins[2:8], *ins[9:], *outs[1:3])]
        + [dma((len(ins),)), dma((2,))],
        compiler_params=PARAMS,
        cost_estimate=cost_of(500, 8),
    )(*in_hbm(*ins))
    flags = pltpu.with_memory_space_constraint(flags, pltpu.SMEM)

    outs = [
        pltpu.VMEM((members, MAIN, LANES), jnp.int16),
        pltpu.VMEM((MAIN, LANES), f32),
        pltpu.VMEM((grid_rows, LANES), f32),
        pltpu.VMEM((grid_rows, width), f32),
        pltpu.VMEM((grid_rows, width), f32),
        pltpu.VMEM((grid_rows, 1), f32),
    ]
    shared, folded, lead, gate, normed, inverse = pl.pallas_call(
        forward_kernel,
        out_shape=outs,
        in_specs=[SMEM] + [VMEM] * 8 + [HBM],
        out_specs=[VMEM] * len(outs),
        scratch_shapes=[held(low), pltpu.VMEM((grid_rows, width), f32), dma],
        compiler_params=PARAMS,
        cost_estimate=cost_of(1000, 8),
    )(flags, high, base, first, second, node, out_turned, target_turned, weight, *in_hbm(low))
    everyone = lax.all_to_all(shared, "member", 0, 0, tiled=True)

    pair_scale = (1.0 - (1.0 - ALPHA) / members) / (members - 1)
    outs = [
        pltpu.VMEM((members // 2, grid_rows // 2, LANES), f32),
        pltpu.VMEM((members // 2, grid_rows // 2, LANES), b16),
        pltpu.VMEM((mesh_rows, width), b16),
        pltpu.VMEM((mesh_rows, width), b16),
        pltpu.VMEM((grid_rows, width), b16),
    ]
    keep, give, first_part, second_part, grad_send = pl.pallas_call(
        functools.partial(backward_kernel, pair_scale=pair_scale),
        out_shape=outs,
        in_specs=[SMEM] + [VMEM] * 10 + [HBM],
        out_specs=[VMEM] * 5,
        scratch_shapes=[held(back_low), pltpu.VMEM((FOLDS, members, LANES), f32), dma],
        compiler_params=PARAMS,
        cost_estimate=cost_of(1000, 8),
    )(
        flags, everyone, folded, lead, weight, gate, out_pad, node_turned, normed, inverse, back_high,
        *in_hbm(back_low),
    )
    got = lax.ppermute(give, "member", [(member, member ^ 1) for member in range(members)])
    first_back = to_neighbours(first_part, 0)
    second_back = to_neighbours(second_part, 1)
    (blocks,) = pl.pallas_call(
        pair_add_kernel,
        out_shape=[pltpu.VMEM(give.shape, b16)],
        in_specs=[VMEM] * 2,
        out_specs=[VMEM],
        compiler_params=PARAMS,
        cost_estimate=cost_of(1, 1),
    )(keep, got)
    cores = [[core + 2 * chip for chip in range(members // 2)] for core in range(2)]
    landed = lax.all_to_all(blocks, "member", 0, 0, axis_index_groups=cores, tiled=True)
    grad_latent, grid_share = pl.pallas_call(
        tail_kernel,
        out_shape=[pltpu.HBM((mesh_rows, width), b16), shape((width // members, grid_rows), b16)],
        in_specs=[SMEM] + [VMEM] * 5 + [HBM],
        out_specs=[HBM, VMEM],
        scratch_shapes=[
            held(back_low),
            pltpu.VMEM((mesh_rows, width), f32),
            pltpu.VMEM((mesh_rows, width), b16),
            dma,
            dma((4,)),
        ],
        compiler_params=PARAMS,
        cost_estimate=cost_of(130, 3),
    )(flags, back_high, grad_send, first_back, second_back, landed, *in_hbm(back_low))
    return (grad_latent[None], grid_share.T)


def solution(mesh):
    return jax.shard_map(
        per_device,
        mesh=mesh,
        in_specs=(
            P("member", "grid", None),
            P("grid", None),
            P(),
            P(),
            P(None, "grid"),
            P("grid"),
            P(),
            P("grid", None, None),
            P("grid", None, None),
            P("grid", None),
        ),
        out_specs=(P("member", "grid", None), P("grid", "member")),
        check_vma=False,
    )
```

```python
import functools

import jax
import jax.numpy as jnp
from jax import lax
from jax.experimental import pallas as pl
from jax.experimental.pallas import tpu as pltpu
from jax.sharding import PartitionSpec as P

SMOOTH = 0.1
ALPHA = 0.95
EPS = 1e-05
LANES = 128
VARS = 100
MAIN = 208
FOLD = 25
FOLDS = 4
STEPS = 32767.0
CODE = 256.0
LOWEST = -20.0
VMEM_LIMIT = 20 * 1024 * 1024


def to_neighbours(value, side):
    members, shards = lax.axis_size("member"), lax.axis_size("grid")
    pairs = [
        (member * shards + shard, member * shards + (shard + (1 if member % 2 == side else -1)) % shards)
        for member in range(members)
        for shard in range(shards)
    ]
    return lax.ppermute(value, ("member", "grid"), pairs)


def smooth_slope(difference):
    return difference * lax.rsqrt(difference * difference + SMOOTH * SMOOTH)


def turn(values, shift):
    shift = shift % LANES
    return pltpu.roll(values, shift, 1) if shift else values


def lanes_of(values):
    return lax.broadcasted_iota(jnp.int32, values.shape, 1)


def one_hot(picks, rows):
    places = lax.broadcasted_iota(jnp.int32, (rows, picks.shape[1]), 0)
    return jnp.where(places == picks, 1.0, 0.0).astype(jnp.bfloat16)


def count_pairs(row_hot, column_hot):
    return lax.dot_general(
        row_hot, column_hot, (((1,), (1,)), ((), ())), preferred_element_type=jnp.float32
    )


def store_counts(counts, at, high_ref, low_ref):
    high = counts.astype(jnp.bfloat16)
    high_ref[:, at] = high
    low_ref[:, at] = (counts - high.astype(jnp.float32)).astype(jnp.bfloat16)
    return jnp.max(counts)


def edges_kernel(
    me_hbm, count_hbm, src_hbm, dst_hbm, area_hbm, var_hbm, out_hbm, target_hbm, node_hbm, latent_hbm, grid_hbm,
    flags_ref, low_hbm, back_low_hbm,
    high_ref, back_high_ref, base_ref, node_ref, node_turned_ref, pad_ref, turned_ref, target_turned_ref, weight_ref,
    me_ref, count_ref, src_ref, dst_ref, area_ref, var_ref, out_ref, target_ref, latent_ref, grid_ref,
    low_ref, back_low_ref, in_sems, out_sems,
):
    loads = start_all(
        (me_hbm, count_hbm, src_hbm, dst_hbm, area_hbm, var_hbm, out_hbm, target_hbm, node_hbm, latent_hbm, grid_hbm),
        (me_ref, count_ref, src_ref, dst_ref, area_ref, var_ref, out_ref, target_ref, node_ref, latent_ref, grid_ref),
        in_sems,
    )
    size = high_ref.shape[0]
    slots = src_ref.shape[1] // 3
    slot = lax.broadcasted_iota(jnp.int32, (1, slots), 1)
    for load in loads[:4]:
        load.wait()
    odd = lax.rem(me_ref[0], 2)
    most = 0.0
    for place, offset in enumerate((2 - 2 * odd, 1, 2 * odd)):
        at = pl.ds(pl.multiple_of(offset * slots, LANES), slots)
        live = slot < count_ref[0, offset]
        targets = one_hot(jnp.where(live, dst_ref[:, at], -1), size)
        sources = one_hot(src_ref[:, at], size)
        counts = count_pairs(targets, sources)
        most = jnp.maximum(
            most, store_counts(counts, slice(place * size, (place + 1) * size), high_ref, low_ref)
        )
        back = 2 - place
        store_counts(
            count_pairs(sources, targets), slice(back * size, (back + 1) * size), back_high_ref, back_low_ref
        )
    flags_ref[0] = (most > 256.0).astype(jnp.int32)
    flags_ref[1] = me_ref[0]
    stores = start_all((low_ref, back_low_ref), (low_hbm, back_low_hbm), out_sems)
    for load in loads[4:8]:
        load.wait()
    variables, width = out_ref.shape
    padded = jnp.concatenate(
        [out_ref[...].astype(jnp.float32), jnp.zeros((LANES - variables, width), jnp.float32)], axis=0
    )
    pad_ref[...] = padded.astype(jnp.bfloat16)
    turned_ref[...] = padded.T.astype(jnp.bfloat16)
    target = jnp.concatenate(
        [target_ref[...], jnp.zeros((LANES - variables, target_ref.shape[1]), jnp.float32)], axis=0
    )
    target_turned_ref[...] = target.T
    area = jnp.broadcast_to(area_ref[...], (LANES, area_ref.shape[1])).T
    scales = jnp.concatenate([var_ref[...], jnp.zeros((1, LANES - variables), jnp.float32)], axis=1)
    weight_ref[...] = area * scales
    for load in loads[8:]:
        load.wait()
    node_turned_ref[...] = node_ref[...].T
    own = slice(size, 2 * size)
    base_ref[...] = dot(high_ref[:, own], latent_ref[...]) + grid_ref[...].astype(jnp.float32)

    @pl.when(flags_ref[0] > 0)
    def _():
        base_ref[...] += dot(low_ref[:, own], latent_ref[...])

    for store in stores:
        store.wait()


def start_all(sources, targets, sems):
    copies = [pltpu.make_async_copy(s, t, sems.at[i]) for i, (s, t) in enumerate(zip(sources, targets))]
    for copy in copies:
        copy.start()
    return copies


def dot(left, right):
    return jnp.dot(left, right, preferred_element_type=jnp.float32)


def forward_kernel(
    flags_ref, high_ref, base_ref, first_ref, second_ref, node_ref, turned_ref, target_ref, weight_ref, low_hbm,
    shared_ref, fold_ref, lead_ref, gate_ref, normed_ref, inverse_ref,
    low_ref, sum_ref, low_sem,
):
    size = first_ref.shape[0]

    def gather(counts_ref):
        return dot(counts_ref[:, :size], first_ref[...]) + dot(counts_ref[:, 2 * size :], second_ref[...])

    sum_ref[...] = gather(high_ref) + base_ref[...]

    @pl.when(flags_ref[0] > 0)
    def _():
        copy = pltpu.make_async_copy(low_hbm, low_ref, low_sem)
        copy.start()
        copy.wait()
        sum_ref[...] += gather(low_ref)

    summed = sum_ref[...]
    centered = summed - jnp.mean(summed, axis=-1, keepdims=True)
    inverse = lax.rsqrt(jnp.mean(centered * centered, axis=-1, keepdims=True) + EPS)
    normed = centered * inverse
    normed_ref[...] = normed
    inverse_ref[...] = inverse
    pre_act = dot(normed.astype(jnp.bfloat16), node_ref[...])
    gate_sig = 0.5 + 0.5 * jnp.tanh(0.5 * pre_act)
    gate_ref[...] = gate_sig * (1.0 + pre_act * (1.0 - gate_sig))
    hidden = (pre_act * gate_sig).astype(jnp.bfloat16)
    pred = dot(hidden, turned_ref[...])
    largest = jnp.max(jnp.abs(pred), axis=0, keepdims=True)
    code = jnp.ceil(jnp.log2(jnp.maximum(largest, 2.0**LOWEST)) * CODE)
    whole = jnp.round(pred * (jnp.exp2(code * (-1.0 / CODE)) * STEPS))
    packed = fold(whole, code).astype(jnp.int16)
    for member in range(shared_ref.shape[0]):
        shared_ref[member] = packed
    lead_ref[...] = weight_ref[...] * smooth_slope(pred - target_ref[...])
    fold_ref[...] = fold(pred)


def fold(values, code=None):
    rest = values[MAIN:, :]
    tail = jnp.zeros((MAIN - FOLDS * rest.shape[0], LANES), values.dtype)
    if code is not None:
        wide = jnp.broadcast_to(code, tail.shape)
        row = lax.broadcasted_iota(jnp.int32, tail.shape, 0)
        for k in range(FOLDS):
            tail = jnp.where(row == k, turn(wide, VARS - FOLD * k), tail)
    pieces = [turn(rest, VARS - FOLD * k) for k in range(FOLDS)] + [tail]
    spare = jnp.concatenate(pieces, axis=0)
    main = values[:MAIN, :]
    lane = lanes_of(main)
    return jnp.where(lane < VARS, main, jnp.where(lane < VARS + FOLD, spare, jnp.zeros_like(main)))


def unfold(values, rows):
    rest_rows = rows - MAIN
    lane = lax.broadcasted_iota(jnp.int32, (rest_rows, LANES), 1)
    rest = jnp.zeros((rest_rows, LANES), values.dtype)
    for k in range(FOLDS):
        piece = turn(values[k * rest_rows : (k + 1) * rest_rows, :], FOLD * k - VARS)
        rest = jnp.where((lane >= FOLD * k) & (lane < FOLD * (k + 1)), piece, rest)
    return jnp.concatenate([values, rest], axis=0)


def backward_kernel(
    flags_ref, alike_ref, unlike_ref, fold_ref, lead_ref, weight_ref, gate_ref,
    pad_ref, turned_ref, normed_ref, inverse_ref, high_ref, low_hbm,
    keep_ref, give_ref, first_ref, second_ref, send_ref,
    low_ref, scale_ref, low_sem, *, pair_scale
):
    chips = alike_ref.shape[0]
    grid_rows, width = normed_ref.shape
    rest_rows = grid_rows - MAIN
    me = flags_ref[1]
    first = FOLDS * rest_rows
    lane = lax.broadcasted_iota(jnp.int32, (chips, LANES), 1)
    for core, ref in enumerate((alike_ref, unlike_ref)):
        tails = ref[:, first:MAIN, :].astype(jnp.float32)
        code = jnp.zeros((chips, LANES), jnp.float32)
        for k in range(FOLDS):
            piece = turn(tails[:, k, :], FOLD * k - VARS)
            code = jnp.where((lane >= FOLD * k) & (lane < FOLD * (k + 1)), piece, code)
        scale = jnp.exp2(code * (1.0 / CODE)) * (1.0 / STEPS)
        for k in range(FOLDS):
            scale_ref[core, k] = jnp.where(lane < VARS, scale, turn(scale, VARS - FOLD * k))

    bounds = [(k * rest_rows, (k + 1) * rest_rows) for k in range(FOLDS)] + [(first, MAIN)]
    parts = [jnp.zeros((high - low, LANES), jnp.float32) for low, high in bounds]
    others = [(0, alike_ref, lax.rem(me // 2 + step, chips)) for step in range(1, chips)]
    others += [(1, unlike_ref, chip) for chip in range(chips)]
    for core, ref, other in others:
        for i, (low, high) in enumerate(bounds):
            factor = scale_ref[core, min(i, FOLDS - 1), pl.ds(other, 1), :]
            theirs = ref[other, low:high, :].astype(jnp.float32) * factor
            parts[i] = parts[i] + smooth_slope(fold_ref[low:high, :] - theirs)
    pair_sum = unfold(jnp.concatenate(parts, axis=0), grid_rows)
    real = lanes_of(pair_sum) < VARS
    grad_pred = lead_ref[...] - pair_scale * weight_ref[...] * jnp.where(real, pair_sum, 0.0)
    grad_hidden = dot(grad_pred.astype(jnp.bfloat16), pad_ref[...])
    grad_pre = (grad_hidden * gate_ref[...]).astype(jnp.bfloat16)
    grad_normed = dot(grad_pre, turned_ref[...])
    normed = normed_ref[...]
    grad_summed = inverse_ref[...] * (
        grad_normed
        - jnp.mean(grad_normed, axis=-1, keepdims=True)
        - normed * jnp.mean(grad_normed * normed, axis=-1, keepdims=True)
    )
    send_ref[...] = grad_summed.astype(jnp.bfloat16)
    half = grid_rows // 2
    lower = lax.broadcasted_iota(jnp.int32, (half, LANES), 1) < LANES // 2
    odd = lax.rem(me, 2) == 1
    for pair in range(width // LANES):
        at = slice(pair * LANES, (pair + 1) * LANES)
        top = grad_summed[:half, at]
        bottom = grad_summed[half:, at]
        even_block = jnp.where(lower, top, turn(bottom, LANES // 2))
        odd_block = jnp.where(lower, turn(top, LANES // 2), bottom)
        keep_ref[pair] = jnp.where(odd, odd_block, even_block)
        give_ref[pair] = jnp.where(odd, even_block, odd_block).astype(jnp.bfloat16)
    places = ((first_ref, slice(0, grid_rows)), (second_ref, slice(2 * grid_rows, 3 * grid_rows)))
    for ref, at in places:
        ref[...] = dot(high_ref[:, at], send_ref[...]).astype(jnp.bfloat16)

    @pl.when(flags_ref[0] > 0)
    def _():
        copy = pltpu.make_async_copy(low_hbm, low_ref, low_sem)
        copy.start()
        copy.wait()
        for ref, at in places:
            total = dot(high_ref[:, at], send_ref[...]) + dot(low_ref[:, at], send_ref[...])
            ref[...] = total.astype(jnp.bfloat16)


def pair_add_kernel(keep_ref, got_ref, out_ref):
    out_ref[...] = (keep_ref[...] + got_ref[...].astype(jnp.float32)).astype(jnp.bfloat16)


def tail_kernel(
    flags_ref, high_ref, send_ref, first_ref, second_ref, landed_ref, low_hbm, out_hbm, share_ref,
    low_ref, sum_ref, out_ref, low_sem, out_sems
):
    rows = send_ref.shape[0]
    own = slice(rows, 2 * rows)
    sum_ref[...] = dot(high_ref[:, own], send_ref[...])

    @pl.when(flags_ref[0] > 0)
    def _():
        copy = pltpu.make_async_copy(low_hbm, low_ref, low_sem)
        copy.start()
        copy.wait()
        sum_ref[...] += dot(low_ref[:, own], send_ref[...])

    parts = out_sems.shape[0]
    stores = []
    for part in range(parts):
        at = slice(part * rows // parts, (part + 1) * rows // parts)
        total = sum_ref[at, :] + first_ref[at, :].astype(jnp.float32) + second_ref[at, :].astype(jnp.float32)
        out_ref[at, :] = total.astype(jnp.bfloat16)
        stores.append(pltpu.make_async_copy(out_ref.at[at, :], out_hbm.at[at, :], out_sems.at[part]))
        stores[-1].start()
    total = landed_ref[0].astype(jnp.float32)
    for member in range(1, landed_ref.shape[0]):
        total = total + landed_ref[member].astype(jnp.float32)
    half = total.shape[0]
    share = share_ref.shape[0]
    flipped = total.T
    share_ref[:, :half] = flipped[:share, :].astype(jnp.bfloat16)
    share_ref[:, half:] = flipped[share:, :].astype(jnp.bfloat16)
    for store in stores:
        store.wait()


def shape(dims, dtype):
    return jax.ShapeDtypeStruct(dims, dtype)


SMEM = pl.BlockSpec(memory_space=pltpu.SMEM)
VMEM = pl.BlockSpec(memory_space=pltpu.VMEM)
HBM = pl.BlockSpec(memory_space=pltpu.HBM)


def in_hbm(*values):
    return [pltpu.with_memory_space_constraint(v, pltpu.HBM) for v in values]


def cost_of(mega_flops, mega_bytes):
    return pl.CostEstimate(
        flops=mega_flops << 20, bytes_accessed=mega_bytes << 20, transcendentals=0
    )


PARAMS = pltpu.CompilerParams(vmem_limit_bytes=VMEM_LIMIT)


def held(value):
    return pltpu.VMEM(value.shape, value.dtype)


def per_device(
    mesh_latent, grid_latent, node_weight, out_weight, target, area_weight, var_weight, edge_src, edge_dst, edge_count
):
    f32, b16, i32 = jnp.float32, jnp.bfloat16, jnp.int32
    members = lax.axis_size("member")
    me = lax.axis_index("member").astype(i32)[None]
    latent = mesh_latent[0]
    mesh_rows = latent.shape[0]
    grid_rows, width = grid_latent.shape
    variables = out_weight.shape[0]
    dma = pltpu.SemaphoreType.DMA

    first = to_neighbours(latent, 0)
    second = to_neighbours(latent, 1)
    outs = [
        pltpu.SMEM((2,), i32),
        pltpu.HBM((grid_rows, 3 * mesh_rows), b16),
        pltpu.HBM((mesh_rows, 3 * grid_rows), b16),
        pltpu.VMEM((grid_rows, 3 * mesh_rows), b16),
        pltpu.VMEM((mesh_rows, 3 * grid_rows), b16),
        pltpu.VMEM((grid_rows, width), f32),
        pltpu.VMEM((width, width), b16),
        pltpu.VMEM((width, width), b16),
        pltpu.VMEM((LANES, width), b16),
        pltpu.VMEM((width, LANES), b16),
        pltpu.VMEM((grid_rows, LANES), f32),
        pltpu.VMEM((grid_rows, LANES), f32),
    ]
    ins = [
        me,
        edge_count,
        edge_src.reshape(1, -1),
        edge_dst.reshape(1, -1),
        area_weight[None, :],
        var_weight[None, :],
        out_weight,
        target,
        node_weight,
        latent,
        grid_latent,
    ]
    smem = pltpu.SMEM
    (
        flags, low, back_low, high, back_high, base, node, node_turned, out_pad, out_turned, target_turned, weight
    ) = pl.pallas_call(
        edges_kernel,
        out_shape=outs,
        in_specs=[HBM] * len(ins),
        out_specs=[SMEM] + [HBM] * 2 + [VMEM] * 9,
        scratch_shapes=[smem((1,), i32), smem(edge_count.shape, i32)]
        + [held(v) for v in (*ins[2:8], *ins[9:], *outs[1:3])]
        + [dma((len(ins),)), dma((2,))],
        compiler_params=PARAMS,
        cost_estimate=cost_of(500, 8),
    )(*in_hbm(*ins))
    flags = pltpu.with_memory_space_constraint(flags, pltpu.SMEM)

    outs = [
        pltpu.VMEM((members // 2, MAIN, LANES), jnp.int16),
        pltpu.VMEM((MAIN, LANES), f32),
        pltpu.VMEM((grid_rows, LANES), f32),
        pltpu.VMEM((grid_rows, width), f32),
        pltpu.VMEM((grid_rows, width), f32),
        pltpu.VMEM((grid_rows, 1), f32),
    ]
    shared, folded, lead, gate, normed, inverse = pl.pallas_call(
        forward_kernel,
        out_shape=outs,
        in_specs=[SMEM] + [VMEM] * 8 + [HBM],
        out_specs=[VMEM] * len(outs),
        scratch_shapes=[held(low), pltpu.VMEM((grid_rows, width), f32), dma],
        compiler_params=PARAMS,
        cost_estimate=cost_of(1000, 8),
    )(flags, high, base, first, second, node, out_turned, target_turned, weight, *in_hbm(low))
    cores = [[core + 2 * chip for chip in range(members // 2)] for core in range(2)]
    swap = [(member, member ^ 1) for member in range(members)]
    alike = lax.all_to_all(shared, "member", 0, 0, axis_index_groups=cores, tiled=True)
    unlike = lax.ppermute(alike, "member", swap)

    pair_scale = (1.0 - (1.0 - ALPHA) / members) / (members - 1)
    outs = [
        pltpu.VMEM((members // 2, grid_rows // 2, LANES), f32),
        pltpu.VMEM((members // 2, grid_rows // 2, LANES), b16),
        pltpu.VMEM((mesh_rows, width), b16),
        pltpu.VMEM((mesh_rows, width), b16),
        pltpu.VMEM((grid_rows, width), b16),
    ]
    keep, give, first_part, second_part, grad_send = pl.pallas_call(
        functools.partial(backward_kernel, pair_scale=pair_scale),
        out_shape=outs,
        in_specs=[SMEM] + [VMEM] * 11 + [HBM],
        out_specs=[VMEM] * 5,
        scratch_shapes=[held(back_low), pltpu.VMEM((2, FOLDS, members // 2, LANES), f32), dma],
        compiler_params=PARAMS,
        cost_estimate=cost_of(1000, 8),
    )(
        flags, alike, unlike, folded, lead, weight, gate, out_pad, node_turned, normed, inverse, back_high,
        *in_hbm(back_low),
    )
    got = lax.ppermute(give, "member", swap)
    first_back = to_neighbours(first_part, 0)
    second_back = to_neighbours(second_part, 1)
    (blocks,) = pl.pallas_call(
        pair_add_kernel,
        out_shape=[pltpu.VMEM(give.shape, b16)],
        in_specs=[VMEM] * 2,
        out_specs=[VMEM],
        compiler_params=PARAMS,
        cost_estimate=cost_of(1, 1),
    )(keep, got)
    landed = lax.all_to_all(blocks, "member", 0, 0, axis_index_groups=cores, tiled=True)
    grad_latent, grid_share = pl.pallas_call(
        tail_kernel,
        out_shape=[pltpu.HBM((mesh_rows, width), b16), shape((width // members, grid_rows), b16)],
        in_specs=[SMEM] + [VMEM] * 5 + [HBM],
        out_specs=[HBM, VMEM],
        scratch_shapes=[
            held(back_low),
            pltpu.VMEM((mesh_rows, width), f32),
            pltpu.VMEM((mesh_rows, width), b16),
            dma,
            dma((4,)),
        ],
        compiler_params=PARAMS,
        cost_estimate=cost_of(130, 3),
    )(flags, back_high, grad_send, first_back, second_back, landed, *in_hbm(back_low))
    return (grad_latent[None], grid_share.T)


def solution(mesh):
    return jax.shard_map(
        per_device,
        mesh=mesh,
        in_specs=(
            P("member", "grid", None),
            P("grid", None),
            P(),
            P(),
            P(None, "grid"),
            P("grid"),
            P(),
            P("grid", None, None),
            P("grid", None, None),
            P("grid", None),
        ),
        out_specs=(P("member", "grid", None), P("grid", "member")),
        check_vma=False,
    )
```

```python
import functools

import jax
import jax.numpy as jnp
from jax import lax
from jax.experimental import pallas as pl
from jax.experimental.pallas import tpu as pltpu
from jax.sharding import PartitionSpec as P

SMOOTH = 0.1
ALPHA = 0.95
EPS = 1e-05
LANES = 128
VARS = 100
MAIN = 208
TAIL = 16
FOLD = 25
FOLDS = 4
STEPS = 32767.0
CODE = 256.0
LOWEST = -20.0
BLOCK = 256
EARLY = 2
VMEM_LIMIT = 20 * 1024 * 1024


def to_neighbours(value, side):
    members, shards = lax.axis_size("member"), lax.axis_size("grid")
    pairs = [
        (member * shards + shard, member * shards + (shard + (1 if member % 2 == side else -1)) % shards)
        for member in range(members)
        for shard in range(shards)
    ]
    return lax.ppermute(value, ("member", "grid"), pairs)


def smooth_slope(difference):
    return difference * lax.rsqrt(difference * difference + SMOOTH * SMOOTH)


def turn(values, shift):
    shift = shift % LANES
    return pltpu.roll(values, shift, 1) if shift else values


def lanes_of(values):
    return lax.broadcasted_iota(jnp.int32, values.shape, 1)


def one_hot(picks, rows):
    places = lax.broadcasted_iota(jnp.int32, (rows, picks.shape[1]), 0)
    return jnp.where(places == picks, 1.0, 0.0).astype(jnp.bfloat16)


def count_pairs(row_hot, column_hot):
    return lax.dot_general(
        row_hot, column_hot, (((1,), (1,)), ((), ())), preferred_element_type=jnp.float32
    )


def parts_of(counts):
    high = counts.astype(jnp.bfloat16)
    return (counts - high.astype(jnp.float32)).astype(jnp.bfloat16), high


def edges_kernel(
    me_hbm, count_hbm, src_hbm, dst_hbm, area_hbm, var_hbm, out_hbm, target_hbm, node_hbm, latent_hbm, grid_hbm,
    flags_ref, low_hbm, back_low_hbm,
    high_ref, back_ref, back_own_ref, base_ref, node_ref, node_turned_ref, pad_ref, turned_ref, target_turned_ref, weight_ref,
    me_ref, count_ref, src_ref, dst_ref, area_ref, var_ref, out_ref, target_ref, latent_ref, grid_ref,
    low_ref, back_low_ref, in_sems, out_sems,
):
    loads = start_all(
        (me_hbm, count_hbm, src_hbm, dst_hbm, area_hbm, var_hbm, out_hbm, target_hbm, node_hbm, latent_hbm, grid_hbm),
        (me_ref, count_ref, src_ref, dst_ref, area_ref, var_ref, out_ref, target_ref, node_ref, latent_ref, grid_ref),
        in_sems,
    )
    size = high_ref.shape[0]
    slots = src_ref.shape[1] // 3
    slot = lax.broadcasted_iota(jnp.int32, (1, slots), 1)
    for load in loads[:4]:
        load.wait()
    odd = lax.rem(me_ref[0], 2)
    most = 0.0
    for place, offset in enumerate((2 - 2 * odd, 1, 2 * odd)):
        at = pl.ds(pl.multiple_of(offset * slots, LANES), slots)
        live = slot < count_ref[0, offset]
        targets = one_hot(jnp.where(live, dst_ref[:, at], -1), size)
        sources = one_hot(src_ref[:, at], size)
        counts = count_pairs(targets, sources)
        most = jnp.maximum(most, jnp.max(counts))
        columns = slice(place * size, (place + 1) * size)
        low_ref[:, columns], high_ref[:, columns] = parts_of(counts)
        back = 2 - place
        back_low_ref[:, back * size : (back + 1) * size], high = parts_of(count_pairs(sources, targets))
        if place == 1:
            back_own_ref[...] = high
        else:
            back_ref[:, (back // 2) * size : (back // 2 + 1) * size] = high
    flags_ref[0] = (most > 256.0).astype(jnp.int32)
    flags_ref[1] = me_ref[0]
    stores = start_all((low_ref, back_low_ref), (low_hbm, back_low_hbm), out_sems)
    for load in loads[4:8]:
        load.wait()
    variables, width = out_ref.shape
    padded = jnp.concatenate(
        [out_ref[...].astype(jnp.float32), jnp.zeros((LANES - variables, width), jnp.float32)], axis=0
    )
    pad_ref[...] = padded.astype(jnp.bfloat16)
    turned_ref[...] = padded.T.astype(jnp.bfloat16)
    target = jnp.concatenate(
        [target_ref[...], jnp.zeros((LANES - variables, target_ref.shape[1]), jnp.float32)], axis=0
    )
    target_turned_ref[...] = target.T
    area = jnp.broadcast_to(area_ref[...], (LANES, area_ref.shape[1])).T
    scales = jnp.concatenate([var_ref[...], jnp.zeros((1, LANES - variables), jnp.float32)], axis=1)
    weight_ref[...] = area * scales
    for load in loads[8:]:
        load.wait()
    node_turned_ref[...] = node_ref[...].T
    own = slice(size, 2 * size)
    base_ref[...] = dot(high_ref[:, own], latent_ref[...]) + grid_ref[...].astype(jnp.float32)

    @pl.when(flags_ref[0] > 0)
    def _():
        base_ref[...] += dot(low_ref[:, own], latent_ref[...])

    for store in stores:
        store.wait()


def start_all(sources, targets, sems):
    copies = [pltpu.make_async_copy(s, t, sems.at[i]) for i, (s, t) in enumerate(zip(sources, targets))]
    for copy in copies:
        copy.start()
    return copies


def blocks_of(width):
    return [slice(start, start + BLOCK) for start in range(0, width, BLOCK)]


def dot(left, right):
    return jnp.dot(left, right, preferred_element_type=jnp.float32)


def gather_kernel(flags_ref, high_ref, base_ref, rows_ref, low_hbm, out_ref, low_ref, low_sem, *, place):
    size = rows_ref.shape[0]
    at = slice(place * size, (place + 1) * size)
    out_ref[...] = base_ref[...] + dot(high_ref[:, at], rows_ref[...])

    @pl.when(flags_ref[0] > 0)
    def _():
        copy = pltpu.make_async_copy(low_hbm, low_ref, low_sem)
        copy.start()
        copy.wait()
        out_ref[...] += dot(low_ref[:, at], rows_ref[...])


def forward_kernel(
    flags_ref, high_ref, base_ref, rows_ref, node_ref, turned_ref, target_ref, weight_ref, low_hbm,
    shared_ref, fold_ref, lead_ref, gate_ref, normed_ref, inverse_ref,
    low_ref, sum_ref, low_sem, *, place
):
    gather_kernel(flags_ref, high_ref, base_ref, rows_ref, low_hbm, sum_ref, low_ref, low_sem, place=place)
    summed = sum_ref[...]
    centered = summed - jnp.mean(summed, axis=-1, keepdims=True)
    inverse = lax.rsqrt(jnp.mean(centered * centered, axis=-1, keepdims=True) + EPS)
    normed = centered * inverse
    normed_ref[...] = normed
    inverse_ref[...] = inverse
    pre_act = dot(normed.astype(jnp.bfloat16), node_ref[...])
    gate_sig = 0.5 + 0.5 * jnp.tanh(0.5 * pre_act)
    gate_ref[...] = gate_sig * (1.0 + pre_act * (1.0 - gate_sig))
    pred = dot((pre_act * gate_sig).astype(jnp.bfloat16), turned_ref[...])
    largest = jnp.max(jnp.abs(pred), axis=0, keepdims=True)
    code = jnp.ceil(jnp.log2(jnp.maximum(largest, 2.0**LOWEST)) * CODE)
    whole = jnp.round(pred * (jnp.exp2(code * (-1.0 / CODE)) * STEPS))
    packed = fold(whole, code).astype(jnp.int16)
    for member in range(shared_ref.shape[0]):
        shared_ref[member] = packed
    lead_ref[...] = weight_ref[...] * smooth_slope(pred - target_ref[...])
    fold_ref[...] = fold(pred)


def fold(values, code=None):
    rest = values[MAIN:, :]
    tail = jnp.zeros((MAIN - FOLDS * rest.shape[0], LANES), values.dtype)
    if code is not None:
        wide = jnp.broadcast_to(code, tail.shape)
        row = lax.broadcasted_iota(jnp.int32, tail.shape, 0)
        for k in range(FOLDS):
            tail = jnp.where(row == k, turn(wide, VARS - FOLD * k), tail)
    pieces = [turn(rest, VARS - FOLD * k) for k in range(FOLDS)] + [tail]
    spare = jnp.concatenate(pieces, axis=0)
    main = values[:MAIN, :]
    lane = lanes_of(main)
    return jnp.where(lane < VARS, main, jnp.where(lane < VARS + FOLD, spare, jnp.zeros_like(main)))


def unfold(values, rows):
    rest_rows = rows - MAIN
    lane = lax.broadcasted_iota(jnp.int32, (rest_rows, LANES), 1)
    rest = jnp.zeros((rest_rows, LANES), values.dtype)
    for k in range(FOLDS):
        piece = turn(values[k * rest_rows : (k + 1) * rest_rows, :], FOLD * k - VARS)
        rest = jnp.where((lane >= FOLD * k) & (lane < FOLD * (k + 1)), piece, rest)
    return jnp.concatenate([values, rest], axis=0)


def pair_parts(ref, others, fold_ref, scale_ref):
    chips = ref.shape[0]
    rest_rows = (MAIN - TAIL) // FOLDS
    first = FOLDS * rest_rows
    lane = lax.broadcasted_iota(jnp.int32, (chips, LANES), 1)
    tails = ref[:, first:MAIN, :].astype(jnp.float32)
    code = jnp.zeros((chips, LANES), jnp.float32)
    for k in range(FOLDS):
        piece = turn(tails[:, k, :], FOLD * k - VARS)
        code = jnp.where((lane >= FOLD * k) & (lane < FOLD * (k + 1)), piece, code)
    scale = jnp.exp2(code * (1.0 / CODE)) * (1.0 / STEPS)
    for k in range(FOLDS):
        scale_ref[k] = jnp.where(lane < VARS, scale, turn(scale, VARS - FOLD * k))

    bounds = [(k * rest_rows, (k + 1) * rest_rows) for k in range(FOLDS)] + [(first, MAIN)]
    parts = [jnp.zeros((high - low, LANES), jnp.float32) for low, high in bounds]
    for other in others:
        for i, (low, high) in enumerate(bounds):
            factor = scale_ref[min(i, FOLDS - 1), pl.ds(other, 1), :]
            theirs = ref[other, low:high, :].astype(jnp.float32) * factor
            parts[i] = parts[i] + smooth_slope(fold_ref[low:high, :] - theirs)
    return parts


def alike_kernel(flags_ref, alike_ref, fold_ref, out_ref, scale_ref):
    chips = alike_ref.shape[0]
    others = [lax.rem(flags_ref[1] // 2 + step, chips) for step in range(1, chips)]
    out_ref[...] = jnp.concatenate(pair_parts(alike_ref, others, fold_ref, scale_ref), axis=0)


def backward_kernel(
    flags_ref, alike_sum_ref, unlike_ref, fold_ref, lead_ref, weight_ref, gate_ref,
    pad_ref, turned_ref, normed_ref, inverse_ref, high_ref, low_hbm,
    keep_ref, give_ref, first_ref, second_ref, send_ref,
    low_ref, scale_ref, pre_ref, grad_ref, low_sem, *, pair_scale
):
    grid_rows, width = normed_ref.shape
    me = flags_ref[1]
    chips = unlike_ref.shape[0]
    parts = pair_parts(unlike_ref, list(range(chips)), fold_ref, scale_ref)
    pair_sum = unfold(jnp.concatenate(parts, axis=0) + alike_sum_ref[...], grid_rows)
    real = lanes_of(pair_sum) < VARS
    grad_pred = lead_ref[...] - pair_scale * weight_ref[...] * jnp.where(real, pair_sum, 0.0)
    grad_pred_b = grad_pred.astype(jnp.bfloat16)
    for at in blocks_of(width):
        pre_ref[:, at] = (dot(grad_pred_b, pad_ref[:, at]) * gate_ref[:, at]).astype(jnp.bfloat16)
    plain = jnp.zeros((grid_rows, LANES), jnp.float32)
    along = jnp.zeros((grid_rows, LANES), jnp.float32)
    for at in blocks_of(width):
        grad_normed = dot(pre_ref[...], turned_ref[:, at])
        grad_ref[:, at] = grad_normed
        product = grad_normed * normed_ref[:, at]
        for lane in range(0, BLOCK, LANES):
            plain = plain + grad_normed[:, lane : lane + LANES]
            along = along + product[:, lane : lane + LANES]
    plain = jnp.sum(plain, axis=-1, keepdims=True) * (1.0 / width)
    along = jnp.sum(along, axis=-1, keepdims=True) * (1.0 / width)
    inverse = inverse_ref[...]
    half = grid_rows // 2
    lower = lax.broadcasted_iota(jnp.int32, (half, LANES), 1) < LANES // 2
    odd = lax.rem(me, 2) == 1
    for pair in range(width // LANES):
        at = slice(pair * LANES, (pair + 1) * LANES)
        grad_summed = inverse * (grad_ref[:, at] - plain - normed_ref[:, at] * along)
        send_ref[:, at] = grad_summed.astype(jnp.bfloat16)
        top = grad_summed[:half, :]
        bottom = grad_summed[half:, :]
        even_block = jnp.where(lower, top, turn(bottom, LANES // 2))
        odd_block = jnp.where(lower, turn(top, LANES // 2), bottom)
        keep_ref[pair] = jnp.where(odd, odd_block, even_block)
        give_ref[pair] = jnp.where(odd, even_block, odd_block).astype(jnp.bfloat16)
    sides = ((first_ref, 0), (second_ref, 1))
    for ref, side in sides:
        for at in blocks_of(width):
            counts = high_ref[:, side * grid_rows : (side + 1) * grid_rows]
            ref[:, at] = dot(counts, send_ref[:, at]).astype(jnp.bfloat16)

    @pl.when(flags_ref[0] > 0)
    def _():
        copy = pltpu.make_async_copy(low_hbm, low_ref, low_sem)
        copy.start()
        copy.wait()
        for ref, side in sides:
            at = slice(side * grid_rows, (side + 1) * grid_rows)
            low_at = slice(2 * side * grid_rows, (2 * side + 1) * grid_rows)
            total = dot(high_ref[:, at], send_ref[...]) + dot(low_ref[:, low_at], send_ref[...])
            ref[...] = total.astype(jnp.bfloat16)


def pair_add_kernel(keep_ref, got_ref, out_ref):
    out_ref[...] = (keep_ref[...] + got_ref[...].astype(jnp.float32)).astype(jnp.bfloat16)


def tail_kernel(
    flags_ref, own_ref, send_ref, first_ref, second_ref, landed_ref, low_hbm, out_hbm, share_hbm,
    low_ref, sum_ref, out_ref, share_ref, low_sem, out_sems, share_sem
):
    rows = send_ref.shape[0]
    sum_ref[...] = dot(own_ref[...], send_ref[...])

    @pl.when(flags_ref[0] > 0)
    def _():
        copy = pltpu.make_async_copy(low_hbm, low_ref, low_sem)
        copy.start()
        copy.wait()
        sum_ref[...] += dot(low_ref[:, rows : 2 * rows], send_ref[...])

    parts = out_sems.shape[0]
    stores = []
    for part in range(parts):
        at = slice(part * rows // parts, (part + 1) * rows // parts)
        total = sum_ref[at, :] + first_ref[at, :].astype(jnp.float32) + second_ref[at, :].astype(jnp.float32)
        out_ref[at, :] = total.astype(jnp.bfloat16)
        stores.append(pltpu.make_async_copy(out_ref.at[at, :], out_hbm.at[at, :], out_sems.at[part]))
        stores[-1].start()
    total = landed_ref[0].astype(jnp.float32)
    for member in range(1, landed_ref.shape[0]):
        total = total + landed_ref[member].astype(jnp.float32)
    half = total.shape[0]
    share = share_ref.shape[0]
    flipped = total.T
    share_ref[:, :half] = flipped[:share, :].astype(jnp.bfloat16)
    share_ref[:, half:] = flipped[share:, :].astype(jnp.bfloat16)
    stores.append(pltpu.make_async_copy(share_ref, share_hbm, share_sem))
    stores[-1].start()
    for store in stores:
        store.wait()


def shape(dims, dtype):
    return jax.ShapeDtypeStruct(dims, dtype)


SMEM = pl.BlockSpec(memory_space=pltpu.SMEM)
VMEM = pl.BlockSpec(memory_space=pltpu.VMEM)
HBM = pl.BlockSpec(memory_space=pltpu.HBM)


def in_hbm(*values):
    return [pltpu.with_memory_space_constraint(v, pltpu.HBM) for v in values]


def cost_of(mega_flops, mega_bytes):
    return pl.CostEstimate(
        flops=mega_flops << 20, bytes_accessed=mega_bytes << 20, transcendentals=0
    )


PARAMS = pltpu.CompilerParams(vmem_limit_bytes=VMEM_LIMIT)


def held(value):
    return pltpu.VMEM(value.shape, value.dtype)


def per_device(
    mesh_latent, grid_latent, node_weight, out_weight, target, area_weight, var_weight, edge_src, edge_dst, edge_count
):
    f32, b16, i32 = jnp.float32, jnp.bfloat16, jnp.int32
    members = lax.axis_size("member")
    me = lax.axis_index("member").astype(i32)[None]
    latent = mesh_latent[0]
    mesh_rows = latent.shape[0]
    grid_rows, width = grid_latent.shape
    variables = out_weight.shape[0]
    dma = pltpu.SemaphoreType.DMA

    first = to_neighbours(latent, 0)
    second = to_neighbours(latent, 1)
    outs = [
        pltpu.SMEM((2,), i32),
        pltpu.HBM((grid_rows, 3 * mesh_rows), b16),
        pltpu.HBM((mesh_rows, 3 * grid_rows), b16),
        pltpu.VMEM((grid_rows, 3 * mesh_rows), b16),
        pltpu.VMEM((mesh_rows, 2 * grid_rows), b16),
        pltpu.VMEM((mesh_rows, grid_rows), b16),
        pltpu.VMEM((grid_rows, width), f32),
        pltpu.VMEM((width, width), b16),
        pltpu.VMEM((width, width), b16),
        pltpu.VMEM((LANES, width), b16),
        pltpu.VMEM((width, LANES), b16),
        pltpu.VMEM((grid_rows, LANES), f32),
        pltpu.VMEM((grid_rows, LANES), f32),
    ]
    ins = [
        me,
        edge_count,
        edge_src.reshape(1, -1),
        edge_dst.reshape(1, -1),
        area_weight[None, :],
        var_weight[None, :],
        out_weight,
        target,
        node_weight,
        latent,
        grid_latent,
    ]
    smem = pltpu.SMEM
    (
        flags, low, back_low, high, back, back_own, base, node, node_turned, out_pad, out_turned, target_turned, weight
    ) = pl.pallas_call(
        edges_kernel,
        out_shape=outs,
        in_specs=[HBM] * len(ins),
        out_specs=[SMEM] + [HBM] * 2 + [VMEM] * 10,
        scratch_shapes=[smem((1,), i32), smem(edge_count.shape, i32)]
        + [held(v) for v in (*ins[2:8], *ins[9:], *outs[1:3])]
        + [dma((len(ins),)), dma((2,))],
        compiler_params=PARAMS,
        cost_estimate=cost_of(500, 8),
    )(*in_hbm(*ins))
    flags = pltpu.with_memory_space_constraint(flags, pltpu.SMEM)

    some_cost = cost_of(1000, 8)
    (most_rows,) = pl.pallas_call(
        functools.partial(gather_kernel, place=EARLY),
        out_shape=[pltpu.VMEM((grid_rows, width), f32)],
        in_specs=[SMEM] + [VMEM] * 3 + [HBM],
        out_specs=[VMEM],
        scratch_shapes=[held(low), dma],
        compiler_params=PARAMS,
        cost_estimate=cost_of(130, 2),
    )(flags, high, base, (first, second)[EARLY // 2], *in_hbm(low))
    outs = [
        pltpu.VMEM((members // 2, MAIN, LANES), jnp.int16),
        pltpu.VMEM((MAIN, LANES), f32),
        pltpu.VMEM((grid_rows, LANES), f32),
        pltpu.VMEM((grid_rows, width), f32),
        pltpu.VMEM((grid_rows, width), f32),
        pltpu.VMEM((grid_rows, 1), f32),
    ]
    shared, folded, lead, gate, normed, inverse = pl.pallas_call(
        functools.partial(forward_kernel, place=2 - EARLY),
        out_shape=outs,
        in_specs=[SMEM] + [VMEM] * 7 + [HBM],
        out_specs=[VMEM] * len(outs),
        scratch_shapes=[held(low), pltpu.VMEM((grid_rows, width), f32), dma],
        compiler_params=PARAMS,
        cost_estimate=some_cost,
    )(
        flags, high, most_rows, (second, first)[EARLY // 2], node, out_turned, target_turned, weight, *in_hbm(low)
    )
    cores = [[core + 2 * chip for chip in range(members // 2)] for core in range(2)]
    swap = [(member, member ^ 1) for member in range(members)]
    alike = lax.all_to_all(shared, "member", 0, 0, axis_index_groups=cores, tiled=True)
    unlike = lax.ppermute(alike, "member", swap)
    (alike_sum,) = pl.pallas_call(
        alike_kernel,
        out_shape=[pltpu.VMEM((MAIN, LANES), f32)],
        in_specs=[SMEM] + [VMEM] * 2,
        out_specs=[VMEM],
        scratch_shapes=[pltpu.VMEM((FOLDS, members // 2, LANES), f32)],
        compiler_params=PARAMS,
        cost_estimate=cost_of(10, 1),
    )(flags, alike, folded)

    pair_scale = (1.0 - (1.0 - ALPHA) / members) / (members - 1)
    outs = [
        pltpu.VMEM((members // 2, grid_rows // 2, LANES), f32),
        pltpu.VMEM((members // 2, grid_rows // 2, LANES), b16),
        pltpu.VMEM((mesh_rows, width), b16),
        pltpu.VMEM((mesh_rows, width), b16),
        pltpu.VMEM((grid_rows, width), b16),
    ]
    keep, give, first_part, second_part, grad_send = pl.pallas_call(
        functools.partial(backward_kernel, pair_scale=pair_scale),
        out_shape=outs,
        in_specs=[SMEM] + [VMEM] * 11 + [HBM],
        out_specs=[VMEM] * 5,
        scratch_shapes=[
            held(back_low),
            pltpu.VMEM((FOLDS, members // 2, LANES), f32),
            pltpu.VMEM((grid_rows, width), b16),
            pltpu.VMEM((grid_rows, width), f32),
            dma,
        ],
        compiler_params=PARAMS,
        cost_estimate=cost_of(1000, 8),
    )(
        flags, alike_sum, unlike, folded, lead, weight, gate, out_pad, node_turned, normed, inverse, back,
        *in_hbm(back_low),
    )
    got = lax.ppermute(give, "member", swap)
    first_back = to_neighbours(first_part, 0)
    second_back = to_neighbours(second_part, 1)
    (blocks,) = pl.pallas_call(
        pair_add_kernel,
        out_shape=[pltpu.VMEM(give.shape, b16)],
        in_specs=[VMEM] * 2,
        out_specs=[VMEM],
        compiler_params=PARAMS,
        cost_estimate=cost_of(1, 1),
    )(keep, got)
    landed = lax.all_to_all(blocks, "member", 0, 0, axis_index_groups=cores, tiled=True)
    share = shape((width // members, grid_rows), b16)
    grad_latent, grid_share = pl.pallas_call(
        tail_kernel,
        out_shape=[pltpu.HBM((mesh_rows, width), b16), pltpu.HBM(share.shape, b16)],
        in_specs=[SMEM] + [VMEM] * 5 + [HBM],
        out_specs=[HBM, HBM],
        scratch_shapes=[
            held(back_low),
            pltpu.VMEM((mesh_rows, width), f32),
            pltpu.VMEM((mesh_rows, width), b16),
            held(share),
            dma,
            dma((4,)),
            dma,
        ],
        compiler_params=PARAMS,
        cost_estimate=cost_of(130, 3),
    )(flags, back_own, grad_send, first_back, second_back, landed, *in_hbm(back_low))
    return (grad_latent[None], grid_share.T)


def solution(mesh):
    return jax.shard_map(
        per_device,
        mesh=mesh,
        in_specs=(
            P("member", "grid", None),
            P("grid", None),
            P(),
            P(),
            P(None, "grid"),
            P("grid"),
            P(),
            P("grid", None, None),
            P("grid", None, None),
            P("grid", None),
        ),
        out_specs=(P("member", "grid", None), P("grid", "member")),
        check_vma=False,
    )
```

```python
import functools

import jax
import jax.numpy as jnp
from jax import lax
from jax.experimental import pallas as pl
from jax.experimental.pallas import tpu as pltpu
from jax.sharding import PartitionSpec as P

SMOOTH = 0.1
ALPHA = 0.95
EPS = 1e-05
LANES = 128
VARS = 100
MAIN = 208
TAIL = 16
FOLD = 25
FOLDS = 4
STEPS = 32767.0
CODE = 256.0
LOWEST = -20.0
BLOCK = 256
EARLY = 2
VMEM_LIMIT = 20 * 1024 * 1024


def to_neighbours(value, side):
    members, shards = lax.axis_size("member"), lax.axis_size("grid")
    pairs = [
        (member * shards + shard, member * shards + (shard + (1 if member % 2 == side else -1)) % shards)
        for member in range(members)
        for shard in range(shards)
    ]
    return lax.ppermute(value, ("member", "grid"), pairs)


def smooth_slope(difference):
    return difference * lax.rsqrt(difference * difference + SMOOTH * SMOOTH)


def turn(values, shift):
    shift = shift % LANES
    return pltpu.roll(values, shift, 1) if shift else values


def lanes_of(values):
    return lax.broadcasted_iota(jnp.int32, values.shape, 1)


def one_hot(picks, rows):
    places = lax.broadcasted_iota(jnp.int32, (rows, picks.shape[1]), 0)
    return jnp.where(places == picks, 1.0, 0.0).astype(jnp.bfloat16)


def count_pairs(row_hot, column_hot):
    return lax.dot_general(
        row_hot, column_hot, (((1,), (1,)), ((), ())), preferred_element_type=jnp.float32
    )


def parts_of(counts):
    high = counts.astype(jnp.bfloat16)
    return (counts - high.astype(jnp.float32)).astype(jnp.bfloat16), high


def edges_kernel(
    me_hbm, count_hbm, src_hbm, dst_hbm, area_hbm, var_hbm, out_hbm, target_hbm, node_hbm, latent_hbm, grid_hbm,
    flags_ref, low_hbm, back_low_hbm,
    high_ref, back_ref, back_own_ref, base_ref, node_ref, node_turned_ref, pad_ref, turned_ref, target_turned_ref, weight_ref,
    me_ref, count_ref, src_ref, dst_ref, area_ref, var_ref, out_ref, target_ref, latent_ref, grid_ref,
    low_ref, back_low_ref, in_sems, out_sems,
):
    loads = start_all(
        (me_hbm, count_hbm, src_hbm, dst_hbm, area_hbm, var_hbm, out_hbm, target_hbm, node_hbm, latent_hbm, grid_hbm),
        (me_ref, count_ref, src_ref, dst_ref, area_ref, var_ref, out_ref, target_ref, node_ref, latent_ref, grid_ref),
        in_sems,
    )
    size = high_ref.shape[0]
    slots = src_ref.shape[1] // 3
    slot = lax.broadcasted_iota(jnp.int32, (1, slots), 1)
    for load in loads[:4]:
        load.wait()
    odd = lax.rem(me_ref[0], 2)
    most = 0.0
    for place, offset in enumerate((2 - 2 * odd, 1, 2 * odd)):
        at = pl.ds(pl.multiple_of(offset * slots, LANES), slots)
        live = slot < count_ref[0, offset]
        targets = one_hot(jnp.where(live, dst_ref[:, at], -1), size)
        sources = one_hot(src_ref[:, at], size)
        counts = count_pairs(targets, sources)
        most = jnp.maximum(most, jnp.max(counts))
        columns = slice(place * size, (place + 1) * size)
        low_ref[:, columns], high_ref[:, columns] = parts_of(counts)
        back = 2 - place
        back_low_ref[:, back * size : (back + 1) * size], high = parts_of(count_pairs(sources, targets))
        if place == 1:
            back_own_ref[...] = high
        else:
            back_ref[:, (back // 2) * size : (back // 2 + 1) * size] = high
    flags_ref[0] = (most > 256.0).astype(jnp.int32)
    flags_ref[1] = me_ref[0]
    stores = start_all((low_ref, back_low_ref), (low_hbm, back_low_hbm), out_sems)
    for load in loads[4:8]:
        load.wait()
    variables, width = out_ref.shape
    padded = jnp.concatenate(
        [out_ref[...].astype(jnp.float32), jnp.zeros((LANES - variables, width), jnp.float32)], axis=0
    )
    pad_ref[...] = padded.astype(jnp.bfloat16)
    turned_ref[...] = padded.T.astype(jnp.bfloat16)
    target = jnp.concatenate(
        [target_ref[...], jnp.zeros((LANES - variables, target_ref.shape[1]), jnp.float32)], axis=0
    )
    target_turned_ref[...] = target.T
    area = jnp.broadcast_to(area_ref[...], (LANES, area_ref.shape[1])).T
    scales = jnp.concatenate([var_ref[...], jnp.zeros((1, LANES - variables), jnp.float32)], axis=1)
    weight_ref[...] = area * scales
    for load in loads[8:]:
        load.wait()
    node_turned_ref[...] = node_ref[...].T
    own = slice(size, 2 * size)
    base_ref[...] = dot(high_ref[:, own], latent_ref[...]) + grid_ref[...].astype(jnp.float32)

    @pl.when(flags_ref[0] > 0)
    def _():
        base_ref[...] += dot(low_ref[:, own], latent_ref[...])

    for store in stores:
        store.wait()


def start_all(sources, targets, sems):
    copies = [pltpu.make_async_copy(s, t, sems.at[i]) for i, (s, t) in enumerate(zip(sources, targets))]
    for copy in copies:
        copy.start()
    return copies


def blocks_of(width):
    return [slice(start, start + BLOCK) for start in range(0, width, BLOCK)]


def dot(left, right):
    return jnp.dot(left, right, preferred_element_type=jnp.float32)


def gather_kernel(flags_ref, high_ref, base_ref, rows_ref, low_hbm, out_ref, low_ref, low_sem, *, place):
    size = rows_ref.shape[0]
    at = slice(place * size, (place + 1) * size)
    out_ref[...] = base_ref[...] + dot(high_ref[:, at], rows_ref[...])

    @pl.when(flags_ref[0] > 0)
    def _():
        copy = pltpu.make_async_copy(low_hbm, low_ref, low_sem)
        copy.start()
        copy.wait()
        out_ref[...] += dot(low_ref[:, at], rows_ref[...])


def forward_kernel(
    flags_ref, high_ref, base_ref, rows_ref, node_ref, turned_ref, low_hbm,
    shared_ref, pred_ref, pre_ref, normed_ref, inverse_ref,
    low_ref, sum_ref, low_sem, *, place
):
    gather_kernel(flags_ref, high_ref, base_ref, rows_ref, low_hbm, sum_ref, low_ref, low_sem, place=place)
    summed = sum_ref[...]
    centered = summed - jnp.mean(summed, axis=-1, keepdims=True)
    inverse = lax.rsqrt(jnp.mean(centered * centered, axis=-1, keepdims=True) + EPS)
    normed = centered * inverse
    normed_ref[...] = normed
    inverse_ref[...] = inverse
    pre_act = dot(normed.astype(jnp.bfloat16), node_ref[...])
    pre_ref[...] = pre_act
    gate_sig = 0.5 + 0.5 * jnp.tanh(0.5 * pre_act)
    pred = dot((pre_act * gate_sig).astype(jnp.bfloat16), turned_ref[...])
    pred_ref[...] = pred
    largest = jnp.max(jnp.abs(pred), axis=0, keepdims=True)
    code = jnp.ceil(jnp.log2(jnp.maximum(largest, 2.0**LOWEST)) * CODE)
    whole = jnp.round(pred * (jnp.exp2(code * (-1.0 / CODE)) * STEPS))
    packed = fold(whole, code).astype(jnp.int16)
    for member in range(shared_ref.shape[0]):
        shared_ref[member] = packed


def fold(values, code=None):
    rest = values[MAIN:, :]
    tail = jnp.zeros((MAIN - FOLDS * rest.shape[0], LANES), values.dtype)
    if code is not None:
        wide = jnp.broadcast_to(code, tail.shape)
        row = lax.broadcasted_iota(jnp.int32, tail.shape, 0)
        for k in range(FOLDS):
            tail = jnp.where(row == k, turn(wide, VARS - FOLD * k), tail)
    pieces = [turn(rest, VARS - FOLD * k) for k in range(FOLDS)] + [tail]
    spare = jnp.concatenate(pieces, axis=0)
    main = values[:MAIN, :]
    lane = lanes_of(main)
    return jnp.where(lane < VARS, main, jnp.where(lane < VARS + FOLD, spare, jnp.zeros_like(main)))


def unfold(values, rows):
    rest_rows = rows - MAIN
    lane = lax.broadcasted_iota(jnp.int32, (rest_rows, LANES), 1)
    rest = jnp.zeros((rest_rows, LANES), values.dtype)
    for k in range(FOLDS):
        piece = turn(values[k * rest_rows : (k + 1) * rest_rows, :], FOLD * k - VARS)
        rest = jnp.where((lane >= FOLD * k) & (lane < FOLD * (k + 1)), piece, rest)
    return jnp.concatenate([values, rest], axis=0)


def pair_parts(ref, others, fold_ref, scale_ref):
    chips = ref.shape[0]
    rest_rows = (MAIN - TAIL) // FOLDS
    first = FOLDS * rest_rows
    lane = lax.broadcasted_iota(jnp.int32, (chips, LANES), 1)
    tails = ref[:, first:MAIN, :].astype(jnp.float32)
    code = jnp.zeros((chips, LANES), jnp.float32)
    for k in range(FOLDS):
        piece = turn(tails[:, k, :], FOLD * k - VARS)
        code = jnp.where((lane >= FOLD * k) & (lane < FOLD * (k + 1)), piece, code)
    scale = jnp.exp2(code * (1.0 / CODE)) * (1.0 / STEPS)
    for k in range(FOLDS):
        scale_ref[k] = jnp.where(lane < VARS, scale, turn(scale, VARS - FOLD * k))

    bounds = [(k * rest_rows, (k + 1) * rest_rows) for k in range(FOLDS)] + [(first, MAIN)]
    parts = [jnp.zeros((high - low, LANES), jnp.float32) for low, high in bounds]
    for other in others:
        for i, (low, high) in enumerate(bounds):
            factor = scale_ref[min(i, FOLDS - 1), pl.ds(other, 1), :]
            theirs = ref[other, low:high, :].astype(jnp.float32) * factor
            parts[i] = parts[i] + smooth_slope(fold_ref[low:high, :] - theirs)
    return parts


def alike_kernel(
    flags_ref, alike_ref, pred_ref, pre_ref, target_ref, weight_ref,
    out_ref, fold_ref, lead_ref, gate_ref, scale_ref
):
    pred = pred_ref[...]
    fold_ref[...] = fold(pred)
    lead_ref[...] = weight_ref[...] * smooth_slope(pred - target_ref[...])
    chips = alike_ref.shape[0]
    others = [lax.rem(flags_ref[1] // 2 + step, chips) for step in range(1, chips)]
    out_ref[...] = jnp.concatenate(pair_parts(alike_ref, others, fold_ref, scale_ref), axis=0)
    pre_act = pre_ref[...]
    gate_sig = 0.5 + 0.5 * jnp.tanh(0.5 * pre_act)
    gate_ref[...] = gate_sig * (1.0 + pre_act * (1.0 - gate_sig))


def backward_kernel(
    flags_ref, alike_sum_ref, unlike_ref, fold_ref, lead_ref, weight_ref, gate_ref,
    pad_ref, turned_ref, normed_ref, inverse_ref, high_ref, low_hbm,
    keep_ref, give_ref, first_ref, second_ref, send_ref,
    low_ref, scale_ref, pre_ref, grad_ref, low_sem, *, pair_scale
):
    grid_rows, width = normed_ref.shape
    me = flags_ref[1]
    chips = unlike_ref.shape[0]
    parts = pair_parts(unlike_ref, list(range(chips)), fold_ref, scale_ref)
    pair_sum = unfold(jnp.concatenate(parts, axis=0) + alike_sum_ref[...], grid_rows)
    real = lanes_of(pair_sum) < VARS
    grad_pred = lead_ref[...] - pair_scale * weight_ref[...] * jnp.where(real, pair_sum, 0.0)
    grad_pred_b = grad_pred.astype(jnp.bfloat16)
    for at in blocks_of(width):
        pre_ref[:, at] = (dot(grad_pred_b, pad_ref[:, at]) * gate_ref[:, at]).astype(jnp.bfloat16)
    plain = jnp.zeros((grid_rows, LANES), jnp.float32)
    along = jnp.zeros((grid_rows, LANES), jnp.float32)
    for at in blocks_of(width):
        grad_normed = dot(pre_ref[...], turned_ref[:, at])
        grad_ref[:, at] = grad_normed
        product = grad_normed * normed_ref[:, at]
        for lane in range(0, BLOCK, LANES):
            plain = plain + grad_normed[:, lane : lane + LANES]
            along = along + product[:, lane : lane + LANES]
    plain = jnp.sum(plain, axis=-1, keepdims=True) * (1.0 / width)
    along = jnp.sum(along, axis=-1, keepdims=True) * (1.0 / width)
    inverse = inverse_ref[...]
    half = grid_rows // 2
    lower = lax.broadcasted_iota(jnp.int32, (half, LANES), 1) < LANES // 2
    odd = lax.rem(me, 2) == 1
    sides = ((first_ref, 0), (second_ref, 1))
    for block in blocks_of(width):
        summed_b = []
        for start in range(block.start, block.stop, LANES):
            at = slice(start, start + LANES)
            pair = start // LANES
            grad_summed = inverse * (grad_ref[:, at] - plain - normed_ref[:, at] * along)
            summed_b.append(grad_summed.astype(jnp.bfloat16))
            top = grad_summed[:half, :]
            bottom = grad_summed[half:, :]
            even_block = jnp.where(lower, top, turn(bottom, LANES // 2))
            odd_block = jnp.where(lower, turn(top, LANES // 2), bottom)
            keep_ref[pair] = jnp.where(odd, odd_block, even_block)
            give_ref[pair] = jnp.where(odd, even_block, odd_block).astype(jnp.bfloat16)
        summed_b = jnp.concatenate(summed_b, axis=1)
        send_ref[:, block] = summed_b
        for ref, side in sides:
            counts = high_ref[:, side * grid_rows : (side + 1) * grid_rows]
            ref[:, block] = dot(counts, summed_b).astype(jnp.bfloat16)

    @pl.when(flags_ref[0] > 0)
    def _():
        copy = pltpu.make_async_copy(low_hbm, low_ref, low_sem)
        copy.start()
        copy.wait()
        for ref, side in sides:
            at = slice(side * grid_rows, (side + 1) * grid_rows)
            low_at = slice(2 * side * grid_rows, (2 * side + 1) * grid_rows)
            total = dot(high_ref[:, at], send_ref[...]) + dot(low_ref[:, low_at], send_ref[...])
            ref[...] = total.astype(jnp.bfloat16)


def pair_add_kernel(keep_ref, got_ref, after_ref, out_ref):
    out_ref[...] = (keep_ref[...] + got_ref[...].astype(jnp.float32)).astype(jnp.bfloat16)


def own_kernel(flags_ref, own_ref, send_ref, low_hbm, out_ref, low_ref, low_sem):
    rows = send_ref.shape[0]
    out_ref[...] = dot(own_ref[...], send_ref[...])

    @pl.when(flags_ref[0] > 0)
    def _():
        copy = pltpu.make_async_copy(low_hbm, low_ref, low_sem)
        copy.start()
        copy.wait()
        out_ref[...] += dot(low_ref[:, rows : 2 * rows], send_ref[...])


def tail_kernel(
    own_ref, first_ref, second_ref, landed_ref, out_hbm, share_hbm, out_ref, share_ref, out_sems, share_sem
):
    rows = own_ref.shape[0]
    parts = out_sems.shape[0]
    stores = []
    for part in range(parts):
        at = slice(part * rows // parts, (part + 1) * rows // parts)
        total = own_ref[at, :] + first_ref[at, :].astype(jnp.float32) + second_ref[at, :].astype(jnp.float32)
        out_ref[at, :] = total.astype(jnp.bfloat16)
        stores.append(pltpu.make_async_copy(out_ref.at[at, :], out_hbm.at[at, :], out_sems.at[part]))
        stores[-1].start()
    total = landed_ref[0].astype(jnp.float32)
    for member in range(1, landed_ref.shape[0]):
        total = total + landed_ref[member].astype(jnp.float32)
    half = total.shape[0]
    share = share_ref.shape[0]
    flipped = total.T
    share_ref[:, :half] = flipped[:share, :].astype(jnp.bfloat16)
    share_ref[:, half:] = flipped[share:, :].astype(jnp.bfloat16)
    stores.append(pltpu.make_async_copy(share_ref, share_hbm, share_sem))
    stores[-1].start()
    for store in stores:
        store.wait()


def shape(dims, dtype):
    return jax.ShapeDtypeStruct(dims, dtype)


SMEM = pl.BlockSpec(memory_space=pltpu.SMEM)
VMEM = pl.BlockSpec(memory_space=pltpu.VMEM)
HBM = pl.BlockSpec(memory_space=pltpu.HBM)


def in_hbm(*values):
    return [pltpu.with_memory_space_constraint(v, pltpu.HBM) for v in values]


def cost_of(mega_flops, mega_bytes):
    return pl.CostEstimate(
        flops=mega_flops << 20, bytes_accessed=mega_bytes << 20, transcendentals=0
    )


PARAMS = pltpu.CompilerParams(vmem_limit_bytes=VMEM_LIMIT)


def held(value):
    return pltpu.VMEM(value.shape, value.dtype)


def per_device(
    mesh_latent, grid_latent, node_weight, out_weight, target, area_weight, var_weight, edge_src, edge_dst, edge_count
):
    f32, b16, i32 = jnp.float32, jnp.bfloat16, jnp.int32
    members = lax.axis_size("member")
    me = lax.axis_index("member").astype(i32)[None]
    latent = mesh_latent[0]
    mesh_rows = latent.shape[0]
    grid_rows, width = grid_latent.shape
    variables = out_weight.shape[0]
    dma = pltpu.SemaphoreType.DMA

    first = to_neighbours(latent, 0)
    second = to_neighbours(latent, 1)
    outs = [
        pltpu.SMEM((2,), i32),
        pltpu.HBM((grid_rows, 3 * mesh_rows), b16),
        pltpu.HBM((mesh_rows, 3 * grid_rows), b16),
        pltpu.VMEM((grid_rows, 3 * mesh_rows), b16),
        pltpu.VMEM((mesh_rows, 2 * grid_rows), b16),
        pltpu.VMEM((mesh_rows, grid_rows), b16),
        pltpu.VMEM((grid_rows, width), f32),
        pltpu.VMEM((width, width), b16),
        pltpu.VMEM((width, width), b16),
        pltpu.VMEM((LANES, width), b16),
        pltpu.VMEM((width, LANES), b16),
        pltpu.VMEM((grid_rows, LANES), f32),
        pltpu.VMEM((grid_rows, LANES), f32),
    ]
    ins = [
        me,
        edge_count,
        edge_src.reshape(1, -1),
        edge_dst.reshape(1, -1),
        area_weight[None, :],
        var_weight[None, :],
        out_weight,
        target,
        node_weight,
        latent,
        grid_latent,
    ]
    smem = pltpu.SMEM
    (
        flags, low, back_low, high, back, back_own, base, node, node_turned, out_pad, out_turned, target_turned, weight
    ) = pl.pallas_call(
        edges_kernel,
        out_shape=outs,
        in_specs=[HBM] * len(ins),
        out_specs=[SMEM] + [HBM] * 2 + [VMEM] * 10,
        scratch_shapes=[smem((1,), i32), smem(edge_count.shape, i32)]
        + [held(v) for v in (*ins[2:8], *ins[9:], *outs[1:3])]
        + [dma((len(ins),)), dma((2,))],
        compiler_params=PARAMS,
        cost_estimate=cost_of(500, 8),
    )(*in_hbm(*ins))
    flags = pltpu.with_memory_space_constraint(flags, pltpu.SMEM)

    some_cost = cost_of(1000, 8)
    (most_rows,) = pl.pallas_call(
        functools.partial(gather_kernel, place=EARLY),
        out_shape=[pltpu.VMEM((grid_rows, width), f32)],
        in_specs=[SMEM] + [VMEM] * 3 + [HBM],
        out_specs=[VMEM],
        scratch_shapes=[held(low), dma],
        compiler_params=PARAMS,
        cost_estimate=cost_of(130, 2),
    )(flags, high, base, (first, second)[EARLY // 2], *in_hbm(low))
    outs = [
        pltpu.VMEM((members // 2, MAIN, LANES), jnp.int16),
        pltpu.VMEM((grid_rows, LANES), f32),
        pltpu.VMEM((grid_rows, width), f32),
        pltpu.VMEM((grid_rows, width), f32),
        pltpu.VMEM((grid_rows, 1), f32),
    ]
    shared, pred, pre_act, normed, inverse = pl.pallas_call(
        functools.partial(forward_kernel, place=2 - EARLY),
        out_shape=outs,
        in_specs=[SMEM] + [VMEM] * 5 + [HBM],
        out_specs=[VMEM] * len(outs),
        scratch_shapes=[held(low), pltpu.VMEM((grid_rows, width), f32), dma],
        compiler_params=PARAMS,
        cost_estimate=some_cost,
    )(
        flags, high, most_rows, (second, first)[EARLY // 2], node, out_turned, *in_hbm(low)
    )
    cores = [[core + 2 * chip for chip in range(members // 2)] for core in range(2)]
    swap = [(member, member ^ 1) for member in range(members)]
    alike = lax.all_to_all(shared, "member", 0, 0, axis_index_groups=cores, tiled=True)
    unlike = lax.ppermute(alike, "member", swap)
    alike_sum, folded, lead, gate = pl.pallas_call(
        alike_kernel,
        out_shape=[
            pltpu.VMEM((MAIN, LANES), f32),
            pltpu.VMEM((MAIN, LANES), f32),
            pltpu.VMEM((grid_rows, LANES), f32),
            pltpu.VMEM((grid_rows, width), f32),
        ],
        in_specs=[SMEM] + [VMEM] * 5,
        out_specs=[VMEM] * 4,
        scratch_shapes=[pltpu.VMEM((FOLDS, members // 2, LANES), f32)],
        compiler_params=PARAMS,
        cost_estimate=cost_of(10, 1),
    )(flags, alike, pred, pre_act, target_turned, weight)

    pair_scale = (1.0 - (1.0 - ALPHA) / members) / (members - 1)
    outs = [
        pltpu.VMEM((members // 2, grid_rows // 2, LANES), f32),
        pltpu.VMEM((members // 2, grid_rows // 2, LANES), b16),
        pltpu.VMEM((mesh_rows, width), b16),
        pltpu.VMEM((mesh_rows, width), b16),
        pltpu.VMEM((grid_rows, width), b16),
    ]
    keep, give, first_part, second_part, grad_send = pl.pallas_call(
        functools.partial(backward_kernel, pair_scale=pair_scale),
        out_shape=outs,
        in_specs=[SMEM] + [VMEM] * 11 + [HBM],
        out_specs=[VMEM] * 5,
        scratch_shapes=[
            held(back_low),
            pltpu.VMEM((FOLDS, members // 2, LANES), f32),
            pltpu.VMEM((grid_rows, width), b16),
            pltpu.VMEM((grid_rows, width), f32),
            dma,
        ],
        compiler_params=PARAMS,
        cost_estimate=cost_of(1000, 8),
    )(
        flags, alike_sum, unlike, folded, lead, weight, gate, out_pad, node_turned, normed, inverse, back,
        *in_hbm(back_low),
    )
    got = lax.ppermute(give, "member", swap)
    first_back = to_neighbours(first_part, 0)
    second_back = to_neighbours(second_part, 1)
    (own_part,) = pl.pallas_call(
        own_kernel,
        out_shape=[pltpu.VMEM((mesh_rows, width), f32)],
        in_specs=[SMEM] + [VMEM] * 2 + [HBM],
        out_specs=[VMEM],
        scratch_shapes=[held(back_low), dma],
        compiler_params=PARAMS,
        cost_estimate=cost_of(130, 2),
    )(flags, back_own, grad_send, *in_hbm(back_low))
    (blocks,) = pl.pallas_call(
        pair_add_kernel,
        out_shape=[pltpu.VMEM(give.shape, b16)],
        in_specs=[VMEM] * 3,
        out_specs=[VMEM],
        compiler_params=PARAMS,
        cost_estimate=cost_of(1, 1),
    )(keep, got, own_part)
    landed = lax.all_to_all(blocks, "member", 0, 0, axis_index_groups=cores, tiled=True)
    share = shape((width // members, grid_rows), b16)
    grad_latent, grid_share = pl.pallas_call(
        tail_kernel,
        out_shape=[pltpu.HBM((mesh_rows, width), b16), pltpu.HBM(share.shape, b16)],
        in_specs=[VMEM] * 4,
        out_specs=[HBM, HBM],
        scratch_shapes=[pltpu.VMEM((mesh_rows, width), b16), held(share), dma((4,)), dma],
        compiler_params=PARAMS,
        cost_estimate=cost_of(1, 3),
    )(own_part, first_back, second_back, landed)
    return (grad_latent[None], grid_share.T)


def solution(mesh):
    return jax.shard_map(
        per_device,
        mesh=mesh,
        in_specs=(
            P("member", "grid", None),
            P("grid", None),
            P(),
            P(),
            P(None, "grid"),
            P("grid"),
            P(),
            P("grid", None, None),
            P("grid", None, None),
            P("grid", None),
        ),
        out_specs=(P("member", "grid", None), P("grid", "member")),
        check_vma=False,
    )
```

```python
import functools

import jax
import jax.numpy as jnp
from jax import lax
from jax.experimental import pallas as pl
from jax.experimental.pallas import tpu as pltpu
from jax.sharding import PartitionSpec as P

SMOOTH = 0.1
ALPHA = 0.95
EPS = 1e-05
LANES = 128
VARS = 100
MAIN = 208
TAIL = 16
FOLD = 25
FOLDS = 4
STEPS = 32767.0
CODE = 256.0
LOWEST = -20.0
BLOCK = 256
EARLY = 2
VMEM_LIMIT = 20 * 1024 * 1024


def to_neighbours(value, side):
    members, shards = lax.axis_size("member"), lax.axis_size("grid")
    pairs = [
        (member * shards + shard, member * shards + (shard + (1 if member % 2 == side else -1)) % shards)
        for member in range(members)
        for shard in range(shards)
    ]
    return lax.ppermute(value, ("member", "grid"), pairs)


def smooth_slope(difference):
    return difference * lax.rsqrt(difference * difference + SMOOTH * SMOOTH)


def turn(values, shift):
    shift = shift % LANES
    return pltpu.roll(values, shift, 1) if shift else values


def lanes_of(values):
    return lax.broadcasted_iota(jnp.int32, values.shape, 1)


def one_hot(picks, rows):
    places = lax.broadcasted_iota(jnp.int32, (rows, picks.shape[1]), 0)
    return jnp.where(places == picks, 1.0, 0.0).astype(jnp.bfloat16)


def count_pairs(row_hot, column_hot):
    return lax.dot_general(
        row_hot, column_hot, (((1,), (1,)), ((), ())), preferred_element_type=jnp.float32
    )


def parts_of(counts):
    high = counts.astype(jnp.bfloat16)
    return (counts - high.astype(jnp.float32)).astype(jnp.bfloat16), high


def edges_kernel(
    me_hbm, count_hbm, src_hbm, dst_hbm, area_hbm, var_hbm, out_hbm, target_hbm, node_hbm, latent_hbm, grid_hbm,
    flags_ref, low_hbm, back_low_hbm,
    high_ref, back_ref, back_own_ref, base_ref, node_ref, node_turned_ref, pad_ref, turned_ref, target_turned_ref, weight_ref,
    me_ref, count_ref, src_ref, dst_ref, area_ref, var_ref, out_ref, target_ref, latent_ref, grid_ref,
    low_ref, back_low_ref, in_sems, out_sems,
):
    loads = start_all(
        (me_hbm, count_hbm, src_hbm, dst_hbm, area_hbm, var_hbm, out_hbm, target_hbm, node_hbm, latent_hbm, grid_hbm),
        (me_ref, count_ref, src_ref, dst_ref, area_ref, var_ref, out_ref, target_ref, node_ref, latent_ref, grid_ref),
        in_sems,
    )
    size = high_ref.shape[0]
    slots = src_ref.shape[1] // 3
    slot = lax.broadcasted_iota(jnp.int32, (1, slots), 1)
    for load in loads[:4]:
        load.wait()
    odd = lax.rem(me_ref[0], 2)
    most = 0.0
    for place, offset in enumerate((2 - 2 * odd, 1, 2 * odd)):
        at = pl.ds(pl.multiple_of(offset * slots, LANES), slots)
        live = slot < count_ref[0, offset]
        targets = one_hot(jnp.where(live, dst_ref[:, at], -1), size)
        sources = one_hot(src_ref[:, at], size)
        counts = count_pairs(targets, sources)
        most = jnp.maximum(most, jnp.max(counts))
        columns = slice(place * size, (place + 1) * size)
        low_ref[:, columns], high_ref[:, columns] = parts_of(counts)
        back = 2 - place
        back_low_ref[:, back * size : (back + 1) * size], high = parts_of(count_pairs(sources, targets))
        if place == 1:
            back_own_ref[...] = high
        else:
            back_ref[:, (back // 2) * size : (back // 2 + 1) * size] = high
    flags_ref[0] = (most > 256.0).astype(jnp.int32)
    flags_ref[1] = me_ref[0]
    stores = start_all((low_ref, back_low_ref), (low_hbm, back_low_hbm), out_sems)
    for load in loads[4:8]:
        load.wait()
    variables, width = out_ref.shape
    padded = jnp.concatenate(
        [out_ref[...].astype(jnp.float32), jnp.zeros((LANES - variables, width), jnp.float32)], axis=0
    )
    pad_ref[...] = padded.astype(jnp.bfloat16)
    turned_ref[...] = padded.T.astype(jnp.bfloat16)
    target = jnp.concatenate(
        [target_ref[...], jnp.zeros((LANES - variables, target_ref.shape[1]), jnp.float32)], axis=0
    )
    target_turned_ref[...] = target.T
    area = jnp.broadcast_to(area_ref[...], (LANES, area_ref.shape[1])).T
    scales = jnp.concatenate([var_ref[...], jnp.zeros((1, LANES - variables), jnp.float32)], axis=1)
    weight_ref[...] = area * scales
    for load in loads[8:]:
        load.wait()
    node_turned_ref[...] = node_ref[...].T
    own = slice(size, 2 * size)
    base_ref[...] = dot(high_ref[:, own], latent_ref[...]) + grid_ref[...].astype(jnp.float32)

    @pl.when(flags_ref[0] > 0)
    def _():
        base_ref[...] += dot(low_ref[:, own], latent_ref[...])

    for store in stores:
        store.wait()


def start_all(sources, targets, sems):
    copies = [pltpu.make_async_copy(s, t, sems.at[i]) for i, (s, t) in enumerate(zip(sources, targets))]
    for copy in copies:
        copy.start()
    return copies


def blocks_of(width):
    return [slice(start, start + BLOCK) for start in range(0, width, BLOCK)]


def dot(left, right):
    return jnp.dot(left, right, preferred_element_type=jnp.float32)


def gather_kernel(flags_ref, high_ref, base_ref, rows_ref, low_hbm, out_ref, low_ref, low_sem, *, place):
    size = rows_ref.shape[0]
    at = slice(place * size, (place + 1) * size)
    out_ref[...] = base_ref[...] + dot(high_ref[:, at], rows_ref[...])

    @pl.when(flags_ref[0] > 0)
    def _():
        copy = pltpu.make_async_copy(low_hbm, low_ref, low_sem)
        copy.start()
        copy.wait()
        out_ref[...] += dot(low_ref[:, at], rows_ref[...])


def forward_kernel(
    flags_ref, high_ref, base_ref, rows_ref, node_ref, turned_ref, low_hbm,
    shared_ref, pred_ref, pre_ref, normed_ref, inverse_ref,
    low_ref, sum_ref, low_sem, *, place
):
    gather_kernel(flags_ref, high_ref, base_ref, rows_ref, low_hbm, sum_ref, low_ref, low_sem, place=place)
    summed = sum_ref[...]
    centered = summed - jnp.mean(summed, axis=-1, keepdims=True)
    inverse = lax.rsqrt(jnp.mean(centered * centered, axis=-1, keepdims=True) + EPS)
    normed = centered * inverse
    normed_ref[...] = normed
    inverse_ref[...] = inverse
    pre_act = dot(normed.astype(jnp.bfloat16), node_ref[...])
    pre_ref[...] = pre_act
    gate_sig = 0.5 + 0.5 * jnp.tanh(0.5 * pre_act)
    pred = dot((pre_act * gate_sig).astype(jnp.bfloat16), turned_ref[...])
    pred_ref[...] = pred
    largest = jnp.max(jnp.abs(pred), axis=0, keepdims=True)
    code = jnp.ceil(jnp.log2(jnp.maximum(largest, 2.0**LOWEST)) * CODE)
    whole = jnp.round(pred * (jnp.exp2(code * (-1.0 / CODE)) * STEPS))
    packed = fold(whole, code).astype(jnp.int16)
    for member in range(shared_ref.shape[0]):
        shared_ref[member] = packed


def fold(values, code=None):
    rest = values[MAIN:, :]
    tail = jnp.zeros((MAIN - FOLDS * rest.shape[0], LANES), values.dtype)
    if code is not None:
        wide = jnp.broadcast_to(code, tail.shape)
        row = lax.broadcasted_iota(jnp.int32, tail.shape, 0)
        for k in range(FOLDS):
            tail = jnp.where(row == k, turn(wide, VARS - FOLD * k), tail)
    pieces = [turn(rest, VARS - FOLD * k) for k in range(FOLDS)] + [tail]
    spare = jnp.concatenate(pieces, axis=0)
    main = values[:MAIN, :]
    lane = lanes_of(main)
    return jnp.where(lane < VARS, main, jnp.where(lane < VARS + FOLD, spare, jnp.zeros_like(main)))


def unfold(values, rows):
    rest_rows = rows - MAIN
    lane = lax.broadcasted_iota(jnp.int32, (rest_rows, LANES), 1)
    rest = jnp.zeros((rest_rows, LANES), values.dtype)
    for k in range(FOLDS):
        piece = turn(values[k * rest_rows : (k + 1) * rest_rows, :], FOLD * k - VARS)
        rest = jnp.where((lane >= FOLD * k) & (lane < FOLD * (k + 1)), piece, rest)
    return jnp.concatenate([values, rest], axis=0)


def pair_parts(ref, others, fold_ref, scale_ref):
    cores, chips = ref.shape[:2]
    rest_rows = (MAIN - TAIL) // FOLDS
    first = FOLDS * rest_rows
    lane = lax.broadcasted_iota(jnp.int32, (chips, LANES), 1)
    for core in range(cores):
        tails = ref[core, :, first:MAIN, :].astype(jnp.float32)
        code = jnp.zeros((chips, LANES), jnp.float32)
        for k in range(FOLDS):
            piece = turn(tails[:, k, :], FOLD * k - VARS)
            code = jnp.where((lane >= FOLD * k) & (lane < FOLD * (k + 1)), piece, code)
        scale = jnp.exp2(code * (1.0 / CODE)) * (1.0 / STEPS)
        for k in range(FOLDS):
            scale_ref[core, k] = jnp.where(lane < VARS, scale, turn(scale, VARS - FOLD * k))

    bounds = [(k * rest_rows, (k + 1) * rest_rows) for k in range(FOLDS)] + [(first, MAIN)]
    parts = [jnp.zeros((high - low, LANES), jnp.float32) for low, high in bounds]
    for core, chip in others:
        for i, (low, high) in enumerate(bounds):
            factor = scale_ref[core, min(i, FOLDS - 1), pl.ds(chip, 1), :]
            theirs = ref[core, chip, low:high, :].astype(jnp.float32) * factor
            parts[i] = parts[i] + smooth_slope(fold_ref[low:high, :] - theirs)
    return parts


def backward_kernel(
    flags_ref, everyone_ref, pred_ref, target_ref, weight_ref, pre_act_ref,
    pad_ref, turned_ref, normed_ref, inverse_ref, high_ref, own_ref, low_hbm,
    keep_ref, give_ref, first_ref, second_ref, own_out_ref,
    low_ref, scale_ref, fold_ref, pre_ref, grad_ref, send_ref, low_sem, *, pair_scale
):
    grid_rows, width = normed_ref.shape
    me = flags_ref[1]
    chips = everyone_ref.shape[1]
    pred = pred_ref[...]
    fold_ref[...] = fold(pred)
    lead = weight_ref[...] * smooth_slope(pred - target_ref[...])
    core, chip = lax.rem(me, 2), me // 2
    others = [(core, lax.rem(chip + step, chips)) for step in range(1, chips)]
    others += [(1 - core, step) for step in range(chips)]
    parts = pair_parts(everyone_ref, others, fold_ref, scale_ref)
    pair_sum = unfold(jnp.concatenate(parts, axis=0), grid_rows)
    real = lanes_of(pair_sum) < VARS
    grad_pred = lead - pair_scale * weight_ref[...] * jnp.where(real, pair_sum, 0.0)
    grad_pred_b = grad_pred.astype(jnp.bfloat16)
    for at in blocks_of(width):
        pre_act = pre_act_ref[:, at]
        gate_sig = 0.5 + 0.5 * jnp.tanh(0.5 * pre_act)
        gate = gate_sig * (1.0 + pre_act * (1.0 - gate_sig))
        pre_ref[:, at] = (dot(grad_pred_b, pad_ref[:, at]) * gate).astype(jnp.bfloat16)
    plain = jnp.zeros((grid_rows, LANES), jnp.float32)
    along = jnp.zeros((grid_rows, LANES), jnp.float32)
    for at in blocks_of(width):
        grad_normed = dot(pre_ref[...], turned_ref[:, at])
        grad_ref[:, at] = grad_normed
        product = grad_normed * normed_ref[:, at]
        for lane in range(0, BLOCK, LANES):
            plain = plain + grad_normed[:, lane : lane + LANES]
            along = along + product[:, lane : lane + LANES]
    plain = jnp.sum(plain, axis=-1, keepdims=True) * (1.0 / width)
    along = jnp.sum(along, axis=-1, keepdims=True) * (1.0 / width)
    inverse = inverse_ref[...]
    half = grid_rows // 2
    lower = lax.broadcasted_iota(jnp.int32, (half, LANES), 1) < LANES // 2
    odd = lax.rem(me, 2) == 1
    sides = ((first_ref, 0), (second_ref, 1))
    for block in blocks_of(width):
        summed_b = []
        for start in range(block.start, block.stop, LANES):
            at = slice(start, start + LANES)
            pair = start // LANES
            grad_summed = inverse * (grad_ref[:, at] - plain - normed_ref[:, at] * along)
            summed_b.append(grad_summed.astype(jnp.bfloat16))
            top = grad_summed[:half, :]
            bottom = grad_summed[half:, :]
            even_block = jnp.where(lower, top, turn(bottom, LANES // 2))
            odd_block = jnp.where(lower, turn(top, LANES // 2), bottom)
            keep_ref[pair] = jnp.where(odd, odd_block, even_block)
            give_ref[pair] = jnp.where(odd, even_block, odd_block).astype(jnp.bfloat16)
        summed_b = jnp.concatenate(summed_b, axis=1)
        send_ref[:, block] = summed_b
        for ref, side in sides:
            counts = high_ref[:, side * grid_rows : (side + 1) * grid_rows]
            ref[:, block] = dot(counts, summed_b).astype(jnp.bfloat16)
        own_out_ref[:, block] = dot(own_ref[...], summed_b)

    @pl.when(flags_ref[0] > 0)
    def _():
        copy = pltpu.make_async_copy(low_hbm, low_ref, low_sem)
        copy.start()
        copy.wait()
        for ref, side in sides:
            at = slice(side * grid_rows, (side + 1) * grid_rows)
            low_at = slice(2 * side * grid_rows, (2 * side + 1) * grid_rows)
            total = dot(high_ref[:, at], send_ref[...]) + dot(low_ref[:, low_at], send_ref[...])
            ref[...] = total.astype(jnp.bfloat16)
        own_out_ref[...] += dot(low_ref[:, grid_rows : 2 * grid_rows], send_ref[...])


def pair_add_kernel(flags_ref, keep_ref, given_ref, out_ref):
    other = 1 - lax.rem(flags_ref[1], 2)
    out_ref[...] = (keep_ref[...] + given_ref[other].astype(jnp.float32)).astype(jnp.bfloat16)


def tail_kernel(
    own_ref, first_ref, second_ref, landed_ref, out_hbm, share_hbm, out_ref, share_ref, out_sems, share_sem
):
    rows = own_ref.shape[0]
    parts = out_sems.shape[0]
    stores = []
    for part in range(parts):
        at = slice(part * rows // parts, (part + 1) * rows // parts)
        total = own_ref[at, :] + first_ref[at, :].astype(jnp.float32) + second_ref[at, :].astype(jnp.float32)
        out_ref[at, :] = total.astype(jnp.bfloat16)
        stores.append(pltpu.make_async_copy(out_ref.at[at, :], out_hbm.at[at, :], out_sems.at[part]))
        stores[-1].start()
    total = landed_ref[0].astype(jnp.float32)
    for member in range(1, landed_ref.shape[0]):
        total = total + landed_ref[member].astype(jnp.float32)
    half = total.shape[0]
    share = share_ref.shape[0]
    flipped = total.T
    share_ref[:, :half] = flipped[:share, :].astype(jnp.bfloat16)
    share_ref[:, half:] = flipped[share:, :].astype(jnp.bfloat16)
    stores.append(pltpu.make_async_copy(share_ref, share_hbm, share_sem))
    stores[-1].start()
    for store in stores:
        store.wait()


def shape(dims, dtype):
    return jax.ShapeDtypeStruct(dims, dtype)


SMEM = pl.BlockSpec(memory_space=pltpu.SMEM)
VMEM = pl.BlockSpec(memory_space=pltpu.VMEM)
HBM = pl.BlockSpec(memory_space=pltpu.HBM)


def in_hbm(*values):
    return [pltpu.with_memory_space_constraint(v, pltpu.HBM) for v in values]


def cost_of(mega_flops, mega_bytes):
    return pl.CostEstimate(
        flops=mega_flops << 20, bytes_accessed=mega_bytes << 20, transcendentals=0
    )


PARAMS = pltpu.CompilerParams(vmem_limit_bytes=VMEM_LIMIT)


def held(value):
    return pltpu.VMEM(value.shape, value.dtype)


def per_device(
    mesh_latent, grid_latent, node_weight, out_weight, target, area_weight, var_weight, edge_src, edge_dst, edge_count
):
    f32, b16, i32 = jnp.float32, jnp.bfloat16, jnp.int32
    members = lax.axis_size("member")
    me = lax.axis_index("member").astype(i32)[None]
    latent = mesh_latent[0]
    mesh_rows = latent.shape[0]
    grid_rows, width = grid_latent.shape
    variables = out_weight.shape[0]
    dma = pltpu.SemaphoreType.DMA

    first = to_neighbours(latent, 0)
    second = to_neighbours(latent, 1)
    outs = [
        pltpu.SMEM((2,), i32),
        pltpu.HBM((grid_rows, 3 * mesh_rows), b16),
        pltpu.HBM((mesh_rows, 3 * grid_rows), b16),
        pltpu.VMEM((grid_rows, 3 * mesh_rows), b16),
        pltpu.VMEM((mesh_rows, 2 * grid_rows), b16),
        pltpu.VMEM((mesh_rows, grid_rows), b16),
        pltpu.VMEM((grid_rows, width), f32),
        pltpu.VMEM((width, width), b16),
        pltpu.VMEM((width, width), b16),
        pltpu.VMEM((LANES, width), b16),
        pltpu.VMEM((width, LANES), b16),
        pltpu.VMEM((grid_rows, LANES), f32),
        pltpu.VMEM((grid_rows, LANES), f32),
    ]
    ins = [
        me,
        edge_count,
        edge_src.reshape(1, -1),
        edge_dst.reshape(1, -1),
        area_weight[None, :],
        var_weight[None, :],
        out_weight,
        target,
        node_weight,
        latent,
        grid_latent,
    ]
    smem = pltpu.SMEM
    (
        flags, low, back_low, high, back, back_own, base, node, node_turned, out_pad, out_turned, target_turned, weight
    ) = pl.pallas_call(
        edges_kernel,
        out_shape=outs,
        in_specs=[HBM] * len(ins),
        out_specs=[SMEM] + [HBM] * 2 + [VMEM] * 10,
        scratch_shapes=[smem((1,), i32), smem(edge_count.shape, i32)]
        + [held(v) for v in (*ins[2:8], *ins[9:], *outs[1:3])]
        + [dma((len(ins),)), dma((2,))],
        compiler_params=PARAMS,
        cost_estimate=cost_of(500, 8),
    )(*in_hbm(*ins))
    flags = pltpu.with_memory_space_constraint(flags, pltpu.SMEM)

    some_cost = cost_of(1000, 8)
    (most_rows,) = pl.pallas_call(
        functools.partial(gather_kernel, place=EARLY),
        out_shape=[pltpu.VMEM((grid_rows, width), f32)],
        in_specs=[SMEM] + [VMEM] * 3 + [HBM],
        out_specs=[VMEM],
        scratch_shapes=[held(low), dma],
        compiler_params=PARAMS,
        cost_estimate=cost_of(130, 2),
    )(flags, high, base, (first, second)[EARLY // 2], *in_hbm(low))
    outs = [
        pltpu.VMEM((members // 2, MAIN, LANES), jnp.int16),
        pltpu.VMEM((grid_rows, LANES), f32),
        pltpu.VMEM((grid_rows, width), f32),
        pltpu.VMEM((grid_rows, width), f32),
        pltpu.VMEM((grid_rows, 1), f32),
    ]
    shared, pred, pre_act, normed, inverse = pl.pallas_call(
        functools.partial(forward_kernel, place=2 - EARLY),
        out_shape=outs,
        in_specs=[SMEM] + [VMEM] * 5 + [HBM],
        out_specs=[VMEM] * len(outs),
        scratch_shapes=[held(low), pltpu.VMEM((grid_rows, width), f32), dma],
        compiler_params=PARAMS,
        cost_estimate=some_cost,
    )(
        flags, high, most_rows, (second, first)[EARLY // 2], node, out_turned, *in_hbm(low)
    )
    cores = [[core + 2 * chip for chip in range(members // 2)] for core in range(2)]
    pairs = [[2 * chip, 2 * chip + 1] for chip in range(members // 2)]
    alike = lax.all_to_all(shared, "member", 0, 0, axis_index_groups=cores, tiled=True)
    everyone = lax.all_gather(alike, "member", axis=0, axis_index_groups=pairs, tiled=False)
    pair_scale = (1.0 - (1.0 - ALPHA) / members) / (members - 1)
    outs = [
        pltpu.VMEM((members // 2, grid_rows // 2, LANES), f32),
        pltpu.VMEM((members // 2, grid_rows // 2, LANES), b16),
        pltpu.VMEM((mesh_rows, width), b16),
        pltpu.VMEM((mesh_rows, width), b16),
        pltpu.VMEM((mesh_rows, width), f32),
    ]
    keep, give, first_part, second_part, own_part = pl.pallas_call(
        functools.partial(backward_kernel, pair_scale=pair_scale),
        out_shape=outs,
        in_specs=[SMEM] + [VMEM] * 11 + [HBM],
        out_specs=[VMEM] * 5,
        scratch_shapes=[
            held(back_low),
            pltpu.VMEM((2, FOLDS, members // 2, LANES), f32),
            pltpu.VMEM((MAIN, LANES), f32),
            pltpu.VMEM((grid_rows, width), b16),
            pltpu.VMEM((grid_rows, width), f32),
            pltpu.VMEM((grid_rows, width), b16),
            dma,
        ],
        compiler_params=PARAMS,
        cost_estimate=cost_of(1000, 8),
    )(
        flags, everyone, pred, target_turned, weight, pre_act, out_pad, node_turned, normed, inverse, back, back_own,
        *in_hbm(back_low),
    )
    given = lax.all_gather(give, "member", axis=0, axis_index_groups=pairs, tiled=False)
    first_back = to_neighbours(first_part, 0)
    second_back = to_neighbours(second_part, 1)
    (blocks,) = pl.pallas_call(
        pair_add_kernel,
        out_shape=[pltpu.VMEM(give.shape, b16)],
        in_specs=[SMEM] + [VMEM] * 2,
        out_specs=[VMEM],
        compiler_params=PARAMS,
        cost_estimate=cost_of(1, 1),
    )(flags, keep, given)
    landed = lax.all_to_all(blocks, "member", 0, 0, axis_index_groups=cores, tiled=True)
    share = shape((width // members, grid_rows), b16)
    grad_latent, grid_share = pl.pallas_call(
        tail_kernel,
        out_shape=[pltpu.HBM((mesh_rows, width), b16), pltpu.HBM(share.shape, b16)],
        in_specs=[VMEM] * 4,
        out_specs=[HBM, HBM],
        scratch_shapes=[pltpu.VMEM((mesh_rows, width), b16), held(share), dma((4,)), dma],
        compiler_params=PARAMS,
        cost_estimate=cost_of(1, 3),
    )(own_part, first_back, second_back, landed)
    return (grad_latent[None], grid_share.T)


def solution(mesh):
    return jax.shard_map(
        per_device,
        mesh=mesh,
        in_specs=(
            P("member", "grid", None),
            P("grid", None),
            P(),
            P(),
            P(None, "grid"),
            P("grid"),
            P(),
            P("grid", None, None),
            P("grid", None, None),
            P("grid", None),
        ),
        out_specs=(P("member", "grid", None), P("grid", "member")),
        check_vma=False,
    )
```

```python
import functools

import jax
import jax.numpy as jnp
from jax import lax
from jax.experimental import pallas as pl
from jax.experimental.pallas import tpu as pltpu
from jax.sharding import PartitionSpec as P

SMOOTH = 0.1
ALPHA = 0.95
EPS = 1e-05
LANES = 128
VARS = 100
MAIN = 208
TAIL = 16
FOLD = 25
FOLDS = 4
STEPS = 32767.0
CODE = 1.0
LOWEST = -20.0
BLOCK = 256
EARLY = 2
VMEM_LIMIT = 20 * 1024 * 1024


def to_neighbours(value, side):
    members, shards = lax.axis_size("member"), lax.axis_size("grid")
    pairs = [
        (member * shards + shard, member * shards + (shard + (1 if member % 2 == side else -1)) % shards)
        for member in range(members)
        for shard in range(shards)
    ]
    return lax.ppermute(value, ("member", "grid"), pairs)


def smooth_slope(difference):
    return difference * lax.rsqrt(difference * difference + SMOOTH * SMOOTH)


def turn(values, shift):
    shift = shift % LANES
    return pltpu.roll(values, shift, 1) if shift else values


def lanes_of(values):
    return lax.broadcasted_iota(jnp.int32, values.shape, 1)


def one_hot(picks, rows):
    places = lax.broadcasted_iota(jnp.int32, (rows, picks.shape[1]), 0)
    return jnp.where(places == picks, 1.0, 0.0).astype(jnp.bfloat16)


def count_pairs(row_hot, column_hot):
    return lax.dot_general(
        row_hot, column_hot, (((1,), (1,)), ((), ())), preferred_element_type=jnp.float32
    )


def parts_of(counts):
    high = counts.astype(jnp.bfloat16)
    return (counts - high.astype(jnp.float32)).astype(jnp.bfloat16), high


def edges_kernel(
    me_hbm, count_hbm, src_hbm, dst_hbm, area_hbm, var_hbm, out_hbm, target_hbm, node_hbm, latent_hbm, grid_hbm,
    flags_ref, low_hbm, back_low_hbm,
    high_ref, back_ref, back_own_ref, base_ref, node_ref, node_turned_ref, pad_ref, turned_ref, target_turned_ref, weight_ref,
    me_ref, count_ref, src_ref, dst_ref, area_ref, var_ref, out_ref, target_ref, latent_ref, grid_ref,
    low_ref, back_low_ref, in_sems, out_sems,
):
    loads = start_all(
        (me_hbm, count_hbm, src_hbm, dst_hbm, area_hbm, var_hbm, out_hbm, target_hbm, node_hbm, latent_hbm, grid_hbm),
        (me_ref, count_ref, src_ref, dst_ref, area_ref, var_ref, out_ref, target_ref, node_ref, latent_ref, grid_ref),
        in_sems,
    )
    size = high_ref.shape[0]
    slots = src_ref.shape[1] // 3
    slot = lax.broadcasted_iota(jnp.int32, (1, slots), 1)
    for load in loads[:4]:
        load.wait()
    odd = lax.rem(me_ref[0], 2)
    most = 0.0
    for place, offset in enumerate((2 - 2 * odd, 1, 2 * odd)):
        at = pl.ds(pl.multiple_of(offset * slots, LANES), slots)
        live = slot < count_ref[0, offset]
        targets = one_hot(jnp.where(live, dst_ref[:, at], -1), size)
        sources = one_hot(src_ref[:, at], size)
        counts = count_pairs(targets, sources)
        most = jnp.maximum(most, jnp.max(counts))
        columns = slice(place * size, (place + 1) * size)
        low_ref[:, columns], high_ref[:, columns] = parts_of(counts)
        back = 2 - place
        back_low_ref[:, back * size : (back + 1) * size], high = parts_of(count_pairs(sources, targets))
        if place == 1:
            back_own_ref[...] = high
        else:
            back_ref[:, (back // 2) * size : (back // 2 + 1) * size] = high
    flags_ref[0] = (most > 256.0).astype(jnp.int32)
    flags_ref[1] = me_ref[0]
    stores = start_all((low_ref, back_low_ref), (low_hbm, back_low_hbm), out_sems)
    for load in loads[4:8]:
        load.wait()
    variables, width = out_ref.shape
    padded = jnp.concatenate(
        [out_ref[...].astype(jnp.float32), jnp.zeros((LANES - variables, width), jnp.float32)], axis=0
    )
    pad_ref[...] = padded.astype(jnp.bfloat16)
    turned_ref[...] = padded.T.astype(jnp.bfloat16)
    target = jnp.concatenate(
        [target_ref[...], jnp.zeros((LANES - variables, target_ref.shape[1]), jnp.float32)], axis=0
    )
    target_turned_ref[...] = target.T
    area = jnp.broadcast_to(area_ref[...], (LANES, area_ref.shape[1])).T
    scales = jnp.concatenate([var_ref[...], jnp.zeros((1, LANES - variables), jnp.float32)], axis=1)
    weight_ref[...] = area * scales
    for load in loads[8:]:
        load.wait()
    node_turned_ref[...] = node_ref[...].T
    own = slice(size, 2 * size)
    base_ref[...] = dot(high_ref[:, own], latent_ref[...]) + grid_ref[...].astype(jnp.float32)

    @pl.when(flags_ref[0] > 0)
    def _():
        base_ref[...] += dot(low_ref[:, own], latent_ref[...])

    for store in stores:
        store.wait()


def start_all(sources, targets, sems):
    copies = [pltpu.make_async_copy(s, t, sems.at[i]) for i, (s, t) in enumerate(zip(sources, targets))]
    for copy in copies:
        copy.start()
    return copies


def blocks_of(width):
    return [slice(start, start + BLOCK) for start in range(0, width, BLOCK)]


def dot(left, right):
    return jnp.dot(left, right, preferred_element_type=jnp.float32)


def gather_kernel(flags_ref, high_ref, base_ref, rows_ref, low_hbm, out_ref, low_ref, low_sem, *, place):
    size = rows_ref.shape[0]
    at = slice(place * size, (place + 1) * size)
    out_ref[...] = base_ref[...] + dot(high_ref[:, at], rows_ref[...])

    @pl.when(flags_ref[0] > 0)
    def _():
        copy = pltpu.make_async_copy(low_hbm, low_ref, low_sem)
        copy.start()
        copy.wait()
        out_ref[...] += dot(low_ref[:, at], rows_ref[...])


def forward_kernel(
    flags_ref, high_ref, base_ref, rows_ref, node_ref, turned_ref, low_hbm,
    shared_ref, pred_ref, sent_ref, pre_ref, normed_ref, inverse_ref,
    low_ref, sum_ref, low_sem, *, place
):
    gather_kernel(flags_ref, high_ref, base_ref, rows_ref, low_hbm, sum_ref, low_ref, low_sem, place=place)
    summed = sum_ref[...]
    centered = summed - jnp.mean(summed, axis=-1, keepdims=True)
    inverse = lax.rsqrt(jnp.mean(centered * centered, axis=-1, keepdims=True) + EPS)
    normed = centered * inverse
    normed_ref[...] = normed
    inverse_ref[...] = inverse
    pre_act = dot(normed.astype(jnp.bfloat16), node_ref[...])
    pre_ref[...] = pre_act
    gate_sig = 0.5 + 0.5 * jnp.tanh(0.5 * pre_act)
    pred = dot((pre_act * gate_sig).astype(jnp.bfloat16), turned_ref[...])
    pred_ref[...] = pred
    largest = jnp.max(jnp.abs(pred), axis=0, keepdims=True)
    code = jnp.ceil(jnp.log2(jnp.maximum(largest, 2.0**LOWEST)) * CODE)
    whole = jnp.round(pred * (jnp.exp2(code * (-1.0 / CODE)) * STEPS))
    sent_ref[...] = whole * (jnp.exp2(code * (1.0 / CODE)) * (1.0 / STEPS))
    packed = fold(whole, code).astype(jnp.int16)
    for member in range(shared_ref.shape[0]):
        shared_ref[member] = packed


def fold(values, code=None):
    rest = values[MAIN:, :]
    tail = jnp.zeros((MAIN - FOLDS * rest.shape[0], LANES), values.dtype)
    if code is not None:
        wide = jnp.broadcast_to(code, tail.shape)
        row = lax.broadcasted_iota(jnp.int32, tail.shape, 0)
        for k in range(FOLDS):
            tail = jnp.where(row == k, turn(wide, VARS - FOLD * k), tail)
    pieces = [turn(rest, VARS - FOLD * k) for k in range(FOLDS)] + [tail]
    spare = jnp.concatenate(pieces, axis=0)
    main = values[:MAIN, :]
    lane = lanes_of(main)
    return jnp.where(lane < VARS, main, jnp.where(lane < VARS + FOLD, spare, jnp.zeros_like(main)))


def unfold(values, rows):
    rest_rows = rows - MAIN
    lane = lax.broadcasted_iota(jnp.int32, (rest_rows, LANES), 1)
    rest = jnp.zeros((rest_rows, LANES), values.dtype)
    for k in range(FOLDS):
        piece = turn(values[k * rest_rows : (k + 1) * rest_rows, :], FOLD * k - VARS)
        rest = jnp.where((lane >= FOLD * k) & (lane < FOLD * (k + 1)), piece, rest)
    return jnp.concatenate([values, rest], axis=0)


def pair_parts(ref, others, fold_ref, scale_ref):
    cores, chips = ref.shape[:2]
    rest_rows = (MAIN - TAIL) // FOLDS
    first = FOLDS * rest_rows
    lane = lax.broadcasted_iota(jnp.int32, (chips, LANES), 1)
    for core in range(cores):
        tails = ref[core, :, first:MAIN, :].astype(jnp.float32)
        code = jnp.zeros((chips, LANES), jnp.float32)
        for k in range(FOLDS):
            piece = turn(tails[:, k, :], FOLD * k - VARS)
            code = jnp.where((lane >= FOLD * k) & (lane < FOLD * (k + 1)), piece, code)
        scale = jnp.exp2(code * (1.0 / CODE)) * (1.0 / STEPS)
        for k in range(FOLDS):
            scale_ref[core, k] = jnp.where(lane < VARS, scale, turn(scale, VARS - FOLD * k))

    bounds = [(k * rest_rows, (k + 1) * rest_rows) for k in range(FOLDS)] + [(first, MAIN)]
    parts = [jnp.zeros((high - low, LANES), jnp.float32) for low, high in bounds]
    for core, chip in others:
        for i, (low, high) in enumerate(bounds):
            factor = scale_ref[core, min(i, FOLDS - 1), pl.ds(chip, 1), :]
            theirs = ref[core, chip, low:high, :].astype(jnp.float32) * factor
            parts[i] = parts[i] + smooth_slope(fold_ref[low:high, :] - theirs)
    return parts


def backward_kernel(
    flags_ref, everyone_ref, pred_ref, sent_ref, target_ref, weight_ref, pre_act_ref,
    pad_ref, turned_ref, normed_ref, inverse_ref, high_ref, own_ref, low_hbm,
    keep_ref, give_ref, first_ref, second_ref, own_out_ref,
    low_ref, scale_ref, fold_ref, pre_ref, grad_ref, send_ref, low_sem, *, pair_scale
):
    grid_rows, width = normed_ref.shape
    me = flags_ref[1]
    chips = everyone_ref.shape[1]
    pred = pred_ref[...]
    fold_ref[...] = fold(sent_ref[...])
    lead = weight_ref[...] * smooth_slope(pred - target_ref[...])
    core, chip = lax.rem(me, 2), me // 2
    others = [(core, lax.rem(chip + step, chips)) for step in range(1, chips)]
    others += [(1 - core, step) for step in range(chips)]
    parts = pair_parts(everyone_ref, others, fold_ref, scale_ref)
    pair_sum = unfold(jnp.concatenate(parts, axis=0), grid_rows)
    real = lanes_of(pair_sum) < VARS
    grad_pred = lead - pair_scale * weight_ref[...] * jnp.where(real, pair_sum, 0.0)
    grad_pred_b = grad_pred.astype(jnp.bfloat16)
    for at in blocks_of(width):
        pre_act = pre_act_ref[:, at]
        gate_sig = 0.5 + 0.5 * jnp.tanh(0.5 * pre_act)
        gate = gate_sig * (1.0 + pre_act * (1.0 - gate_sig))
        pre_ref[:, at] = (dot(grad_pred_b, pad_ref[:, at]) * gate).astype(jnp.bfloat16)
    plain = jnp.zeros((grid_rows, LANES), jnp.float32)
    along = jnp.zeros((grid_rows, LANES), jnp.float32)
    for at in blocks_of(width):
        grad_normed = dot(pre_ref[...], turned_ref[:, at])
        grad_ref[:, at] = grad_normed
        product = grad_normed * normed_ref[:, at]
        for lane in range(0, BLOCK, LANES):
            plain = plain + grad_normed[:, lane : lane + LANES]
            along = along + product[:, lane : lane + LANES]
    plain = jnp.sum(plain, axis=-1, keepdims=True) * (1.0 / width)
    along = jnp.sum(along, axis=-1, keepdims=True) * (1.0 / width)
    inverse = inverse_ref[...]
    half = grid_rows // 2
    lower = lax.broadcasted_iota(jnp.int32, (half, LANES), 1) < LANES // 2
    odd = lax.rem(me, 2) == 1
    sides = ((first_ref, 0), (second_ref, 1))
    for block in blocks_of(width):
        summed_b = []
        for start in range(block.start, block.stop, LANES):
            at = slice(start, start + LANES)
            pair = start // LANES
            grad_summed = inverse * (grad_ref[:, at] - plain - normed_ref[:, at] * along)
            summed_b.append(grad_summed.astype(jnp.bfloat16))
            top = grad_summed[:half, :]
            bottom = grad_summed[half:, :]
            even_block = jnp.where(lower, top, turn(bottom, LANES // 2))
            odd_block = jnp.where(lower, turn(top, LANES // 2), bottom)
            keep_ref[pair] = jnp.where(odd, odd_block, even_block)
            give_ref[pair] = jnp.where(odd, even_block, odd_block).astype(jnp.bfloat16)
        summed_b = jnp.concatenate(summed_b, axis=1)
        send_ref[:, block] = summed_b
        for ref, side in sides:
            counts = high_ref[:, side * grid_rows : (side + 1) * grid_rows]
            ref[:, block] = dot(counts, summed_b).astype(jnp.bfloat16)
        own_out_ref[:, block] = dot(own_ref[...], summed_b)

    @pl.when(flags_ref[0] > 0)
    def _():
        copy = pltpu.make_async_copy(low_hbm, low_ref, low_sem)
        copy.start()
        copy.wait()
        for ref, side in sides:
            at = slice(side * grid_rows, (side + 1) * grid_rows)
            low_at = slice(2 * side * grid_rows, (2 * side + 1) * grid_rows)
            total = dot(high_ref[:, at], send_ref[...]) + dot(low_ref[:, low_at], send_ref[...])
            ref[...] = total.astype(jnp.bfloat16)
        own_out_ref[...] += dot(low_ref[:, grid_rows : 2 * grid_rows], send_ref[...])


def pair_add_kernel(flags_ref, keep_ref, given_ref, out_ref):
    other = 1 - lax.rem(flags_ref[1], 2)
    out_ref[...] = (keep_ref[...] + given_ref[other].astype(jnp.float32)).astype(jnp.bfloat16)


def tail_kernel(
    own_ref, first_ref, second_ref, landed_ref, out_hbm, share_hbm, out_ref, share_ref, out_sems, share_sem
):
    rows = own_ref.shape[0]
    parts = out_sems.shape[0]
    stores = []
    for part in range(parts):
        at = slice(part * rows // parts, (part + 1) * rows // parts)
        total = own_ref[at, :] + first_ref[at, :].astype(jnp.float32) + second_ref[at, :].astype(jnp.float32)
        out_ref[at, :] = total.astype(jnp.bfloat16)
        stores.append(pltpu.make_async_copy(out_ref.at[at, :], out_hbm.at[at, :], out_sems.at[part]))
        stores[-1].start()
    total = landed_ref[0].astype(jnp.float32)
    for member in range(1, landed_ref.shape[0]):
        total = total + landed_ref[member].astype(jnp.float32)
    half = total.shape[0]
    share = share_ref.shape[0]
    flipped = total.T
    share_ref[:, :half] = flipped[:share, :].astype(jnp.bfloat16)
    share_ref[:, half:] = flipped[share:, :].astype(jnp.bfloat16)
    stores.append(pltpu.make_async_copy(share_ref, share_hbm, share_sem))
    stores[-1].start()
    for store in stores:
        store.wait()


def shape(dims, dtype):
    return jax.ShapeDtypeStruct(dims, dtype)


SMEM = pl.BlockSpec(memory_space=pltpu.SMEM)
VMEM = pl.BlockSpec(memory_space=pltpu.VMEM)
HBM = pl.BlockSpec(memory_space=pltpu.HBM)


def in_hbm(*values):
    return [pltpu.with_memory_space_constraint(v, pltpu.HBM) for v in values]


def cost_of(mega_flops, mega_bytes):
    return pl.CostEstimate(
        flops=mega_flops << 20, bytes_accessed=mega_bytes << 20, transcendentals=0
    )


PARAMS = pltpu.CompilerParams(vmem_limit_bytes=VMEM_LIMIT)


def held(value):
    return pltpu.VMEM(value.shape, value.dtype)


def per_device(
    mesh_latent, grid_latent, node_weight, out_weight, target, area_weight, var_weight, edge_src, edge_dst, edge_count
):
    f32, b16, i32 = jnp.float32, jnp.bfloat16, jnp.int32
    members = lax.axis_size("member")
    me = lax.axis_index("member").astype(i32)[None]
    latent = mesh_latent[0]
    mesh_rows = latent.shape[0]
    grid_rows, width = grid_latent.shape
    variables = out_weight.shape[0]
    dma = pltpu.SemaphoreType.DMA

    first = to_neighbours(latent, 0)
    second = to_neighbours(latent, 1)
    outs = [
        pltpu.SMEM((2,), i32),
        pltpu.HBM((grid_rows, 3 * mesh_rows), b16),
        pltpu.HBM((mesh_rows, 3 * grid_rows), b16),
        pltpu.VMEM((grid_rows, 3 * mesh_rows), b16),
        pltpu.VMEM((mesh_rows, 2 * grid_rows), b16),
        pltpu.VMEM((mesh_rows, grid_rows), b16),
        pltpu.VMEM((grid_rows, width), f32),
        pltpu.VMEM((width, width), b16),
        pltpu.VMEM((width, width), b16),
        pltpu.VMEM((LANES, width), b16),
        pltpu.VMEM((width, LANES), b16),
        pltpu.VMEM((grid_rows, LANES), f32),
        pltpu.VMEM((grid_rows, LANES), f32),
    ]
    ins = [
        me,
        edge_count,
        edge_src.reshape(1, -1),
        edge_dst.reshape(1, -1),
        area_weight[None, :],
        var_weight[None, :],
        out_weight,
        target,
        node_weight,
        latent,
        grid_latent,
    ]
    smem = pltpu.SMEM
    (
        flags, low, back_low, high, back, back_own, base, node, node_turned, out_pad, out_turned, target_turned, weight
    ) = pl.pallas_call(
        edges_kernel,
        out_shape=outs,
        in_specs=[HBM] * len(ins),
        out_specs=[SMEM] + [HBM] * 2 + [VMEM] * 10,
        scratch_shapes=[smem((1,), i32), smem(edge_count.shape, i32)]
        + [held(v) for v in (*ins[2:8], *ins[9:], *outs[1:3])]
        + [dma((len(ins),)), dma((2,))],
        compiler_params=PARAMS,
        cost_estimate=cost_of(500, 8),
    )(*in_hbm(*ins))
    flags = pltpu.with_memory_space_constraint(flags, pltpu.SMEM)

    some_cost = cost_of(1000, 8)
    (most_rows,) = pl.pallas_call(
        functools.partial(gather_kernel, place=EARLY),
        out_shape=[pltpu.VMEM((grid_rows, width), f32)],
        in_specs=[SMEM] + [VMEM] * 3 + [HBM],
        out_specs=[VMEM],
        scratch_shapes=[held(low), dma],
        compiler_params=PARAMS,
        cost_estimate=cost_of(130, 2),
    )(flags, high, base, (first, second)[EARLY // 2], *in_hbm(low))
    outs = [
        pltpu.VMEM((members // 2, MAIN, LANES), jnp.int16),
        pltpu.VMEM((grid_rows, LANES), f32),
        pltpu.VMEM((grid_rows, LANES), f32),
        pltpu.VMEM((grid_rows, width), f32),
        pltpu.VMEM((grid_rows, width), f32),
        pltpu.VMEM((grid_rows, 1), f32),
    ]
    shared, pred, sent, pre_act, normed, inverse = pl.pallas_call(
        functools.partial(forward_kernel, place=2 - EARLY),
        out_shape=outs,
        in_specs=[SMEM] + [VMEM] * 5 + [HBM],
        out_specs=[VMEM] * len(outs),
        scratch_shapes=[held(low), pltpu.VMEM((grid_rows, width), f32), dma],
        compiler_params=PARAMS,
        cost_estimate=some_cost,
    )(
        flags, high, most_rows, (second, first)[EARLY // 2], node, out_turned, *in_hbm(low)
    )
    cores = [[core + 2 * chip for chip in range(members // 2)] for core in range(2)]
    pairs = [[2 * chip, 2 * chip + 1] for chip in range(members // 2)]
    alike = lax.all_to_all(shared, "member", 0, 0, axis_index_groups=cores, tiled=True)
    everyone = lax.all_gather(alike, "member", axis=0, axis_index_groups=pairs, tiled=False)
    pair_scale = (1.0 - (1.0 - ALPHA) / members) / (members - 1)
    outs = [
        pltpu.VMEM((members // 2, grid_rows // 2, LANES), f32),
        pltpu.VMEM((members // 2, grid_rows // 2, LANES), b16),
        pltpu.VMEM((mesh_rows, width), b16),
        pltpu.VMEM((mesh_rows, width), b16),
        pltpu.VMEM((mesh_rows, width), f32),
    ]
    keep, give, first_part, second_part, own_part = pl.pallas_call(
        functools.partial(backward_kernel, pair_scale=pair_scale),
        out_shape=outs,
        in_specs=[SMEM] + [VMEM] * 12 + [HBM],
        out_specs=[VMEM] * 5,
        scratch_shapes=[
            held(back_low),
            pltpu.VMEM((2, FOLDS, members // 2, LANES), f32),
            pltpu.VMEM((MAIN, LANES), f32),
            pltpu.VMEM((grid_rows, width), b16),
            pltpu.VMEM((grid_rows, width), f32),
            pltpu.VMEM((grid_rows, width), b16),
            dma,
        ],
        compiler_params=PARAMS,
        cost_estimate=cost_of(1000, 8),
    )(
        flags, everyone, pred, sent, target_turned, weight, pre_act, out_pad, node_turned, normed, inverse, back, back_own,
        *in_hbm(back_low),
    )
    given = lax.all_gather(give, "member", axis=0, axis_index_groups=pairs, tiled=False)
    first_back = to_neighbours(first_part, 0)
    second_back = to_neighbours(second_part, 1)
    (blocks,) = pl.pallas_call(
        pair_add_kernel,
        out_shape=[pltpu.VMEM(give.shape, b16)],
        in_specs=[SMEM] + [VMEM] * 2,
        out_specs=[VMEM],
        compiler_params=PARAMS,
        cost_estimate=cost_of(1, 1),
    )(flags, keep, given)
    landed = lax.all_to_all(blocks, "member", 0, 0, axis_index_groups=cores, tiled=True)
    share = shape((width // members, grid_rows), b16)
    grad_latent, grid_share = pl.pallas_call(
        tail_kernel,
        out_shape=[pltpu.HBM((mesh_rows, width), b16), pltpu.HBM(share.shape, b16)],
        in_specs=[VMEM] * 4,
        out_specs=[HBM, HBM],
        scratch_shapes=[pltpu.VMEM((mesh_rows, width), b16), held(share), dma((4,)), dma],
        compiler_params=PARAMS,
        cost_estimate=cost_of(1, 3),
    )(own_part, first_back, second_back, landed)
    return (grad_latent[None], grid_share.T)


def solution(mesh):
    return jax.shard_map(
        per_device,
        mesh=mesh,
        in_specs=(
            P("member", "grid", None),
            P("grid", None),
            P(),
            P(),
            P(None, "grid"),
            P("grid"),
            P(),
            P("grid", None, None),
            P("grid", None, None),
            P("grid", None),
        ),
        out_specs=(P("member", "grid", None), P("grid", "member")),
        check_vma=False,
    )
```

```python
import functools

import jax
import jax.numpy as jnp
from jax import lax
from jax.experimental import pallas as pl
from jax.experimental.pallas import tpu as pltpu
from jax.sharding import PartitionSpec as P

SMOOTH = 0.1
ALPHA = 0.95
EPS = 1e-05
LANES = 128
VARS = 100
MAIN = 208
TAIL = 16
FOLD = 25
FOLDS = 4
STEPS = 32767.0
CODE = 1.0
LOWEST = -20.0
BLOCK = 256
EARLY = 2
VMEM_LIMIT = 20 * 1024 * 1024


def to_neighbours(value, side):
    members, shards = lax.axis_size("member"), lax.axis_size("grid")
    pairs = [
        (member * shards + shard, member * shards + (shard + (1 if member % 2 == side else -1)) % shards)
        for member in range(members)
        for shard in range(shards)
    ]
    return lax.ppermute(value, ("member", "grid"), pairs)


def smooth_slope(difference):
    return difference * lax.rsqrt(difference * difference + SMOOTH * SMOOTH)


def turn(values, shift):
    shift = shift % LANES
    return pltpu.roll(values, shift, 1) if shift else values


def lanes_of(values):
    return lax.broadcasted_iota(jnp.int32, values.shape, 1)


def one_hot(picks, rows):
    places = lax.broadcasted_iota(jnp.int32, (rows, picks.shape[1]), 0)
    return jnp.where(places == picks, 1.0, 0.0).astype(jnp.bfloat16)


def count_pairs(row_hot, column_hot):
    return lax.dot_general(
        row_hot, column_hot, (((1,), (1,)), ((), ())), preferred_element_type=jnp.float32
    )


def parts_of(counts):
    high = counts.astype(jnp.bfloat16)
    return (counts - high.astype(jnp.float32)).astype(jnp.bfloat16), high


def edges_kernel(
    me_hbm, count_hbm, src_hbm, dst_hbm, area_hbm, var_hbm, out_hbm, target_hbm, node_hbm, latent_hbm, grid_hbm,
    flags_ref, low_hbm, back_low_hbm,
    high_ref, back_ref, back_own_ref, base_ref, node_ref, node_turned_ref, pad_ref, turned_ref, target_turned_ref, weight_ref,
    me_ref, count_ref, src_ref, dst_ref, area_ref, var_ref, out_ref, target_ref, latent_ref, grid_ref,
    low_ref, back_low_ref, in_sems, out_sems,
):
    loads = start_all(
        (me_hbm, count_hbm, src_hbm, dst_hbm, area_hbm, var_hbm, out_hbm, target_hbm, node_hbm, latent_hbm, grid_hbm),
        (me_ref, count_ref, src_ref, dst_ref, area_ref, var_ref, out_ref, target_ref, node_ref, latent_ref, grid_ref),
        in_sems,
    )
    size = high_ref.shape[0]
    slots = src_ref.shape[1] // 3
    slot = lax.broadcasted_iota(jnp.int32, (1, slots), 1)
    for load in loads[:4]:
        load.wait()
    odd = lax.rem(me_ref[0], 2)
    most = 0.0
    for place, offset in enumerate((2 - 2 * odd, 1, 2 * odd)):
        at = pl.ds(pl.multiple_of(offset * slots, LANES), slots)
        live = slot < count_ref[0, offset]
        targets = one_hot(jnp.where(live, dst_ref[:, at], -1), size)
        sources = one_hot(src_ref[:, at], size)
        counts = count_pairs(targets, sources)
        most = jnp.maximum(most, jnp.max(counts))
        columns = slice(place * size, (place + 1) * size)
        low_ref[:, columns], high_ref[:, columns] = parts_of(counts)
        back = 2 - place
        back_low_ref[:, back * size : (back + 1) * size], high = parts_of(count_pairs(sources, targets))
        if place == 1:
            back_own_ref[...] = high
        else:
            back_ref[:, (back // 2) * size : (back // 2 + 1) * size] = high
    flags_ref[0] = (most > 256.0).astype(jnp.int32)
    flags_ref[1] = me_ref[0]
    stores = start_all((low_ref, back_low_ref), (low_hbm, back_low_hbm), out_sems)
    for load in loads[4:8]:
        load.wait()
    variables, width = out_ref.shape
    padded = jnp.concatenate(
        [out_ref[...].astype(jnp.float32), jnp.zeros((LANES - variables, width), jnp.float32)], axis=0
    )
    pad_ref[...] = padded.astype(jnp.bfloat16)
    turned_ref[...] = padded.T.astype(jnp.bfloat16)
    target = jnp.concatenate(
        [target_ref[...], jnp.zeros((LANES - variables, target_ref.shape[1]), jnp.float32)], axis=0
    )
    target_turned_ref[...] = target.T
    area = jnp.broadcast_to(area_ref[...], (LANES, area_ref.shape[1])).T
    scales = jnp.concatenate([var_ref[...], jnp.zeros((1, LANES - variables), jnp.float32)], axis=1)
    weight_ref[...] = area * scales
    for load in loads[8:]:
        load.wait()
    node_turned_ref[...] = node_ref[...].T
    own = slice(size, 2 * size)
    base_ref[...] = dot(high_ref[:, own], latent_ref[...]) + grid_ref[...].astype(jnp.float32)

    @pl.when(flags_ref[0] > 0)
    def _():
        base_ref[...] += dot(low_ref[:, own], latent_ref[...])

    for store in stores:
        store.wait()


def start_all(sources, targets, sems):
    copies = [pltpu.make_async_copy(s, t, sems.at[i]) for i, (s, t) in enumerate(zip(sources, targets))]
    for copy in copies:
        copy.start()
    return copies


def blocks_of(width):
    return [slice(start, start + BLOCK) for start in range(0, width, BLOCK)]


def dot(left, right):
    return jnp.dot(left, right, preferred_element_type=jnp.float32)


def gather_kernel(flags_ref, high_ref, base_ref, rows_ref, low_hbm, out_ref, low_ref, low_sem, *, place):
    size = rows_ref.shape[0]
    at = slice(place * size, (place + 1) * size)
    out_ref[...] = base_ref[...] + dot(high_ref[:, at], rows_ref[...])

    @pl.when(flags_ref[0] > 0)
    def _():
        copy = pltpu.make_async_copy(low_hbm, low_ref, low_sem)
        copy.start()
        copy.wait()
        out_ref[...] += dot(low_ref[:, at], rows_ref[...])


def forward_kernel(
    flags_ref, high_ref, base_ref, rows_ref, node_ref, turned_ref, low_hbm,
    shared_ref, pred_ref, sent_ref, pre_ref, normed_ref, inverse_ref,
    low_ref, sum_ref, low_sem, *, place
):
    gather_kernel(flags_ref, high_ref, base_ref, rows_ref, low_hbm, sum_ref, low_ref, low_sem, place=place)
    summed = sum_ref[...]
    centered = summed - jnp.mean(summed, axis=-1, keepdims=True)
    inverse = lax.rsqrt(jnp.mean(centered * centered, axis=-1, keepdims=True) + EPS)
    normed = centered * inverse
    normed_ref[...] = normed
    inverse_ref[...] = inverse
    pre_act = dot(normed.astype(jnp.bfloat16), node_ref[...])
    pre_ref[...] = pre_act
    gate_sig = 0.5 + 0.5 * jnp.tanh(0.5 * pre_act)
    pred = dot((pre_act * gate_sig).astype(jnp.bfloat16), turned_ref[...])
    pred_ref[...] = pred
    largest = jnp.max(jnp.abs(pred), axis=0, keepdims=True)
    code = jnp.ceil(jnp.log2(jnp.maximum(largest, 2.0**LOWEST)) * CODE)
    whole = jnp.round(pred * (jnp.exp2(code * (-1.0 / CODE)) * STEPS))
    sent_ref[...] = whole * (jnp.exp2(code * (1.0 / CODE)) * (1.0 / STEPS))
    packed = fold(whole, code).astype(jnp.int16)
    for member in range(shared_ref.shape[0]):
        shared_ref[member] = packed


def fold(values, code=None):
    rest = values[MAIN:, :]
    tail = jnp.zeros((MAIN - FOLDS * rest.shape[0], LANES), values.dtype)
    if code is not None:
        wide = jnp.broadcast_to(code, tail.shape)
        row = lax.broadcasted_iota(jnp.int32, tail.shape, 0)
        for k in range(FOLDS):
            tail = jnp.where(row == k, turn(wide, VARS - FOLD * k), tail)
    pieces = [turn(rest, VARS - FOLD * k) for k in range(FOLDS)] + [tail]
    spare = jnp.concatenate(pieces, axis=0)
    main = values[:MAIN, :]
    lane = lanes_of(main)
    return jnp.where(lane < VARS, main, jnp.where(lane < VARS + FOLD, spare, jnp.zeros_like(main)))


def unfold(values, rows):
    rest_rows = rows - MAIN
    lane = lax.broadcasted_iota(jnp.int32, (rest_rows, LANES), 1)
    rest = jnp.zeros((rest_rows, LANES), values.dtype)
    for k in range(FOLDS):
        piece = turn(values[k * rest_rows : (k + 1) * rest_rows, :], FOLD * k - VARS)
        rest = jnp.where((lane >= FOLD * k) & (lane < FOLD * (k + 1)), piece, rest)
    return jnp.concatenate([values, rest], axis=0)


def pair_parts(ref, others, fold_ref, scale_ref):
    cores, chips = ref.shape[:2]
    rest_rows = (MAIN - TAIL) // FOLDS
    first = FOLDS * rest_rows
    lane = lax.broadcasted_iota(jnp.int32, (chips, LANES), 1)
    for core in range(cores):
        tails = ref[core, :, first:MAIN, :].astype(jnp.float32)
        code = jnp.zeros((chips, LANES), jnp.float32)
        for k in range(FOLDS):
            piece = turn(tails[:, k, :], FOLD * k - VARS)
            code = jnp.where((lane >= FOLD * k) & (lane < FOLD * (k + 1)), piece, code)
        scale = jnp.exp2(code * (1.0 / CODE)) * (1.0 / STEPS)
        for k in range(FOLDS):
            scale_ref[core, k] = jnp.where(lane < VARS, scale, turn(scale, VARS - FOLD * k))

    bounds = [(k * rest_rows, (k + 1) * rest_rows) for k in range(FOLDS)] + [(first, MAIN)]
    parts = [jnp.zeros((high - low, LANES), jnp.float32) for low, high in bounds]
    for core, chip in others:
        for i, (low, high) in enumerate(bounds):
            factor = scale_ref[core, min(i, FOLDS - 1), pl.ds(chip, 1), :]
            theirs = ref[core, chip, low:high, :].astype(jnp.float32) * factor
            parts[i] = parts[i] + smooth_slope(fold_ref[low:high, :] - theirs)
    return parts


def backward_kernel(
    flags_ref, everyone_ref, pred_ref, sent_ref, target_ref, weight_ref, pre_act_ref,
    pad_ref, turned_ref, normed_ref, inverse_ref, high_ref, own_ref, low_hbm,
    keep_ref, give_ref, first_ref, second_ref, own_out_ref,
    low_ref, scale_ref, fold_ref, pre_ref, grad_ref, send_ref, low_sem, *, pair_scale
):
    grid_rows, width = normed_ref.shape
    me = flags_ref[1]
    chips = everyone_ref.shape[1]
    pred = pred_ref[...]
    fold_ref[...] = fold(sent_ref[...])
    lead = weight_ref[...] * smooth_slope(pred - target_ref[...])
    others = [(core, chip) for core in range(2) for chip in range(chips)]
    parts = pair_parts(everyone_ref, others, fold_ref, scale_ref)
    pair_sum = unfold(jnp.concatenate(parts, axis=0), grid_rows)
    real = lanes_of(pair_sum) < VARS
    grad_pred = lead - pair_scale * weight_ref[...] * jnp.where(real, pair_sum, 0.0)
    grad_pred_b = grad_pred.astype(jnp.bfloat16)
    for at in blocks_of(width):
        pre_act = pre_act_ref[:, at]
        gate_sig = 0.5 + 0.5 * jnp.tanh(0.5 * pre_act)
        gate = gate_sig * (1.0 + pre_act * (1.0 - gate_sig))
        pre_ref[:, at] = (dot(grad_pred_b, pad_ref[:, at]) * gate).astype(jnp.bfloat16)
    plain = jnp.zeros((grid_rows, LANES), jnp.float32)
    along = jnp.zeros((grid_rows, LANES), jnp.float32)
    for at in blocks_of(width):
        grad_normed = dot(pre_ref[...], turned_ref[:, at])
        grad_ref[:, at] = grad_normed
        product = grad_normed * normed_ref[:, at]
        for lane in range(0, BLOCK, LANES):
            plain = plain + grad_normed[:, lane : lane + LANES]
            along = along + product[:, lane : lane + LANES]
    plain = jnp.sum(plain, axis=-1, keepdims=True) * (1.0 / width)
    along = jnp.sum(along, axis=-1, keepdims=True) * (1.0 / width)
    inverse = inverse_ref[...]
    half = grid_rows // 2
    lower = lax.broadcasted_iota(jnp.int32, (half, LANES), 1) < LANES // 2
    odd = lax.rem(me, 2) == 1
    sides = ((first_ref, 0), (second_ref, 1))
    for block in blocks_of(width):
        summed_b = []
        for start in range(block.start, block.stop, LANES):
            at = slice(start, start + LANES)
            pair = start // LANES
            grad_summed = inverse * (grad_ref[:, at] - plain - normed_ref[:, at] * along)
            summed_b.append(grad_summed.astype(jnp.bfloat16))
            top = grad_summed[:half, :]
            bottom = grad_summed[half:, :]
            even_block = jnp.where(lower, top, turn(bottom, LANES // 2))
            odd_block = jnp.where(lower, turn(top, LANES // 2), bottom)
            keep_ref[pair] = jnp.where(odd, odd_block, even_block)
            give_ref[pair] = jnp.where(odd, even_block, odd_block).astype(jnp.bfloat16)
        summed_b = jnp.concatenate(summed_b, axis=1)
        send_ref[:, block] = summed_b
        for ref, side in sides:
            counts = high_ref[:, side * grid_rows : (side + 1) * grid_rows]
            ref[:, block] = dot(counts, summed_b).astype(jnp.bfloat16)
        own_out_ref[:, block] = dot(own_ref[...], summed_b)

    @pl.when(flags_ref[0] > 0)
    def _():
        copy = pltpu.make_async_copy(low_hbm, low_ref, low_sem)
        copy.start()
        copy.wait()
        for ref, side in sides:
            at = slice(side * grid_rows, (side + 1) * grid_rows)
            low_at = slice(2 * side * grid_rows, (2 * side + 1) * grid_rows)
            total = dot(high_ref[:, at], send_ref[...]) + dot(low_ref[:, low_at], send_ref[...])
            ref[...] = total.astype(jnp.bfloat16)
        own_out_ref[...] += dot(low_ref[:, grid_rows : 2 * grid_rows], send_ref[...])


def pair_add_kernel(flags_ref, keep_ref, given_ref, out_ref):
    other = 1 - lax.rem(flags_ref[1], 2)
    out_ref[...] = (keep_ref[...] + given_ref[other].astype(jnp.float32)).astype(jnp.bfloat16)


def tail_kernel(
    own_ref, first_ref, second_ref, landed_ref, out_hbm, share_hbm, out_ref, share_ref, out_sems, share_sem
):
    rows = own_ref.shape[0]
    parts = out_sems.shape[0]
    stores = []
    for part in range(parts):
        at = slice(part * rows // parts, (part + 1) * rows // parts)
        total = own_ref[at, :] + first_ref[at, :].astype(jnp.float32) + second_ref[at, :].astype(jnp.float32)
        out_ref[at, :] = total.astype(jnp.bfloat16)
        stores.append(pltpu.make_async_copy(out_ref.at[at, :], out_hbm.at[at, :], out_sems.at[part]))
        stores[-1].start()
    total = landed_ref[0].astype(jnp.float32)
    for member in range(1, landed_ref.shape[0]):
        total = total + landed_ref[member].astype(jnp.float32)
    half = total.shape[0]
    share = share_ref.shape[0]
    flipped = total.T
    share_ref[:, :half] = flipped[:share, :].astype(jnp.bfloat16)
    share_ref[:, half:] = flipped[share:, :].astype(jnp.bfloat16)
    stores.append(pltpu.make_async_copy(share_ref, share_hbm, share_sem))
    stores[-1].start()
    for store in stores:
        store.wait()


def shape(dims, dtype):
    return jax.ShapeDtypeStruct(dims, dtype)


SMEM = pl.BlockSpec(memory_space=pltpu.SMEM)
VMEM = pl.BlockSpec(memory_space=pltpu.VMEM)
HBM = pl.BlockSpec(memory_space=pltpu.HBM)


def in_hbm(*values):
    return [pltpu.with_memory_space_constraint(v, pltpu.HBM) for v in values]


def cost_of(mega_flops, mega_bytes):
    return pl.CostEstimate(
        flops=mega_flops << 20, bytes_accessed=mega_bytes << 20, transcendentals=0
    )


PARAMS = pltpu.CompilerParams(vmem_limit_bytes=VMEM_LIMIT)


def held(value):
    return pltpu.VMEM(value.shape, value.dtype)


def per_device(
    mesh_latent, grid_latent, node_weight, out_weight, target, area_weight, var_weight, edge_src, edge_dst, edge_count
):
    f32, b16, i32 = jnp.float32, jnp.bfloat16, jnp.int32
    members = lax.axis_size("member")
    me = lax.axis_index("member").astype(i32)[None]
    latent = mesh_latent[0]
    mesh_rows = latent.shape[0]
    grid_rows, width = grid_latent.shape
    variables = out_weight.shape[0]
    dma = pltpu.SemaphoreType.DMA

    first = to_neighbours(latent, 0)
    second = to_neighbours(latent, 1)
    outs = [
        pltpu.SMEM((2,), i32),
        pltpu.HBM((grid_rows, 3 * mesh_rows), b16),
        pltpu.HBM((mesh_rows, 3 * grid_rows), b16),
        pltpu.VMEM((grid_rows, 3 * mesh_rows), b16),
        pltpu.VMEM((mesh_rows, 2 * grid_rows), b16),
        pltpu.VMEM((mesh_rows, grid_rows), b16),
        pltpu.VMEM((grid_rows, width), f32),
        pltpu.VMEM((width, width), b16),
        pltpu.VMEM((width, width), b16),
        pltpu.VMEM((LANES, width), b16),
        pltpu.VMEM((width, LANES), b16),
        pltpu.VMEM((grid_rows, LANES), f32),
        pltpu.VMEM((grid_rows, LANES), f32),
    ]
    ins = [
        me,
        edge_count,
        edge_src.reshape(1, -1),
        edge_dst.reshape(1, -1),
        area_weight[None, :],
        var_weight[None, :],
        out_weight,
        target,
        node_weight,
        latent,
        grid_latent,
    ]
    smem = pltpu.SMEM
    (
        flags, low, back_low, high, back, back_own, base, node, node_turned, out_pad, out_turned, target_turned, weight
    ) = pl.pallas_call(
        edges_kernel,
        out_shape=outs,
        in_specs=[HBM] * len(ins),
        out_specs=[SMEM] + [HBM] * 2 + [VMEM] * 10,
        scratch_shapes=[smem((1,), i32), smem(edge_count.shape, i32)]
        + [held(v) for v in (*ins[2:8], *ins[9:], *outs[1:3])]
        + [dma((len(ins),)), dma((2,))],
        compiler_params=PARAMS,
        cost_estimate=cost_of(500, 8),
    )(*in_hbm(*ins))
    flags = pltpu.with_memory_space_constraint(flags, pltpu.SMEM)

    some_cost = cost_of(1000, 8)
    (most_rows,) = pl.pallas_call(
        functools.partial(gather_kernel, place=EARLY),
        out_shape=[pltpu.VMEM((grid_rows, width), f32)],
        in_specs=[SMEM] + [VMEM] * 3 + [HBM],
        out_specs=[VMEM],
        scratch_shapes=[held(low), dma],
        compiler_params=PARAMS,
        cost_estimate=cost_of(130, 2),
    )(flags, high, base, (first, second)[EARLY // 2], *in_hbm(low))
    outs = [
        pltpu.VMEM((members // 2, MAIN, LANES), jnp.int16),
        pltpu.VMEM((grid_rows, LANES), f32),
        pltpu.VMEM((grid_rows, LANES), f32),
        pltpu.VMEM((grid_rows, width), f32),
        pltpu.VMEM((grid_rows, width), f32),
        pltpu.VMEM((grid_rows, 1), f32),
    ]
    shared, pred, sent, pre_act, normed, inverse = pl.pallas_call(
        functools.partial(forward_kernel, place=2 - EARLY),
        out_shape=outs,
        in_specs=[SMEM] + [VMEM] * 5 + [HBM],
        out_specs=[VMEM] * len(outs),
        scratch_shapes=[held(low), pltpu.VMEM((grid_rows, width), f32), dma],
        compiler_params=PARAMS,
        cost_estimate=some_cost,
    )(
        flags, high, most_rows, (second, first)[EARLY // 2], node, out_turned, *in_hbm(low)
    )
    cores = [[core + 2 * chip for chip in range(members // 2)] for core in range(2)]
    pairs = [[2 * chip, 2 * chip + 1] for chip in range(members // 2)]
    alike = lax.all_to_all(shared, "member", 0, 0, axis_index_groups=cores, tiled=True)
    everyone = lax.all_gather(alike, "member", axis=0, axis_index_groups=pairs, tiled=False)
    pair_scale = (1.0 - (1.0 - ALPHA) / members) / (members - 1)
    outs = [
        pltpu.VMEM((members // 2, grid_rows // 2, LANES), f32),
        pltpu.VMEM((members // 2, grid_rows // 2, LANES), b16),
        pltpu.VMEM((mesh_rows, width), b16),
        pltpu.VMEM((mesh_rows, width), b16),
        pltpu.VMEM((mesh_rows, width), f32),
    ]
    keep, give, first_part, second_part, own_part = pl.pallas_call(
        functools.partial(backward_kernel, pair_scale=pair_scale),
        out_shape=outs,
        in_specs=[SMEM] + [VMEM] * 12 + [HBM],
        out_specs=[VMEM] * 5,
        scratch_shapes=[
            held(back_low),
            pltpu.VMEM((2, FOLDS, members // 2, LANES), f32),
            pltpu.VMEM((MAIN, LANES), f32),
            pltpu.VMEM((grid_rows, width), b16),
            pltpu.VMEM((grid_rows, width), f32),
            pltpu.VMEM((grid_rows, width), b16),
            dma,
        ],
        compiler_params=PARAMS,
        cost_estimate=cost_of(1000, 8),
    )(
        flags, everyone, pred, sent, target_turned, weight, pre_act, out_pad, node_turned, normed, inverse, back, back_own,
        *in_hbm(back_low),
    )
    given = lax.all_gather(give, "member", axis=0, axis_index_groups=pairs, tiled=False)
    first_back = to_neighbours(first_part, 0)
    second_back = to_neighbours(second_part, 1)
    (blocks,) = pl.pallas_call(
        pair_add_kernel,
        out_shape=[pltpu.VMEM(give.shape, b16)],
        in_specs=[SMEM] + [VMEM] * 2,
        out_specs=[VMEM],
        compiler_params=PARAMS,
        cost_estimate=cost_of(1, 1),
    )(flags, keep, given)
    landed = lax.all_to_all(blocks, "member", 0, 0, axis_index_groups=cores, tiled=True)
    share = shape((width // members, grid_rows), b16)
    grad_latent, grid_share = pl.pallas_call(
        tail_kernel,
        out_shape=[pltpu.HBM((mesh_rows, width), b16), pltpu.HBM(share.shape, b16)],
        in_specs=[VMEM] * 4,
        out_specs=[HBM, HBM],
        scratch_shapes=[pltpu.VMEM((mesh_rows, width), b16), held(share), dma((8,)), dma],
        compiler_params=PARAMS,
        cost_estimate=cost_of(1, 3),
    )(own_part, first_back, second_back, landed)
    return (grad_latent[None], grid_share.T)


def solution(mesh):
    return jax.shard_map(
        per_device,
        mesh=mesh,
        in_specs=(
            P("member", "grid", None),
            P("grid", None),
            P(),
            P(),
            P(None, "grid"),
            P("grid"),
            P(),
            P("grid", None, None),
            P("grid", None, None),
            P("grid", None),
        ),
        out_specs=(P("member", "grid", None), P("grid", "member")),
        check_vma=False,
    )
```
